32 devices in a mesh: dp: 8 (over z, x), section: 4 (over y, core).
Axes of the slice: x: 2, y: 2, z: 4, core: 2. Of those that a mesh axis runs over, the one named last changes fastest.
Arguments:
- tokens: bfloat16 [9216, 384], P('dp'), may hold values from -6 to 6
- routes: int32 [9216, 4], P('dp'), may hold values from 0 to 7, all different within a row; in each aligned block of 576 rows (0 to 575, 576 to 1151, ...) at most 288 rows name the same one
- task_ids: int32 [16], P('dp'), may hold values from 0 to 1
- cotangent: bfloat16 [9216, 256], P('dp'), may hold values from -6 to 6
- stem_gains: float32 [2, 384], replicated, may hold values from 0.5 to 1.5
- stem_shifts: float32 [2, 384], replicated, may hold values from -1 to 1
- stem_heads: bfloat16 [384, 1152], replicated, may hold values from -0.3125 to 0.3125
- stem_merge: bfloat16 [384, 384], replicated, may hold values from -2.5 to 2.5
- stem_biases: float32 [4, 384], replicated, may hold values from -1 to 1
- stem_expand: bfloat16 [384, 1536], replicated, may hold values from -0.3125 to 0.3125
- stem_lift: float32 [1536], replicated, may hold values from -1 to 1
- stem_reduce: bfloat16 [1536, 384], replicated, may hold values from -0.15625 to 0.15625
- mix_gains: float32 [2, 384], replicated, may hold values from 0.5 to 1.5
- mix_shifts: float32 [2, 384], replicated, may hold values from -1 to 1
- mix_heads: bfloat16 [384, 1152], replicated, may hold values from -0.3125 to 0.3125
- mix_merge: bfloat16 [384, 384], replicated, may hold values from -2.5 to 2.5
- mix_biases: float32 [3, 384], replicated, may hold values from -1 to 1
- router: bfloat16 [384, 2, 8], replicated, may hold values from -0.15625 to 0.15625
- expert_in: bfloat16 [8, 384, 1536], replicated, may hold values from -0.3125 to 0.3125
- expert_lift: float32 [8, 1536], replicated, may hold values from -1 to 1
- expert_out: bfloat16 [8, 1536, 384], replicated, may hold values from -0.15625 to 0.15625
- expert_drop: float32 [8, 384], replicated, may hold values from -1 to 1
- decoder: bfloat16 [384, 2, 256], replicated, may hold values from -0.3125 to 0.3125
- decoder_bias: float32 [2, 256], replicated, may hold values from -3 to 3
Outputs:
- decoded: float32 [9216, 256], P(('dp', 'section'))
- input_grad: float32 [9216, 384], P(('dp', 'section'))
- grad_stem_gains: float32 [2, 384], P(None, ('dp', 'section'))
- grad_stem_shifts: float32 [2, 384], P(None, ('dp', 'section'))
- grad_stem_heads: float32 [384, 1152], P(('dp', 'section'))
- grad_stem_merge: float32 [384, 384], P(('dp', 'section'))
- grad_stem_biases: float32 [4, 384], P(None, ('dp', 'section'))
- grad_stem_expand: float32 [384, 1536], P(('dp', 'section'))
- grad_stem_lift: float32 [1536], P(('dp', 'section'))
- grad_stem_reduce: float32 [1536, 384], P(('dp', 'section'))
- grad_mix_gains: float32 [2, 384], P(None, ('dp', 'section'))
- grad_mix_shifts: float32 [2, 384], P(None, ('dp', 'section'))
- grad_mix_heads: float32 [384, 1152], P(('dp', 'section'))
- grad_mix_merge: float32 [384, 384], P(('dp', 'section'))
- grad_mix_biases: float32 [3, 384], P(None, ('dp', 'section'))
- grad_router: float32 [384, 2, 8], P(('dp', 'section'))
- grad_expert_in: float32 [8, 384, 1536], P(None, ('dp', 'section'))
- grad_expert_lift: float32 [8, 1536], P(None, ('dp', 'section'))
- grad_expert_out: float32 [8, 1536, 384], P(None, ('dp', 'section'))
- grad_expert_drop: float32 [8, 384], P(None, ('dp', 'section'))
- grad_decoder: float32 [384, 2, 256], P(('dp', 'section'))
- grad_decoder_bias: float32 [2, 256], P(None, ('dp', 'section'))
The draws below stay inside these ranges and needn't reach their ends.
Inputs may be any that keep to these rules, and one draw needn't show every extreme that they name: `routes`: each row names 4 different experts. In each aligned block of 576 rows (one micro-batch of one index of dp) no expert is named by more than 288 rows, a bound that some block reaches.
All inputs are finite; a program needn't handle non-finite values.
Results may differ from the reference program's by a relative error of at most 0.014.
Values may be sent and summed in bfloat16 or wider, within the bound.
No kernel may reach another device: no remote copies, remote signals or barrier semaphores. Data moves between devices by JAX's collectives and lax.ppermute only.
A program may use at most 448 MiB of HBM per device.

```python
import math
import jax
import jax.numpy as jnp
import numpy as np
from jax import lax

D = 384
HEADS = 6
HDIM = 64
FF = 1536
EXPERTS = 8
TOP = 4
TASKS = 2
DEC = 256
PATCHES = 576
TMB = 576
CAP = 288
TOKENS = 9216
IMAGES = 16


def with_ends(entries, stream_key, low, high):
    index_at = [jax.random.randint(jax.random.fold_in(stream_key, axis), (), 0, length) for axis, length in enumerate(entries.shape)]
    widest = entries.shape.index(max(entries.shape))
    beside = index_at[:widest] + [(index_at[widest] + 1) % entries.shape[widest]] + index_at[widest + 1:]
    return entries.at[tuple(index_at)].set(low).at[tuple(beside)].set(high)


def levels(rng, extent, pieces, least, high):
    loudness = 1.0
    for dim, parts in pieces:
        steps = jax.random.uniform(jax.random.fold_in(jax.random.fold_in(rng, 6), dim), (parts,), jnp.float32, least / len(pieces), high / len(pieces))
        loudness = loudness * jnp.repeat(jnp.exp(steps), extent[dim] // parts).reshape((-1,) + (1,) * (len(extent) - 1 - dim))
    return loudness


def deal_out(key, own, number, rows, amount, top, most, skew):
    order = jax.random.permutation(key, amount)
    heavy_load, usual = shares(amount, rows * top, most, skew, True), shares(amount, rows * top, most, skew, False)
    places = jnp.arange(amount)

    def named(lengths, turn):
        used = int((lengths > 0).sum())
        fixed = max(1, used // 4)
        shifted = fixed + (places - fixed + turn * (used - fixed)) % max(1, amount - fixed)
        return jnp.zeros((amount,), jnp.int32).at[order[jnp.where(places < fixed, places, shifted)]].set(jnp.asarray(lengths, jnp.int32))

    lengths = jnp.where(number % 4 == 0, named(heavy_load, number // 4), named(usual, number - number // 4 - 1))
    mixed = jax.random.permutation(jax.random.fold_in(own, 3), amount)
    donor, sink = mixed[0:amount // 2 * 2:2], mixed[1:amount // 2 * 2:2]
    margin = jnp.minimum(lengths[donor] - 1, most - lengths[sink]) // 2
    margin = jnp.where((donor == order[0]) | (sink == order[0]) | (lengths[sink] == 0), 0, jnp.maximum(margin, 0))
    shifted = jax.random.randint(jax.random.fold_in(own, 4), (amount // 2,), 0, 1 << 20) % (margin + 1)
    lengths = lengths.at[donor].add(-shifted).at[sink].add(shifted)
    labels = jnp.searchsorted(jnp.cumsum(lengths), jnp.arange(rows * top), side="right").astype(jnp.int32)
    grid = labels.reshape(top, rows).T
    grid = grid[jax.random.permutation(jax.random.fold_in(own, 1), rows)]
    turn = jax.random.randint(jax.random.fold_in(own, 2), (rows, 1), 0, top)
    return jnp.take_along_axis(grid, (jnp.arange(top)[None, :] + turn) % top, axis=1)


def shares(count, total, limit, slope, full):
    portions = [(1 << 20) // math.isqrt(standing ** slope) + 1 for standing in range(1, count + 1)]
    largest = limit if full else min(limit, max(-(-total // count), total * portions[0] // sum(portions)))
    least = 1 if total - largest >= count - 1 else 0
    given, rest = [largest] + [least] * (count - 1), total - largest - least * (count - 1)
    while rest > 0:
        free = [i for i in range(1, count) if given[i] < largest] or [i for i in range(1, count) if given[i] < limit]
        whole, budget = sum([portions[i] for i in free]), rest
        for i in free:
            more = min(limit - given[i], max(1, budget * portions[i] // whole), rest)
            given[i] = given[i] + more
            rest = rest - more
    return np.array(given)


def gaussian(rng, extent, scale, most, pieces=(), kind=jnp.bfloat16):
    level = levels(rng, extent, pieces, -0.22, 0.18) if pieces else 1.0
    drawn = jax.random.normal(rng, extent, jnp.float32) * scale * level
    return jnp.minimum(jnp.maximum(drawn, -most), most).astype(kind)


def setup_inputs(seed: int = 0) -> dict:
    key_list = jax.random.split(jax.random.key(seed), 25)
    tokens = gaussian(key_list[0], (TOKENS, D), 1.0, 6.0, ((0, 8),))
    routes_keys = jax.random.split(jax.random.fold_in(key_list[1], 1), TOKENS // TMB)
    routes_turns = jax.random.permutation(jax.random.fold_in(key_list[1], 3), TOKENS // TMB)
    routes = jax.vmap(lambda own, number: deal_out(jax.random.fold_in(key_list[1], 2), own, number, TMB, EXPERTS, TOP, CAP, 1))(routes_keys, routes_turns).reshape((TOKENS, TOP))
    task_ids = with_ends(jax.random.randint(key_list[2], (IMAGES,), 0, TASKS), jax.random.fold_in(key_list[2], 1), 0, TASKS - 1).astype(jnp.int32)
    cotangent = gaussian(key_list[3], (TOKENS, DEC), 1.0, 6.0, ((0, 8),))
    stem_gains = jnp.clip(1.0 + 0.1 * jax.random.normal(key_list[4], (2, D), jnp.float32), 0.5, 1.5)
    stem_shifts = gaussian(key_list[5], (2, D), 0.2, 1.0, (), jnp.float32)
    stem_heads = gaussian(key_list[6], (D, 3 * D), D ** -0.5, 0.3125)
    stem_merge = gaussian(key_list[7], (D, D), (D // 64) ** -0.5, 2.5)
    stem_biases = gaussian(key_list[8], (4, D), 0.2, 1.0, (), jnp.float32)
    stem_expand = gaussian(key_list[9], (D, FF), D ** -0.5, 0.3125)
    stem_lift = gaussian(key_list[10], (FF,), 0.2, 1.0, (), jnp.float32)
    stem_reduce = gaussian(key_list[11], (FF, D), FF ** -0.5, 0.15625)
    mix_gains = jnp.clip(1.0 + 0.1 * jax.random.normal(key_list[12], (2, D), jnp.float32), 0.5, 1.5)
    mix_shifts = gaussian(key_list[13], (2, D), 0.2, 1.0, (), jnp.float32)
    mix_heads = gaussian(key_list[14], (D, 3 * D), D ** -0.5, 0.3125)
    mix_merge = gaussian(key_list[15], (D, D), (D // 64) ** -0.5, 2.5)
    mix_biases = gaussian(key_list[16], (3, D), 0.2, 1.0, (), jnp.float32)
    router = gaussian(key_list[17], (D, TASKS, EXPERTS), (4 * D) ** -0.5, 0.15625)
    expert_in = gaussian(key_list[18], (EXPERTS, D, FF), D ** -0.5, 0.3125)
    expert_lift = gaussian(key_list[19], (EXPERTS, FF), 0.2, 1.0, (), jnp.float32)
    expert_out = gaussian(key_list[20], (EXPERTS, FF, D), FF ** -0.5, 0.15625)
    expert_drop = gaussian(key_list[21], (EXPERTS, D), 0.2, 1.0, (), jnp.float32)
    decoder = gaussian(key_list[22], (D, TASKS, DEC), D ** -0.5, 0.3125)
    decoder_bias = gaussian(key_list[23], (TASKS, DEC), 0.5, 3.0, (), jnp.float32)
    return {"tokens": tokens, "routes": routes, "task_ids": task_ids, "cotangent": cotangent, "stem_gains": stem_gains, "stem_shifts": stem_shifts, "stem_heads": stem_heads, "stem_merge": stem_merge, "stem_biases": stem_biases, "stem_expand": stem_expand, "stem_lift": stem_lift, "stem_reduce": stem_reduce, "mix_gains": mix_gains, "mix_shifts": mix_shifts, "mix_heads": mix_heads, "mix_merge": mix_merge, "mix_biases": mix_biases, "router": router, "expert_in": expert_in, "expert_lift": expert_lift, "expert_out": expert_out, "expert_drop": expert_drop, "decoder": decoder, "decoder_bias": decoder_bias}


EPSILON = 1e-06
HIGHEST = lax.Precision.HIGHEST

@jax.custom_vjp
def low(v):
    return lax.optimization_barrier(v.astype(jnp.bfloat16)).astype(jnp.float32)

@jax.custom_vjp
def low_back(v):
    return v

def low_keep(v):
    return (low(v), None)

def low_pass(kept, grad):
    return (grad,)

def back_keep(v):
    return (v, None)

def back_low(kept, grad):
    return (low(grad),)
low.defvjp(low_keep, low_pass)
low_back.defvjp(back_keep, back_low)

def layer_norm(values, gain, shift):
    centred = values - lax.optimization_barrier(jnp.mean(values, axis=-1, keepdims=True))
    spread = lax.optimization_barrier(jnp.mean(centred * centred, axis=-1, keepdims=True))
    return centred * lax.rsqrt(spread + EPSILON) * gain + shift

def gelu_exact(values):
    return jax.nn.gelu(values, approximate=False)

def crossing(values):
    return low(low_back(values))

def attend(stream, gain, shift, heads_w, biases, merge_w):
    width_count = stream.shape[-1]
    normed = low(layer_norm(stream, gain, shift))
    mixed = jnp.dot(normed, heads_w, precision=HIGHEST)
    query = low(low_back(mixed[:, :width_count] + biases[0]))
    keys = low(low_back(mixed[:, width_count:2 * width_count]))
    values = low(low_back(mixed[:, 2 * width_count:] + biases[1]))
    shape3 = (PATCHES, HEADS, HDIM)
    raw = low_back(jnp.einsum('phd,qhd->hpq', query.reshape(shape3), keys.reshape(shape3), precision=HIGHEST))
    probs = jax.nn.softmax(raw * (1.0 / math.sqrt(HDIM)), axis=-1)
    attended = jnp.einsum('hpq,qhd->phd', low(probs), values.reshape(shape3), precision=HIGHEST)
    attended = low(low_back(attended.reshape(PATCHES, width_count)))
    return stream + low_back(jnp.dot(attended, merge_w, precision=HIGHEST) + biases[2])

def expand(stream, gain, shift, expand_w, lift, reduce_w, bias):
    normed = low(layer_norm(stream, gain, shift))
    lifted = low_back(jnp.dot(normed, expand_w, precision=HIGHEST) + lift)
    active = low(gelu_exact(lifted))
    return stream + low_back(jnp.dot(active, reduce_w, precision=HIGHEST) + bias)

def mixture(stream, gain, shift, task_table, expert_in, expert_lift, expert_out, expert_drop, route_rows):
    normed = low(layer_norm(stream, gain, shift))
    logits = jnp.dot(normed, task_table, precision=HIGHEST)
    choose = (route_rows[:, :, None] == jnp.arange(EXPERTS, dtype=jnp.int32)[None, None, :]).astype(jnp.float32)
    chosen = lax.optimization_barrier(jnp.sum(choose * logits[:, None, :], axis=-1))
    gates = jax.nn.softmax(chosen, axis=-1)
    mass = lax.optimization_barrier(jnp.sum(gates[:, :, None] * choose, axis=1))
    lifted = low_back(jnp.einsum('pd,edf->epf', normed, expert_in, precision=HIGHEST) + expert_lift[:, None, :])
    active = low(gelu_exact(lifted))
    produced = low_back(jnp.einsum('epf,efd->epd', active, expert_out, precision=HIGHEST) + expert_drop[:, None, :])
    return stream + jnp.einsum('pe,epd->pd', mass, produced, precision=HIGHEST)

def image_forward(picture, route_rows, task, weights):
    stem_gains, stem_shifts, stem_heads, stem_merge, stem_biases, stem_expand, stem_lift, stem_reduce, mix_gains, mix_shifts, mix_heads, mix_merge, mix_biases, router, expert_in, expert_lift, expert_out, expert_drop, decoder, decoder_bias = weights
    after = attend(picture, stem_gains[0], stem_shifts[0], stem_heads, stem_biases, stem_merge)
    first = crossing(expand(after, stem_gains[1], stem_shifts[1], stem_expand, stem_lift, stem_reduce, stem_biases[3]))
    second = crossing(attend(first, mix_gains[0], mix_shifts[0], mix_heads, mix_biases, mix_merge))
    task_table = lax.dynamic_index_in_dim(router, task, 1, keepdims=False)
    third = crossing(mixture(second, mix_gains[1], mix_shifts[1], task_table, expert_in, expert_lift, expert_out, expert_drop, route_rows))
    task_decoder = lax.dynamic_index_in_dim(decoder, task, 1, keepdims=False)
    task_offset = lax.dynamic_index_in_dim(decoder_bias, task, 0, keepdims=False)
    return jnp.dot(third, task_decoder, precision=HIGHEST) + task_offset

def reference(tokens, routes, task_ids, cotangent, stem_gains, stem_shifts, stem_heads, stem_merge, stem_biases, stem_expand, stem_lift, stem_reduce, mix_gains, mix_shifts, mix_heads, mix_merge, mix_biases, router, expert_in, expert_lift, expert_out, expert_drop, decoder, decoder_bias):
    weights = tuple((member.astype(jnp.float32) for member in (stem_gains, stem_shifts, stem_heads, stem_merge, stem_biases, stem_expand, stem_lift, stem_reduce, mix_gains, mix_shifts, mix_heads, mix_merge, mix_biases, router, expert_in, expert_lift, expert_out, expert_drop, decoder, decoder_bias)))
    inputs = tokens.astype(jnp.float32).reshape(IMAGES, PATCHES, D)
    routed = routes.reshape(IMAGES, PATCHES, TOP)

    def forward(inputs, weights):

        def single(item):
            picture, route_rows, task = item
            return image_forward(picture, route_rows, task, weights)
        return lax.map(jax.checkpoint(single), (inputs, routed, task_ids))
    outputs, pull = jax.vjp(forward, inputs, weights)
    grad_inputs, grads = pull(cotangent.astype(jnp.float32).reshape(IMAGES, PATCHES, DEC))
    return (outputs.reshape(TOKENS, DEC), grad_inputs.reshape(TOKENS, D), grads[0], grads[1], grads[2], grads[3], grads[4], grads[5], grads[6], grads[7], grads[8], grads[9], grads[10], grads[11], grads[12], grads[13], grads[14], grads[15], grads[16], grads[17], grads[18], grads[19])
```

```python
import math

import jax
import jax.numpy as jnp
from jax import lax
from jax.sharding import PartitionSpec as P

HEADS = 6
HDIM = 64
EXPERTS = 8
TOP = 4
PATCHES = 576
HALF = PATCHES // 2
CAP = 288
EPSILON = 1e-06
SCALE = 1.0 / math.sqrt(HDIM)
BF = jnp.bfloat16
F32 = jnp.float32


def mm(a, b):
    return jnp.dot(a, b, preferred_element_type=F32)


def mm_tn(a, b):
    return lax.dot_general(a, b, (((0,), (0,)), ((), ())), preferred_element_type=F32)


def mm_nt(a, b):
    return lax.dot_general(a, b, (((1,), (1,)), ((), ())), preferred_element_type=F32)


def split_low(v):
    high = v.astype(BF)
    return high, (v - high.astype(F32)).astype(BF)


def norm_parts(v):
    centred = v - jnp.mean(v, axis=-1, keepdims=True)
    inverse = lax.rsqrt(jnp.mean(centred * centred, axis=-1, keepdims=True) + EPSILON)
    return centred * inverse, inverse


def norm_back(v, gain, up):
    unit, inverse = norm_parts(v)
    scaled = up * gain
    back = inverse * (
        scaled
        - jnp.mean(scaled, axis=-1, keepdims=True)
        - unit * jnp.mean(scaled * unit, axis=-1, keepdims=True)
    )
    return back, jnp.sum(up * unit, axis=0), jnp.sum(up, axis=0)


def gelu_both(u):
    cdf = 0.5 * (1.0 + lax.erf(u * (1.0 / math.sqrt(2.0))))
    return u * cdf, cdf + u * jnp.exp(-0.5 * u * u) * (1.0 / math.sqrt(2.0 * math.pi))


def attend(h, gain, shift, w, c, m):
    d = h.shape[1]
    unit, unused = norm_parts(h)
    n = (unit * gain + shift).astype(BF)
    mixed = mm(n, w)
    q = (mixed[:, :d] + c[0]).astype(BF)
    k = mixed[:, d : 2 * d].astype(BF)
    v = (mixed[:, 2 * d :] + c[1]).astype(BF)
    outs = []
    for i in range(HEADS):
        at = slice(i * HDIM, (i + 1) * HDIM)
        probs = jax.nn.softmax(mm_nt(q[:, at], k[:, at]) * SCALE, axis=-1)
        outs.append(mm(probs.astype(BF), v[:, at]).astype(BF))
    o = jnp.concatenate(outs, axis=1)
    return h + (mm(o, m) + c[2]), (n, q, k, v, o)


def attend_back(h, gain, w, m, saved, up, core):
    n, q, k, v, o = saved
    d = h.shape[1]
    dc = up.astype(BF)
    grad_m = mm_tn(o, lax.dynamic_slice_in_dim(dc, core * (d // 2), d // 2, 1))
    do = mm_nt(dc, m).astype(BF)
    dq, dk, dv = [], [], []
    for i in range(HEADS):
        at = slice(i * HDIM, (i + 1) * HDIM)
        probs = jax.nn.softmax(mm_nt(q[:, at], k[:, at]) * SCALE, axis=-1)
        dp = mm_nt(do[:, at], v[:, at])
        dv.append(mm_tn(probs.astype(BF), do[:, at]).astype(BF))
        ds = probs * (dp - jnp.sum(probs * dp, axis=-1, keepdims=True))
        dr = (ds * SCALE).astype(BF)
        dq.append(mm(dr, k[:, at]).astype(BF))
        dk.append(mm_tn(dr, q[:, at]).astype(BF))
    dq, dk, dv = (jnp.concatenate(x, axis=1) for x in (dq, dk, dv))
    back, grad_gain, grad_shift = norm_back(
        h, gain, mm_nt(jnp.concatenate([dq, dk, dv], axis=1), w)
    )
    cut = lambda x: lax.dynamic_slice_in_dim(x, core * (d // 2), d // 2, 1)
    first = mm_tn(n, jnp.concatenate([cut(dq), cut(dk)], axis=1))
    second = jnp.concatenate([mm_tn(n, cut(dv)), grad_m], axis=1)
    sums = [jnp.sum(x.astype(F32), axis=0) for x in (dq, dv, dc)]
    return up + back, (first.astype(BF), second.astype(BF)), sums, grad_gain, grad_shift


def swap(x, axis, mask):
    size = lax.axis_size(axis)
    return lax.ppermute(x, axis, [(i, i ^ mask) for i in range(size)])


def line_reduce(x):
    nz = x.shape[0]
    z = lax.axis_index("dp") // 2
    own = lax.dynamic_index_in_dim(x, z, 0, keepdims=False).astype(F32)
    up = down = None
    for step in range(1, nz):
        chunk = lax.dynamic_index_in_dim(x, jnp.clip(z + nz - step, 0, nz - 1), 0, keepdims=False)
        send = chunk if up is None else (chunk.astype(F32) + up.astype(F32)).astype(BF)
        route = [(2 * i + p, 2 * i + 2 + p) for i in range(step) for p in range(2)]
        up = lax.ppermute(send, "dp", route)
        chunk = lax.dynamic_index_in_dim(x, jnp.clip(z - nz + step, 0, nz - 1), 0, keepdims=False)
        send = chunk if down is None else (chunk.astype(F32) + down.astype(F32)).astype(BF)
        route = [(2 * i + p, 2 * i - 2 + p) for i in range(nz - step, nz) for p in range(2)]
        down = lax.ppermute(send, "dp", route)
    return own + up.astype(F32) + down.astype(F32)


def pair_first(x):
    side = lax.axis_index("dp") % 2
    x = x.reshape((x.shape[0] // 2, 2) + x.shape[1:])
    got = swap(lax.dynamic_index_in_dim(x, 1 - side, 1, keepdims=False), "dp", 1)
    own = lax.dynamic_index_in_dim(x, side, 1, keepdims=False)
    return line_reduce((own.astype(F32) + got.astype(F32)).astype(BF))


def line_first(x):
    side = lax.axis_index("dp") % 2
    x = line_reduce(x.reshape((x.shape[0] // 2, 2) + x.shape[1:])).astype(BF)
    got = swap(lax.dynamic_index_in_dim(x, 1 - side, 0, keepdims=False), "dp", 1)
    own = lax.dynamic_index_in_dim(x, side, 0, keepdims=False)
    return own.astype(F32) + got.astype(F32)


def section_exchange(x):
    s = lax.axis_index("section")
    parts = [lax.dynamic_index_in_dim(x, s, 0, keepdims=False)]
    for mask in (1, 2, 3):
        parts.append(swap(lax.dynamic_index_in_dim(x, s ^ mask, 0, keepdims=False), "section", mask))
    stacked = jnp.stack(parts)
    return jnp.stack([lax.dynamic_index_in_dim(stacked, s ^ t, 0, keepdims=False) for t in range(4)])


def body(
    tokens, routes, task_ids, cotangent, stem_gains, stem_shifts, stem_heads, stem_merge,
    stem_biases, stem_expand, stem_lift, stem_reduce, mix_gains, mix_shifts, mix_heads,
    mix_merge, mix_biases, router, expert_in, expert_lift, expert_out, expert_drop, decoder,
    decoder_bias,
):
    s = lax.axis_index("section")
    image, core = s // 2, s % 2
    ndp, ns = lax.axis_size("dp"), lax.axis_size("section")
    d = tokens.shape[1]
    dec = cotangent.shape[1]
    rows = lambda x, i: lax.dynamic_slice_in_dim(x, i * PATCHES, PATCHES, 0)

    h0 = rows(tokens, image).astype(F32)
    a0, saved0 = attend(h0, stem_gains[0], stem_shifts[0], stem_heads, stem_biases, stem_merge)
    unit1, unused = norm_parts(a0)
    n1 = (unit1 * stem_gains[1] + stem_shifts[1]).astype(BF)
    u1 = mm(n1, stem_expand) + stem_lift
    active1, slope1 = gelu_both(u1)
    active1 = active1.astype(BF)
    first = (a0 + (mm(active1, stem_reduce) + stem_biases[3])).astype(BF)
    h2 = first.astype(F32)
    a2, saved2 = attend(h2, mix_gains[0], mix_shifts[0], mix_heads, mix_biases, mix_merge)
    second = a2.astype(BF).astype(F32)
    unit3, unused = norm_parts(second)
    n3 = (unit3 * mix_gains[1] + mix_shifts[1]).astype(BF)

    half = lax.dynamic_slice_in_dim(n3, core * HALF, HALF, 0)
    far = swap(half, "section", 2)
    near = swap(far, "section", 1)
    other = jnp.concatenate(
        [jnp.where(core == 0, far, near), jnp.where(core == 0, near, far)], axis=0
    )

    def routing(n, i):
        task = task_ids[i]
        table = lax.dynamic_index_in_dim(router, task, 1, keepdims=False)
        member = jnp.any(
            rows(routes, i)[:, :, None] == jnp.arange(EXPERTS, dtype=jnp.int32), axis=1
        )
        logits = jnp.where(member, mm(n, table), -jnp.inf)
        gates = jax.nn.softmax(logits, axis=-1)
        place = jnp.where(member, jnp.cumsum(member.astype(jnp.int32), axis=0) - 1, -1)
        g = rows(cotangent, i)
        tab = lax.dynamic_index_in_dim(decoder, task, 1, keepdims=False)
        return gates, place, mm_nt(g, tab).astype(BF), table, g, tab

    w_in = lax.dynamic_slice_in_dim(expert_in, 2 * s, 2, 0)
    w_out = lax.dynamic_slice_in_dim(expert_out, 2 * s, 2, 0)
    lift = lax.dynamic_slice_in_dim(expert_lift, 2 * s, 2, 0)
    drop = lax.dynamic_slice_in_dim(expert_drop, 2 * s, 2, 0)

    grads_in, grads_out, grads_lift, grads_drop = ([0.0, 0.0] for unused in range(4))

    def experts(n, gates, place, d3):
        back = produced = 0.0
        dots = []
        for j in range(2):
            here = lax.dynamic_slice_in_dim(place, 2 * s + j, 1, 1)
            pick = (here == jnp.arange(CAP, dtype=jnp.int32)[None, :]).astype(BF)
            weight = jnp.sum(
                pick.astype(F32) * lax.dynamic_slice_in_dim(gates, 2 * s + j, 1, 1), axis=0
            )[:, None]
            x = mm_tn(pick, n).astype(BF)
            dx = mm_tn(pick, d3)
            dy = (weight * dx).astype(BF)
            u = mm(x, w_in[j]) + lift[j]
            a, slope = gelu_both(u)
            a = a.astype(BF)
            y = mm(a, w_out[j]) + drop[j]
            dots.append(mm(pick, jnp.concatenate(split_low(jnp.sum(y * dx, axis=1, keepdims=True)), 1)))
            du = (slope * mm_nt(dy, w_out[j])).astype(BF)
            grads_out[j] += mm_tn(a, dy)
            grads_in[j] += mm_tn(x, du)
            grads_lift[j] += jnp.sum(du.astype(F32), axis=0)
            grads_drop[j] += jnp.sum(dy.astype(F32), axis=0)
            produced += mm(pick, (weight * y).astype(BF))
            back += mm(pick, mm_nt(du, w_in[j]).astype(BF))
        place2 = jax.nn.one_hot(2 * s + jnp.arange(2), EXPERTS, dtype=F32)
        dots = mm(jnp.stack([jnp.sum(x, 1) for x in dots], 1), place2) * 1.0
        return produced, back, dots

    gates_own, place_own, d3_own, table, g, tab = routing(n3, image)
    gates_far, place_far, d3_far, *unused = routing(other, 1 - image)
    y_own, dn_own, dot_own = experts(n3, gates_own, place_own, d3_own)
    y_far, dn_far, dot_far = experts(other, gates_far, place_far, d3_far)

    def pack(y, dn, dot):
        high, low = split_low(dot)
        pad = jnp.zeros((y.shape[0], 128 - 2 * EXPERTS), BF)
        return jnp.concatenate([y.astype(BF), dn.astype(BF), high, low, pad], axis=1)

    far = pack(y_far, dn_far, dot_far)
    cut = lambda x, c: lax.dynamic_slice_in_dim(x, c * HALF, HALF, 0)
    got = swap(cut(far, 1 - core), "section", 1)
    far = swap((cut(far, core).astype(F32) + got.astype(F32)).astype(BF), "section", 2)
    own = pack(y_own, dn_own, dot_own)
    got = swap(cut(own, 1 - core), "section", 1)
    mine = (cut(own, core).astype(F32) + got.astype(F32) + far.astype(F32)).astype(BF)
    near = swap(mine, "section", 1)
    full = jnp.concatenate(
        [jnp.where(core == 0, mine, near), jnp.where(core == 0, near, mine)], axis=0
    ).astype(F32)
    produced, dn3, dots = full[:, :d], full[:, d : 2 * d], full[:, 2 * d :]
    dots = dots[:, :EXPERTS] + dots[:, EXPERTS : 2 * EXPERTS]

    heavy = [
        pair_first(
            jnp.concatenate(
                [
                    grads_in[j].astype(BF).reshape(ndp, d // ndp, -1),
                    grads_out[j].astype(BF).reshape(ndp, d // ndp, -1),
                ],
                axis=2,
            )
        )
        for j in range(2)
    ]

    third = (second + produced).astype(BF)
    task = task_ids[image]
    decoded = mm(cut(third, core), tab) + lax.dynamic_index_in_dim(decoder_bias, task, 0, keepdims=False)
    hdec = dec // 2
    grad_tab = mm_tn(third, lax.dynamic_slice_in_dim(g, core * hdec, hdec, 1))
    chosen = (task == jnp.arange(2)).astype(F32)
    grad_dec = grad_tab[:, None, :] * chosen[None, :, None]
    grad_decbias = jnp.sum(g.astype(F32), axis=0)[None, :] * chosen[:, None]

    d3 = d3_own.astype(F32)
    dz = gates_own * (dots - jnp.sum(gates_own * dots, axis=-1, keepdims=True))
    high, low = split_low(dz)
    grad_table = mm_tn(n3, high) + mm_tn(n3, low)
    grad_router = grad_table[:, None, :] * chosen[None, :, None]
    dn3 = dn3 + mm_nt(high, table) + mm_nt(low, table)
    back, gain_m1, shift_m1 = norm_back(second, mix_gains[1], dn3)
    d2 = (d3 + back).astype(BF).astype(F32)
    d1, mix_w, mix_sums, gain_m0, shift_m0 = attend_back(
        h2, mix_gains[0], mix_heads, mix_merge, saved2, d2, core
    )
    d1 = d1.astype(BF)

    hff = stem_expand.shape[1] // 2
    grad_reduce = mm_tn(active1, lax.dynamic_slice_in_dim(d1, core * (d // 2), d // 2, 1))
    du1 = (slope1 * mm_nt(d1, stem_reduce)).astype(BF)
    grad_expand = mm_tn(n1, lax.dynamic_slice_in_dim(du1, core * hff, hff, 1))
    grad_lift = jnp.sum(du1.astype(F32), axis=0)
    back, gain_s1, shift_s1 = norm_back(a0, stem_gains[1], mm_nt(du1, stem_expand))
    da = d1.astype(F32) + back
    d0, stem_w, stem_sums, gain_s0, shift_s0 = attend_back(
        h0, stem_gains[0], stem_heads, stem_merge, saved0, da, core
    )

    low_half = [stem_w[0], mix_w[0], grad_expand.astype(BF), grad_dec[:, 0].astype(BF)]
    high_half = [stem_w[1], mix_w[1], grad_reduce.astype(BF), grad_dec[:, 1].astype(BF)]
    blocks = lambda xs: jnp.concatenate([x.reshape(ndp, d // ndp, -1) for x in xs], axis=2)
    low_half, high_half = blocks(low_half), blocks(high_half)
    got = swap(jnp.where(image == 0, high_half, low_half), "section", 2)
    kept = jnp.where(image == 0, low_half, high_half)
    light = line_first((kept.astype(F32) + got.astype(F32)).astype(BF))

    wide = jnp.concatenate([heavy[0], heavy[1], light], axis=1).astype(BF)
    wide = wide.reshape(ns, d // ndp // ns, -1) if False else wide
    ff = stem_expand.shape[1]
    r = d // ndp // ns
    f = ff // ndp // ns
    pieces = []
    for j in range(2):
        pieces.append(heavy[j][:, :ff].reshape(ns, -1))
        pieces.append(heavy[j][:, ff:].reshape(ns, -1))
    q4, e4 = d, hff
    pieces.append(light[:, :q4].reshape(ns, -1))
    pieces.append(light[:, q4 : 2 * q4].reshape(ns, -1))
    pieces.append(light[:, 2 * q4 : 2 * q4 + e4].reshape(ns, -1))
    pieces.append(light[:, 2 * q4 + e4 :].reshape(ns, -1))
    sizes = [p.shape[1] for p in pieces]
    ends = [sum(sizes[: i + 1]) for i in range(len(sizes))]
    out = section_exchange(jnp.concatenate(pieces, axis=1).astype(BF)).astype(F32)
    p = [out[:, e - n : e] for e, n in zip(ends, sizes)]
    grad_in = jnp.stack([p[0].reshape(ns, r, ff), p[2].reshape(ns, r, ff)], 1).reshape(EXPERTS, r, ff)
    grad_out = jnp.stack([p[1].reshape(ns, f, d), p[3].reshape(ns, f, d)], 1).reshape(EXPERTS, f, d)

    def attn_out(x):
        x = x.reshape(ns, r, 2, d // 2)
        gq = jnp.concatenate([x[0, :, 0], x[1, :, 0]], axis=1)
        gk = jnp.concatenate([x[0, :, 1], x[1, :, 1]], axis=1)
        gv = jnp.concatenate([x[2, :, 0], x[3, :, 0]], axis=1)
        gm = jnp.concatenate([x[2, :, 1], x[3, :, 1]], axis=1)
        return jnp.concatenate([gq, gk, gv], axis=1), gm

    g_stem_heads, g_stem_merge = attn_out(p[4])
    g_mix_heads, g_mix_merge = attn_out(p[5])
    fp = p[6]
    g_expand = jnp.concatenate([fp[0].reshape(r, hff), fp[1].reshape(r, hff)], axis=1)
    g_reduce = jnp.concatenate([fp[2].reshape(f, d // 2), fp[3].reshape(f, d // 2)], axis=1)
    dp_ = p[7].reshape(2, 2, r, hdec)
    g_dec = jnp.concatenate([dp_[:, 0], dp_[:, 1]], axis=2).transpose(1, 0, 2)

    own_flag = (core == 0).astype(F32)
    n_all = ndp * ns
    lift_all = jnp.zeros((EXPERTS, ff), F32)
    lift_all = lax.dynamic_update_slice(lift_all, jnp.stack(grads_lift), (2 * s, 0))
    drop_all = jnp.zeros((EXPERTS, d), F32)
    drop_all = lax.dynamic_update_slice(drop_all, jnp.stack(grads_drop), (2 * s, 0))
    flag = lambda x: x * own_flag
    small = [
        flag(jnp.stack([gain_s0, gain_s1])),
        flag(jnp.stack([shift_s0, shift_s1])),
        flag(jnp.stack(stem_sums + [jnp.sum(d1.astype(F32), axis=0)])),
        flag(grad_lift[None]),
        flag(jnp.stack([gain_m0, gain_m1])),
        flag(jnp.stack([shift_m0, shift_m1])),
        flag(jnp.stack(mix_sums)),
        lift_all,
        drop_all,
        flag(grad_decbias),
        flag(grad_router.reshape(d, -1).T),
    ]
    shapes = [(x.shape[0], x.shape[1] // n_all) for x in small]
    flat = jnp.concatenate(
        [x.reshape(a, n_all, b).transpose(1, 0, 2).reshape(n_all, a * b) for x, (a, b) in zip(small, shapes)],
        axis=1,
    )
    flat = lax.psum_scatter(flat, ("dp", "section"), scatter_dimension=0, tiled=True)[0]
    outs, at = [], 0
    for a, b in shapes:
        outs.append(flat[at : at + a * b].reshape(a, b))
        at += a * b
    (o_sg, o_ss, o_sb, o_lift, o_mg, o_ms, o_mb, o_elift, o_edrop, o_db, o_router) = outs
    return (
        decoded, cut(d0, core), o_sg, o_ss, g_stem_heads, g_stem_merge, o_sb, g_expand, o_lift[0],
        g_reduce, o_mg, o_ms, g_mix_heads, g_mix_merge, o_mb, o_router.T.reshape(r, 2, EXPERTS),
        grad_in, o_elift, grad_out, o_edrop, g_dec, o_db,
    )


def solution(mesh):
    both = ("dp", "section")
    placed = (P("dp", None), P("dp", None), P("dp"), P("dp", None)) + (P(),) * 20
    rows, columns = P(both, None), P(None, both)
    return jax.shard_map(
        body,
        mesh=mesh,
        in_specs=placed,
        out_specs=(
            rows, rows, columns, columns, rows, rows, columns, rows, P(both), rows, columns,
            columns, rows, rows, columns, P(both, None, None), P(None, both, None), columns,
            P(None, both, None), columns, P(both, None, None), columns,
        ),
        check_vma=False,
    )
```

```python
import functools
import math

import jax
import jax.numpy as jnp
from jax import lax
from jax.experimental import pallas as pl
from jax.experimental.pallas import tpu as pltpu
from jax.sharding import PartitionSpec as P

HEADS = 6
HDIM = 64
EXPERTS = 8
TOP = 4
PATCHES = 576
HALF = PATCHES // 2
CAP = 288
LANES = 128
EPSILON = 1e-06
SCALE = 1.0 / math.sqrt(HDIM)
BF = jnp.bfloat16
F32 = jnp.float32
VMEM = pltpu.VMEM
MIB = 1 << 20


def mm(a, b):
    return jnp.dot(a, b, preferred_element_type=F32)


def mm_tn(a, b):
    return lax.dot_general(a, b, (((0,), (0,)), ((), ())), preferred_element_type=F32)


def mm_nt(a, b):
    return lax.dot_general(a, b, (((1,), (1,)), ((), ())), preferred_element_type=F32)


def split_low(v):
    high = v.astype(BF)
    return high, (v - high.astype(F32)).astype(BF)


def norm_parts(v):
    centred = v - jnp.mean(v, axis=-1, keepdims=True)
    inverse = lax.rsqrt(jnp.mean(centred * centred, axis=-1, keepdims=True) + EPSILON)
    return centred * inverse, inverse


def norm_back(v, gain, up):
    unit, inverse = norm_parts(v)
    scaled = up * gain
    back = inverse * (
        scaled
        - jnp.mean(scaled, axis=-1, keepdims=True)
        - unit * jnp.mean(scaled * unit, axis=-1, keepdims=True)
    )
    return back, jnp.sum(up * unit, axis=0, keepdims=True), jnp.sum(up, axis=0, keepdims=True)


def gelu_both(u):
    size = jnp.abs(u)
    den = 1.0 + (0.3275911 / math.sqrt(2.0)) * size
    t = pl.reciprocal(den, approx=True)
    t = t * (2.0 - den * t)
    bell = jnp.exp(-0.5 * u * u)
    half = 0.5 * 1.061405429
    poly = t * (0.5 * 0.254829592 + t * (0.5 * -0.284496736 + t * (0.5 * 1.421413741 + t * (0.5 * -1.453152027 + t * half))))
    tail = poly * bell
    cdf = jnp.where(u >= 0.0, 1.0 - tail, tail)
    return u * cdf, cdf + u * bell * (1.0 / math.sqrt(2.0 * math.pi))


def side_masks():
    lane = lax.broadcasted_iota(jnp.int32, (1, LANES), 1)
    left = (lane < HDIM).astype(F32)
    return left.astype(BF), (1.0 - left).astype(BF)


def attend_kernel(h, gain, shift, w, c, m, n_ref, q_ref, k_ref, v_ref, o_ref):
    d = h.shape[1]
    unit, unused = norm_parts(h)
    n_ref[...] = (unit * gain + shift).astype(BF)
    n = n_ref[...]
    q_ref[...] = ((mm(n, w[:, :d]) + c[0:1]) * SCALE).astype(BF)
    k_ref[...] = mm(n, w[:, d : 2 * d]).astype(BF)
    v_ref[...] = (mm(n, w[:, 2 * d :]) + c[1:2]).astype(BF)
    masks = side_masks()
    for p in range(d // LANES):
        at = slice(p * LANES, (p + 1) * LANES)
        keys, values = k_ref[:, at], v_ref[:, at]
        for b in range(2):
            rows = slice(b * HALF, (b + 1) * HALF)
            query = q_ref[rows, at]
            total = None
            for mask in masks:
                scores = mm_nt(query * mask, keys)
                e = jnp.exp(scores - jnp.max(scores, axis=-1, keepdims=True))
                probs = e * (1.0 / jnp.sum(e, axis=-1, keepdims=True))
                part = mm(probs.astype(BF), values * mask)
                total = part if total is None else total + part
            o_ref[rows, at] = total.astype(BF)
    return h + (mm(o_ref[...], m[...]) + c[2:3])


def forward_kernel(
    image, tok, sg, ss, sw, sm, sb, sx, sl, sr, mg, ms, mw, m_m, mb,
    n0, q0, k0, v0, o0, a0, n1, act, slope, first, n2, q2, k2, v2, o2, second, n3,
):
    del image
    h = tok[...].astype(F32)
    a0[...] = attend_kernel(h, sg[0:1], ss[0:1], sw, sb, sm, n0, q0, k0, v0, o0)
    unit, unused = norm_parts(a0[...])
    n1[...] = (unit * sg[1:2] + ss[1:2]).astype(BF)
    step = 512
    for f in range(sx.shape[1] // step):
        at = slice(f * step, (f + 1) * step)
        active, bend = gelu_both(mm(n1[...], sx[:, at]) + sl[:, at])
        act[:, at] = active.astype(BF)
        slope[:, at] = bend.astype(BF)
    first[...] = (a0[...] + (mm(act[...], sr[...]) + sb[3:4])).astype(BF)
    h = first[...].astype(F32)
    second[...] = attend_kernel(h, mg[0:1], ms[0:1], mw, mb, m_m, n2, q2, k2, v2, o2).astype(BF)
    unit, unused = norm_parts(second[...].astype(F32))
    n3[...] = (unit * mg[1:2] + ms[1:2]).astype(BF)


def whole(shape):
    return pl.BlockSpec(shape, lambda *a: (0,) * len(shape))


def call(kernel, scalars, arrays, specs, outs, scratch=(), grid=(1,), out_specs=None, flops=1e9, limit=56):
    return pl.pallas_call(
        kernel,
        out_shape=[jax.ShapeDtypeStruct(*o) for o in outs],
        grid_spec=pltpu.PrefetchScalarGridSpec(
            num_scalar_prefetch=1,
            grid=grid,
            in_specs=specs,
            out_specs=out_specs or [whole(o[0]) for o in outs],
            scratch_shapes=list(scratch),
        ),
        compiler_params=pltpu.CompilerParams(
            vmem_limit_bytes=limit * MIB, dimension_semantics=("arbitrary",) * len(grid)
        ),
        cost_estimate=pl.CostEstimate(flops=int(flops), bytes_accessed=8 * MIB, transcendentals=0),
    )(scalars, *arrays)


def forward(image, tokens, weights):
    d = tokens.shape[1]
    ff = weights[5].shape[1]
    wide = ((PATCHES, d), BF)
    outs = [wide] * 5 + [((PATCHES, d), F32), wide, ((PATCHES, ff), BF), ((PATCHES, ff), BF)] + [wide] * 8
    specs = [pl.BlockSpec((PATCHES, d), lambda i, s: (s[0], 0))] + [whole(w.shape) for w in weights]
    return call(forward_kernel, image[None], [tokens, *weights], specs, outs, flops=4e9)


def lane_ids(rows=1):
    return lax.broadcasted_iota(jnp.int32, (rows, LANES), 1)


def columns_of(rows, lanes):
    count = -(-len(rows) // 8) * 8
    n = rows[0].shape[1]
    stacked = jnp.concatenate(rows + [jnp.zeros((count - len(rows), n), F32)], axis=0)
    place = lax.broadcasted_iota(jnp.int32, (count, LANES), 0)
    lane = lane_ids(count)
    spread = jnp.zeros((count, LANES), F32)
    for i, at in enumerate(lanes):
        spread = spread + jnp.where((place == i) & (lane == at), 1.0, 0.0)
    return mm_tn(stacked.astype(BF), spread.astype(BF))


def spread_blocks(row, first_lane, blocks):
    n = row.shape[1]
    r = n // 4 // blocks
    place = lax.broadcasted_iota(jnp.int32, (8, LANES), 0)
    stacked = jnp.concatenate([row, jnp.zeros((7, n), F32)], axis=0)
    column = mm_tn(stacked.astype(BF), jnp.where(place == 0, 1.0, 0.0).astype(BF))
    lane = lane_ids()
    parts = []
    for b in range(blocks):
        part = None
        for s in range(4):
            at = (4 * b + s) * r
            piece = jnp.where(lane == first_lane + s, column[at : at + r], 0.0)
            part = piece if part is None else part + piece
        parts.append(part)
    return jnp.concatenate(parts, axis=0)


def experts_kernel(blocks, own, *refs):
    scalars, n, routes, router, cot, dec, w_in, lift, w_out, drop = refs[:10]
    refs = refs[10:]
    if own:
        xs, dys, acts, dus, pay, gates, place, d3, total, a_all, du_all = refs
    else:
        xo, dyo, ao, duo, grad, pay, gates, place, d3, total, a_all, du_all = refs
    j = pl.program_id(0)

    @pl.when(j == 0)
    def begin():
        ids = lax.broadcasted_iota(jnp.int32, (EXPERTS, PATCHES), 0)
        member = jnp.zeros((EXPERTS, PATCHES), F32)
        for k in range(TOP):
            member = member + jnp.where(ids == routes[0, k : k + 1, :], 1.0, 0.0)
        logits = jnp.where(member > 0.0, mm_nt(router[0], n[...]), -1e30)
        e = jnp.where(member > 0.0, jnp.exp(logits - jnp.max(logits, axis=0, keepdims=True)), 0.0)
        gates[...] = e / jnp.sum(e, axis=0, keepdims=True)
        before = lax.broadcasted_iota(jnp.int32, (PATCHES, PATCHES), 0)
        after = lax.broadcasted_iota(jnp.int32, (PATCHES, PATCHES), 1)
        upper = jnp.where(before <= after, 1.0, 0.0).astype(BF)
        count = mm(member.astype(BF), upper)
        place[...] = jnp.where(member > 0.0, count - 1.0, -1.0)
        d3[...] = mm_nt(cot[...], dec[...]).astype(BF)

    e = scalars[0] + j
    spot = place[pl.ds(e, 1), :].astype(jnp.int32)
    hit = lax.broadcasted_iota(jnp.int32, (CAP, PATCHES), 0) == spot
    pick = jnp.where(hit, 1.0, 0.0)
    weight = jnp.sum(pick * gates[pl.ds(e, 1), :], axis=1, keepdims=True)
    pick = pick.astype(BF)
    x = mm(pick, n[...]).astype(BF)
    up = mm(pick, d3[...])
    dy = (weight * up).astype(BF)
    ff = lift.shape[-1]
    step = 512
    y = drop[0]
    dx = None
    base = 0 if own else CAP
    for f in range(ff // step):
        at = slice(f * step, (f + 1) * step)
        active, bend = gelu_both(mm(x, w_in[0, :, at]) + lift[0, :, at])
        active = active.astype(BF)
        du = (bend * mm_nt(dy, w_out[0, at, :])).astype(BF)
        y = y + mm(active, w_out[0, at, :])
        part = mm_nt(du, w_in[0, :, at])
        dx = part if dx is None else dx + part
        a_all[base : base + CAP, at] = active
        du_all[base : base + CAP, at] = du
    dots = jnp.sum(y * up, axis=1, keepdims=True)
    high = dots.astype(BF).astype(F32)
    lane = lane_ids()
    marks = jnp.where(lane == e, high, jnp.where(lane == e + EXPERTS, dots - high, 0.0))
    rhs = jnp.concatenate([(weight * y).astype(BF), dx.astype(BF), marks.astype(BF)], axis=1)
    home = mm_tn(pick, rhs)

    @pl.when(j == 0)
    def start():
        total[...] = home

    @pl.when(j == 1)
    def finish():
        pay[...] = (total[...] + home).astype(BF)

    if own:
        xs[0], dys[0], acts[0], dus[0] = x, dy, a_all[...], du_all[...]
    else:
        a_all[:CAP, :] = ao[0]
        du_all[:CAP, :] = duo[0]
        x_both = jnp.concatenate([xo[0], x], axis=0)
        dy_both = jnp.concatenate([dyo[0], dy], axis=0)
        d = x.shape[1]
        r = d // blocks
        for f in range(ff // step):
            at = slice(f * step, (f + 1) * step)
            grad[0, :, at] = mm_tn(x_both, du_all[:, at]).astype(BF)
        out = mm_tn(a_all[...], dy_both)
        for b in range(blocks):
            for s in range(4):
                at = (4 * b + s) * r
                grad[0, b * r : (b + 1) * r, ff + s * d : ff + (s + 1) * d] = out[at : at + r].astype(BF)
        lifts = jnp.sum(du_all[...].astype(F32), axis=0, keepdims=True)
        drops = jnp.sum(dy_both.astype(F32), axis=0, keepdims=True)
        small = spread_blocks(lifts, 0, blocks) + columns_of([drops], [4])
        grad[0, :, ff + 4 * d :] = small.astype(BF)


def experts(own, first_expert, image, task, n, routes_t, router_t, cot, dec, weights, blocks, saved=()):
    expert_in, expert_lift, expert_out, expert_drop = weights
    d, ff = expert_in.shape[1:]
    width = 2 * d + LANES
    one = lambda *shape: pl.BlockSpec((1,) + shape, lambda j, s: (s[0] + j,) + (0,) * len(shape))
    each = lambda *shape: pl.BlockSpec((1,) + shape, lambda j, s: (j,) + (0,) * len(shape))
    specs = [
        whole((PATCHES, d)),
        pl.BlockSpec((1, TOP, PATCHES), lambda j, s: (s[1], 0, 0)),
        pl.BlockSpec((1, EXPERTS, d), lambda j, s: (s[2], 0, 0)),
        pl.BlockSpec((PATCHES, cot.shape[1]), lambda j, s: (s[1], 0)),
        pl.BlockSpec((d, cot.shape[1]), lambda j, s: (0, s[2])),
        one(d, ff), one(1, ff), one(ff, d), one(1, d),
    ]
    arrays = [n, routes_t, router_t, cot, dec, expert_in, expert_lift[:, None], expert_out, expert_drop[:, None]]
    kept = [(CAP, d), (CAP, d), (CAP, ff), (CAP, ff)]
    pay = ((PATCHES, width), BF)
    if own:
        outs = [((2,) + k, BF) for k in kept] + [pay]
        out_specs = [each(*k) for k in kept] + [whole(pay[0])]
    else:
        specs += [each(*k) for k in kept]
        shape = (d, 2 * ff + LANES)
        outs = [((2,) + shape, BF), pay]
        out_specs = [each(*shape), whole(pay[0])]
    rows = CAP if own else 2 * CAP
    scratch = [
        VMEM((EXPERTS, PATCHES), F32), VMEM((EXPERTS, PATCHES), F32), VMEM((PATCHES, d), BF),
        VMEM((PATCHES, width), F32), VMEM((rows, ff), BF), VMEM((rows, ff), BF),
    ]
    return call(
        functools.partial(experts_kernel, blocks, own), jnp.stack([first_expert, image, task]),
        [*arrays, *saved], specs, outs, scratch, (2,), out_specs, flops=5e9,
    )


def attend_back_kernel(h, gain, w, m, n, q, k, v, o, up, core, dc_ref, do_ref, dqkv, first, second):
    d = h.shape[1]
    dc_ref[...] = up.astype(BF)
    do_ref[...] = mm_nt(dc_ref[...], m[...]).astype(BF)
    masks = side_masks()
    blocks = [(0, 256), (256, 256), (512, 64)]
    for p in range(d // LANES):
        at = slice(p * LANES, (p + 1) * LANES)
        keys, values = k[:, at], v[:, at]
        dk = dv = None
        for start, size in blocks:
            rows = slice(start, start + size)
            query, dout = q[rows, at], do_ref[rows, at]
            dq = None
            for mask in masks:
                scores = mm_nt(keys * mask, query)
                e = jnp.exp(scores - jnp.max(scores, axis=0, keepdims=True))
                probs = e * (1.0 / jnp.sum(e, axis=0, keepdims=True))
                dp = mm_nt(values * mask, dout)
                ds = (probs * (dp - jnp.sum(probs * dp, axis=0, keepdims=True))).astype(BF)
                part = mm(probs.astype(BF), dout * mask)
                dv = part if dv is None else dv + part
                part = mm(ds, query * mask)
                dk = part if dk is None else dk + part
                part = mm_tn(ds, keys * mask * SCALE)
                dq = part if dq is None else dq + part
            dqkv[rows, at] = dq.astype(BF)
        dqkv[:, d + p * LANES : d + (p + 1) * LANES] = dk.astype(BF)
        dqkv[:, 2 * d + p * LANES : 2 * d + (p + 1) * LANES] = dv.astype(BF)
    rows = [
        jnp.sum(dqkv[:, :d].astype(F32), axis=0, keepdims=True),
        jnp.sum(dqkv[:, 2 * d :].astype(F32), axis=0, keepdims=True),
        jnp.sum(dc_ref[...].astype(F32), axis=0, keepdims=True),
    ]
    back, grad_gain, grad_shift = norm_back(h, gain, mm_nt(dqkv[...], w[...]))

    @pl.when(core == 0)
    def queries():
        first[...] = mm_tn(n[...], dqkv[:, :d]).astype(BF)
        second[...] = mm_tn(n[...], dqkv[:, 2 * d :]).astype(BF)

    @pl.when(core == 1)
    def keys_and_merge():
        first[...] = mm_tn(n[...], dqkv[:, d : 2 * d]).astype(BF)
        second[...] = mm_tn(o[...], dc_ref[...]).astype(BF)

    return up + back, [grad_gain, grad_shift] + rows


def home_kernel(
    blocks, scalars, mine, near, second, n3, routes, router, cot, dec, dec_bias, mg, h_in, mw, m_m, n, q, k, v, o,
    decoded, d1, pay, small, full, third, dc, do, dqkv,
):
    core, task = scalars[1], scalars[2]
    d = second.shape[1]

    @pl.when(core == 0)
    def in_order():
        full[:HALF, :] = mine[...].astype(F32)
        full[HALF:, :] = near[...].astype(F32)

    @pl.when(core == 1)
    def swapped():
        full[:HALF, :] = near[...].astype(F32)
        full[HALF:, :] = mine[...].astype(F32)

    stream = second[...].astype(F32)
    third[...] = (stream + full[:, :d]).astype(BF)
    half = third[pl.ds(pl.multiple_of(core * HALF, 16), HALF), :]
    decoded[...] = mm(half, dec[...]) + dec_bias[0]
    hdec = cot.shape[1] // 2
    part = cot[:, pl.ds(pl.multiple_of(core * hdec, LANES), hdec)]
    table = mm_tn(third[...], part)
    pay[0, :, d:] = jnp.where(task == 0, table, 0.0).astype(BF)
    pay[1, :, d:] = jnp.where(task == 1, table, 0.0).astype(BF)

    lane = lane_ids()
    member = jnp.zeros((PATCHES, LANES), F32)
    for i in range(TOP):
        member = member + jnp.where(lane == routes[:, i : i + 1], 1.0, 0.0)
    logits = jnp.where(member > 0.0, mm(n3[...], router[0]), -1e30)
    e = jnp.where(member > 0.0, jnp.exp(logits - jnp.max(logits, axis=1, keepdims=True)), 0.0)
    gates = e / jnp.sum(e, axis=1, keepdims=True)
    dots = full[:, 2 * d :]
    dots = dots + pltpu.roll(dots, LANES - EXPERTS, 1)
    dz = gates * (dots - jnp.sum(gates * dots, axis=1, keepdims=True))
    high = dz.astype(BF).astype(F32)
    low = dz - high
    moved = lambda x: jnp.where(task == 0, x, pltpu.roll(x, EXPERTS, 1)).astype(BF)
    grad_router = mm_tn(n3[...], moved(high)) + mm_tn(n3[...], moved(low))
    dn = full[:, d : 2 * d] + mm_nt(high.astype(BF), router[0]) + mm_nt(low.astype(BF), router[0])
    back, gain1, shift1 = norm_back(stream, mg[1:2], dn)
    up = (mm_nt(cot[...], dec[...]).astype(BF).astype(F32) + back).astype(BF).astype(F32)
    result, rows = attend_back_kernel(
        h_in[...].astype(F32), mg[0:1], mw, m_m, n, q, k, v, o, up, core, dc, do, dqkv,
        pay.at[0, :, :d], pay.at[1, :, :d],
    )
    d1[...] = result.astype(BF)
    gain0, shift0, b0, b1, b2 = rows
    small[...] = grad_router + columns_of(
        [gain0, gain1, shift0, shift1, b0, b1, b2], [16, 17, 18, 19, 20, 21, 22]
    )
    owners = jnp.sum(cot[...].astype(F32), axis=0, keepdims=True)
    count = cot.shape[1]
    column = columns_of([owners], [24])
    column = jnp.where(task == 0, column, pltpu.roll(column, 1, 1))
    r, some = d // blocks, count // blocks
    for b in range(blocks):
        small[b * r : b * r + some, :] += column[b * some : (b + 1) * some]


def home(image, core, task, mine, near, second, n3, routes, router, cot, dec, dec_bias, mg, first, mw, m_m, saved, blocks):
    d = second.shape[1]
    width = cot.shape[1]
    at_image = lambda shape: pl.BlockSpec(shape, lambda i, s: (s[0], 0))
    specs = [
        whole(mine.shape), whole(near.shape), whole(second.shape), whole(n3.shape), at_image((PATCHES, TOP)),
        pl.BlockSpec((1, d, LANES), lambda i, s: (s[2], 0, 0)), at_image((PATCHES, width)),
        pl.BlockSpec((d, width), lambda i, s: (0, s[2])), pl.BlockSpec((1, 1, width), lambda i, s: (s[2], 0, 0)),
        whole(mg.shape), whole(first.shape), whole(mw.shape), whole(m_m.shape),
    ] + [whole(x.shape) for x in saved]
    outs = [
        ((HALF, width), F32), ((PATCHES, d), BF), ((2, d, d + width // 2), BF), ((d, LANES), F32),
    ]
    scratch = [
        VMEM((PATCHES, 2 * d + LANES), F32), VMEM((PATCHES, d), BF), VMEM((PATCHES, d), BF), VMEM((PATCHES, d), BF),
        VMEM((PATCHES, 3 * d), BF),
    ]
    return call(
        functools.partial(home_kernel, blocks), jnp.stack([image, core, task]),
        [mine, near, second, n3, routes, router, cot, dec, dec_bias[:, None], mg, first, mw, m_m, *saved],
        specs, outs, scratch, flops=6e9,
    )


def dense_back_kernel(
    blocks, scalars, d1, act, slope, n1, a0, sg, sx, sr, small_in, da, pay, small, du_all
):
    core = scalars[0]
    d, ff = sx.shape
    step = 512
    dn = None
    for f in range(ff // step):
        at = slice(f * step, (f + 1) * step)
        du = (slope[:, at].astype(F32) * mm_nt(d1[...], sr[at, :])).astype(BF)
        du_all[:, at] = du
        part = mm_nt(du, sx[:, at])
        dn = part if dn is None else dn + part
    up = d1[...].astype(F32)
    back, gain1, shift1 = norm_back(a0[...], sg[1:2], dn)
    da[...] = up + back
    lifts = jnp.sum(du_all[...].astype(F32), axis=0, keepdims=True)
    b3 = jnp.sum(up, axis=0, keepdims=True)
    small[...] = (
        small_in[...] + spread_blocks(lifts, 40, blocks) + columns_of([gain1, shift1, b3], [33, 35, 39])
    )

    @pl.when(core == 0)
    def expand():
        for y in range(2):
            pay[y] = mm_tn(n1[...], du_all[:, y * ff // 2 : (y + 1) * ff // 2]).astype(BF)

    @pl.when(core == 1)
    def reduce():
        r = d // blocks
        out = mm_tn(act[...], d1[...])
        for b in range(blocks):
            for s in range(4):
                at = (4 * b + s) * r
                pay[s // 2, b * r : (b + 1) * r, (s % 2) * d : (s % 2 + 1) * d] = out[at : at + r].astype(BF)


def dense_back(core, d1, act, slope, n1, a0, sg, sx, sr, small_in, blocks):
    d, ff = sx.shape
    arrays = [d1, act, slope, n1, a0, sg, sx, sr, small_in]
    outs = [((PATCHES, d), F32), ((2, d, ff // 2), BF), ((d, LANES), F32)]
    return call(
        functools.partial(dense_back_kernel, blocks), core[None], arrays, [whole(x.shape) for x in arrays], outs,
        [VMEM((PATCHES, ff), BF)], flops=4e9,
    )


def stem_back_kernel(scalars, da, tok, sg, sw, sm, n, q, k, v, o, small_in, d0, pay, full, dc, do, dqkv):
    core = scalars[1]
    d = da.shape[1]
    result, rows = attend_back_kernel(
        tok[...].astype(F32), sg[0:1], sw, sm, n, q, k, v, o, da[...], core, dc, do, dqkv,
        pay.at[0, :, :d], pay.at[1, :, :d],
    )
    full[...] = result
    d0[...] = full[pl.ds(pl.multiple_of(core * HALF, 8), HALF), :]
    gain0, shift0, b0, b1, b2 = rows
    small = small_in[...] + columns_of([gain0, shift0, b0, b1, b2], [32, 34, 36, 37, 38])
    pay[0, :, d:] = jnp.where(core == 0, small, 0.0).astype(BF)
    pay[1, :, d:] = jnp.zeros((d, LANES), BF)


def stem_back(image, core, da, tokens, sg, sw, sm, saved, small_in):
    d = da.shape[1]
    specs = [
        whole(da.shape), pl.BlockSpec((PATCHES, d), lambda i, s: (s[0], 0)), whole(sg.shape), whole(sw.shape),
        whole(sm.shape),
    ] + [whole(x.shape) for x in saved] + [whole(small_in.shape)]
    outs = [((HALF, d), F32), ((2, d, d + LANES), BF)]
    scratch = [
        VMEM((PATCHES, d), F32), VMEM((PATCHES, d), BF), VMEM((PATCHES, d), BF), VMEM((PATCHES, 3 * d), BF),
    ]
    return call(
        stem_back_kernel, jnp.stack([image, core]), [da, tokens, sg, sw, sm, *saved, small_in], specs, outs, scratch,
        flops=6e9,
    )


def swap(x, axis, mask):
    size = lax.axis_size(axis)
    return lax.ppermute(x, axis, [(i, i ^ mask) for i in range(size)])


def add_low(*terms):
    return sum(t.astype(F32) for t in terms).astype(BF)


def line_reduce(x):
    nz = x.shape[0]
    z = lax.axis_index("dp") // 2
    own = lax.dynamic_index_in_dim(x, z, 0, keepdims=False)
    up = down = None
    for step in range(1, nz):
        chunk = lax.dynamic_index_in_dim(x, jnp.clip(z + nz - step, 0, nz - 1), 0, keepdims=False)
        send = chunk if up is None else add_low(chunk, up)
        up = lax.ppermute(send, "dp", [(2 * i + p, 2 * i + 2 + p) for i in range(step) for p in range(2)])
        chunk = lax.dynamic_index_in_dim(x, jnp.clip(z - nz + step, 0, nz - 1), 0, keepdims=False)
        send = chunk if down is None else add_low(chunk, down)
        route = [(2 * i + p, 2 * i - 2 + p) for i in range(nz - step, nz) for p in range(2)]
        down = lax.ppermute(send, "dp", route)
    return add_low(own, up, down)


def pair_reduce(x, dim):
    side = lax.axis_index("dp") % 2
    got = swap(lax.dynamic_index_in_dim(x, 1 - side, dim, keepdims=False), "dp", 1)
    return add_low(lax.dynamic_index_in_dim(x, side, dim, keepdims=False), got)


def split_pairs(x):
    ndp = lax.axis_size("dp")
    return x.reshape((ndp // 2, 2, x.shape[0] // ndp) + x.shape[1:])


def pair_first(x):
    return line_reduce(pair_reduce(split_pairs(x), 1))


def line_first(x):
    return pair_reduce(line_reduce(split_pairs(x)), 0)


def section_exchange(x):
    s = lax.axis_index("section")
    parts = [lax.dynamic_index_in_dim(x, s, 0, keepdims=False)]
    for mask in (1, 2, 3):
        parts.append(swap(lax.dynamic_index_in_dim(x, s ^ mask, 0, keepdims=False), "section", mask))
    stacked = jnp.stack(parts)
    return jnp.stack([lax.dynamic_index_in_dim(stacked, s ^ t, 0, keepdims=False) for t in range(4)])


def exchange_pieces(pieces):
    sizes = [p.shape[1] for p in pieces]
    out = section_exchange(jnp.concatenate(pieces, axis=1)).astype(F32)
    ends = [sum(sizes[: i + 1]) for i in range(len(sizes))]
    return [out[:, e - n : e] for e, n in zip(ends, sizes)]


def body(
    tokens, routes, task_ids, cotangent, stem_gains, stem_shifts, stem_heads, stem_merge,
    stem_biases, stem_expand, stem_lift, stem_reduce, mix_gains, mix_shifts, mix_heads,
    mix_merge, mix_biases, router, expert_in, expert_lift, expert_out, expert_drop, decoder,
    decoder_bias,
):
    s = lax.axis_index("section")
    image, core = s // 2, s % 2
    ndp, ns = lax.axis_size("dp"), lax.axis_size("section")
    d, ff, dec = tokens.shape[1], stem_expand.shape[1], cotangent.shape[1]
    r, f = d // ndp, ff // ndp
    q = r // ns

    weights = [
        stem_gains, stem_shifts, stem_heads, stem_merge, stem_biases, stem_expand, stem_lift[None], stem_reduce,
        mix_gains, mix_shifts, mix_heads, mix_merge, mix_biases,
    ]
    (n0, q0, k0, v0, o0, a0, n1, act, slope, first, n2, q2, k2, v2, o2, second, n3) = forward(image, tokens, weights)

    cut = lambda x, c: lax.dynamic_slice_in_dim(x, c * HALF, HALF, 0)
    join = lambda mine, near: jnp.concatenate(
        [jnp.where(core == 0, mine, near), jnp.where(core == 0, near, mine)], axis=0
    )
    far = swap(cut(n3, core), "section", 2)
    other = join(far, swap(far, "section", 1))

    routes_t = routes.reshape(-1, PATCHES, TOP).transpose(0, 2, 1)
    router_t = router.transpose(1, 2, 0)
    router_wide = jnp.pad(router.transpose(1, 0, 2), ((0, 0), (0, 0), (0, LANES - EXPERTS)))
    dec_flat = decoder.reshape(d, -1)
    expert_weights = (expert_in, expert_lift, expert_out, expert_drop)
    *kept, own = experts(
        True, 2 * s, image, task_ids[image], n3, routes_t, router_t, cotangent, dec_flat, expert_weights, ndp
    )
    heavy, away = experts(
        False, 2 * s, 1 - image, task_ids[1 - image], other, routes_t, router_t, cotangent, dec_flat,
        expert_weights, ndp, kept,
    )
    own = add_low(cut(own, core), swap(cut(own, 1 - core), "section", 1))
    away = add_low(cut(away, core), swap(cut(away, 1 - core), "section", 1))
    mine = add_low(own, swap(away, "section", 2))
    near = swap(mine, "section", 1)

    heavy = [line_first(heavy[0]), pair_first(heavy[1])]

    decoded, d1, mix_pay, small = home(
        image, core, task_ids[image], mine, near, second, n3, routes, router_wide, cotangent, dec_flat, decoder_bias,
        mix_gains, first, mix_heads, mix_merge, (n2, q2, k2, v2, o2), ndp,
    )

    def chips(pay):
        got = swap(lax.dynamic_index_in_dim(pay, 1 - image, 0, keepdims=False), "section", 2)
        return add_low(lax.dynamic_index_in_dim(pay, image, 0, keepdims=False), got)

    mix = pair_first(chips(mix_pay))
    da, dense_pay, small = dense_back(
        core, d1, act, slope, n1, a0, stem_gains, stem_expand, stem_reduce, small, ndp
    )
    dense = pair_first(chips(dense_pay))
    d0, stem_pay = stem_back(
        image, core, da, tokens, stem_gains, stem_heads, stem_merge, (n0, q0, k0, v0, o0), small
    )
    stem = pair_first(chips(stem_pay))

    rows = lambda x: x.reshape(ns, -1)
    pieces = []
    for x in heavy:
        pieces.append(rows(x[:, :ff]))
        pieces.append(rows(x[:, ff : ff + ns * d].reshape(r, ns, d).transpose(1, 0, 2)))
        pieces.append(rows(x[:, ff + ns * d : ff + ns * d + ns].T))
        pieces.append(rows(x[:, ff + ns * d + ns]))
    p = exchange_pieces(pieces)
    merge = lambda a, b, *shape: jnp.stack([a.reshape(ns, *shape), b.reshape(ns, *shape)], 1).reshape(EXPERTS, *shape)
    grad_in = merge(p[0], p[4], q, ff)
    grad_out = merge(p[1], p[5], r, d)
    grad_elift = merge(p[2], p[6], r)
    grad_edrop = merge(p[3], p[7], q)

    wide = dense.reshape(r, 2, d)
    owner = jnp.arange(ns)
    reduced = jnp.where(
        (owner // 2 == image)[:, None], jnp.stack([wide[:, 0], wide[:, 1]] * 2).reshape(ns, -1), jnp.zeros((), BF)
    )
    expanded = jnp.pad(rows(dense), ((0, 0), (0, r * d - q * ff // 2)))
    some = dec // ndp
    pieces = [
        rows(mix[:, :d]), rows(mix[:, d:]), jnp.where(core == 0, expanded, reduced), rows(stem[:, :d]),
        rows(stem[:, d:]), rows(stem[:some, d + 24 : d + 26]),
        rows(stem[:, d + 40 : d + 40 + ns].T),
    ]
    p = exchange_pieces(pieces)

    def heads(x):
        x = x.reshape(ns, q, d)
        return jnp.concatenate([x[0], x[1], x[2]], axis=1), x[3]

    g_mix_heads, g_mix_merge = heads(p[0])
    g_stem_heads, g_stem_merge = heads(p[3])
    x = p[1].reshape(2, 2, q, dec // 2)
    g_dec = jnp.concatenate([x[:, 0], x[:, 1]], axis=2).transpose(1, 0, 2)
    half = q * ff // 2
    g_expand = jnp.concatenate([p[2][0, :half].reshape(q, -1), p[2][2, :half].reshape(q, -1)], axis=1)
    g_reduce = jnp.where(s // 2 == 0, p[2][1], p[2][3]).reshape(r, d)
    small = p[4][0].reshape(q, LANES)
    lanes = lambda *at: jnp.stack([small[:, i] for i in at])
    g_db = p[5][0].reshape(some // ns, 2).T
    g_lift = p[6][0]
    return (
        decoded, d0, lanes(32, 33), lanes(34, 35), g_stem_heads, g_stem_merge, lanes(36, 37, 38, 39), g_expand,
        g_lift, g_reduce, lanes(16, 17), lanes(18, 19), g_mix_heads, g_mix_merge, lanes(20, 21, 22),
        small[:, : 2 * EXPERTS].reshape(q, 2, EXPERTS), grad_in, grad_elift, grad_out, grad_edrop, g_dec, g_db,
    )


def solution(mesh):
    both = ("dp", "section")
    placed = (P("dp", None), P("dp", None), P("dp"), P("dp", None)) + (P(),) * 20
    rows, columns = P(both, None), P(None, both)
    return jax.shard_map(
        body,
        mesh=mesh,
        in_specs=placed,
        out_specs=(
            rows, rows, columns, columns, rows, rows, columns, rows, P(both), rows, columns,
            columns, rows, rows, columns, P(both, None, None), P(None, both, None), columns,
            P(None, both, None), columns, P(both, None, None), columns,
        ),
        check_vma=False,
    )
```

```python
import functools
import math

import jax
import jax.numpy as jnp
from jax import lax
from jax.experimental import pallas as pl
from jax.experimental.pallas import tpu as pltpu
from jax.sharding import PartitionSpec as P

HEADS = 6
HDIM = 64
EXPERTS = 8
TOP = 4
PATCHES = 576
HALF = PATCHES // 2
CAP = 288
LANES = 128
EPSILON = 1e-06
SCALE = 1.0 / math.sqrt(HDIM)
BF = jnp.bfloat16
F32 = jnp.float32
VMEM = pltpu.VMEM
MIB = 1 << 20


def mm(a, b):
    return jnp.dot(a, b, preferred_element_type=F32)


def mm_tn(a, b):
    return lax.dot_general(a, b, (((0,), (0,)), ((), ())), preferred_element_type=F32)


def mm_nt(a, b):
    return lax.dot_general(a, b, (((1,), (1,)), ((), ())), preferred_element_type=F32)


def split_low(v):
    high = v.astype(BF)
    return high, (v - high.astype(F32)).astype(BF)


def norm_parts(v):
    centred = v - jnp.mean(v, axis=-1, keepdims=True)
    inverse = lax.rsqrt(jnp.mean(centred * centred, axis=-1, keepdims=True) + EPSILON)
    return centred * inverse, inverse


def norm_back(v, gain, up):
    unit, inverse = norm_parts(v)
    scaled = up * gain
    back = inverse * (
        scaled
        - jnp.mean(scaled, axis=-1, keepdims=True)
        - unit * jnp.mean(scaled * unit, axis=-1, keepdims=True)
    )
    return back, jnp.sum(up * unit, axis=0, keepdims=True), jnp.sum(up, axis=0, keepdims=True)


def gelu_both(u):
    t = pl.reciprocal(1.0 + (0.3275911 / math.sqrt(2.0)) * jnp.abs(u), approx=True)
    bell = jnp.exp2((-0.5 / math.log(2.0)) * u * u)
    poly = 0.5 * 1.421413741 + t * (0.5 * -1.453152027 + t * (0.5 * 1.061405429))
    tail = bell * (t * (0.5 * 0.254829592 + t * (0.5 * -0.284496736 + t * poly)))
    cdf = jnp.where(u >= 0.0, 1.0 - tail, tail)
    return u * cdf, cdf + u * bell * (1.0 / math.sqrt(2.0 * math.pi))


def side_masks():
    lane = lax.broadcasted_iota(jnp.int32, (1, LANES), 1)
    left = (lane < HDIM).astype(F32)
    return left.astype(BF), (1.0 - left).astype(BF)


def deal(pay, value, at):
    r, w = pay.shape[3], value.shape[1]
    for b in range(pay.shape[1] * pay.shape[2]):
        for y in range(2):
            piece = value[(2 * b + y) * r : (2 * b + y + 1) * r]
            pay[y, b % 2, b // 2, :, at : at + w] = piece.astype(BF)


def deal_long(pay, value):
    r, w = pay.shape[3], value.shape[1]
    for b in range(pay.shape[1] * pay.shape[2]):
        for y in range(2):
            for k in range(4):
                piece = value[(8 * b + 4 * y + k) * r : (8 * b + 4 * y + k + 1) * r]
                pay[y, b % 2, b // 2, :, k * w : (k + 1) * w] = piece.astype(BF)


def light_shape(d, blocks, width):
    return (2, 2, blocks // 2, d // blocks // 2, width)


def lane_ids(rows=1):
    return lax.broadcasted_iota(jnp.int32, (rows, LANES), 1)


def columns_of(rows, lanes):
    count = -(-len(rows) // 8) * 8
    n = rows[0].shape[1]
    stacked = jnp.concatenate(rows + [jnp.zeros((count - len(rows), n), F32)], axis=0)
    place = lax.broadcasted_iota(jnp.int32, (count, LANES), 0)
    lane = lane_ids(count)
    spread = jnp.zeros((count, LANES), F32)
    for i, at in enumerate(lanes):
        spread = spread + jnp.where((place == i) & (lane == at), 1.0, 0.0)
    return mm_tn(stacked.astype(BF), spread.astype(BF))


def spread_blocks(row, first_lane, blocks):
    n = row.shape[1]
    r = n // 4 // blocks
    place = lax.broadcasted_iota(jnp.int32, (8, LANES), 0)
    stacked = jnp.concatenate([row, jnp.zeros((7, n), F32)], axis=0)
    column = mm_tn(stacked.astype(BF), jnp.where(place == 0, 1.0, 0.0).astype(BF))
    lane = lane_ids()
    parts = []
    for b in range(blocks):
        part = None
        for s in range(4):
            at = (4 * b + s) * r
            piece = jnp.where(lane == first_lane + s, column[at : at + r], 0.0)
            part = piece if part is None else part + piece
        parts.append(part)
    return jnp.concatenate(parts, axis=0)


class Fetched:
    def __init__(self, moves):
        self.moves = moves
        for move in moves:
            move.start()

    def wait(self):
        for move in self.moves:
            move.wait()
        self.moves = []


def run_kernel(body, n_in, n_out, picks, places, *refs):
    section, tasks = refs[:2]
    inputs, outputs = refs[2 : 2 + n_in], refs[2 + n_in : 2 + n_in + n_out]
    rest = refs[2 + n_in + n_out :]
    kept_in, kept_out = rest[:n_in], rest[n_in : n_in + n_out]
    in_sems, out_sems = rest[n_in + n_out : n_in + n_out + 2]
    at = (section[0], section[0] // 2, section[0] % 2, tasks, section[1])
    fetched, moving = [], []
    for i in range(n_in):
        source = inputs[i] if picks[i] is None else inputs[i].at[picks[i](*at[:4])]
        fetched.append(Fetched([pltpu.make_async_copy(source, kept_in[i], in_sems.at[i])]))

    def get(i):
        fetched[i].wait()
        return kept_in[i]

    def put(i, source=None, part=None):
        source = kept_out[i] if source is None else source
        target = outputs[i] if part is None else outputs[i].at[part]
        move = pltpu.make_async_copy(source, target, out_sems.at[i if part is None else i + part * n_out])
        move.start()
        moving.append(move)

    body(at, get, put, kept_out, *rest[n_in + n_out + 2 :])
    for i in range(n_in):
        get(i)
    for move in moving:
        move.wait()


def call(body, section, tasks, inputs, outs, scratch=(), flops=1e9, limit=56):
    arrays, picks, kept = [], [], []
    for x in inputs:
        array, pick, shape = x if isinstance(x, tuple) else (x, None, x.shape)
        arrays.append(array)
        picks.append(pick)
        kept.append(VMEM(shape, array.dtype))
    kept_out = [VMEM(o[0], o[1]) if len(o) == 2 else VMEM((8, LANES), F32) for o in outs]
    anywhere, scalar = pl.BlockSpec(memory_space=pl.ANY), pl.BlockSpec(memory_space=pltpu.SMEM)
    return pl.pallas_call(
        functools.partial(run_kernel, body, len(arrays), len(outs), picks, None),
        out_shape=[jax.ShapeDtypeStruct(o[0], o[1]) for o in outs],
        in_specs=[scalar, scalar] + [anywhere] * len(arrays),
        out_specs=[anywhere] * len(outs),
        scratch_shapes=[
            *kept, *kept_out, pltpu.SemaphoreType.DMA((len(arrays),)), pltpu.SemaphoreType.DMA((2 * len(outs),)), *scratch
        ],
        compiler_params=pltpu.CompilerParams(vmem_limit_bytes=limit * MIB),
        cost_estimate=pl.CostEstimate(flops=1, bytes_accessed=1, transcendentals=0),
    )(section, tasks, *arrays)


def rows_of(count):
    return lambda s, image, core, tasks: pl.ds(pl.multiple_of(image * count, count), count)


def of_task(s, image, core, tasks):
    return tasks[image]


def attend_kernel(h, gain, shift, get_w, c, get_m, n_ref, q_ref, k_ref, v_ref, o_ref, lse_ref, done):
    d = h.shape[1]
    unit, unused = norm_parts(h)
    n_ref[...] = (unit * gain + shift).astype(BF)
    done(0)
    n, w = n_ref[...], get_w()
    q_ref[...] = ((mm(n, w[:, :d]) + c[0:1]) * SCALE).astype(BF)
    done(1)
    k_ref[...] = mm(n, w[:, d : 2 * d]).astype(BF)
    done(2)
    v_ref[...] = (mm(n, w[:, 2 * d :]) + c[1:2]).astype(BF)
    done(3)
    masks = side_masks()
    lane = lane_ids()
    sums = jnp.zeros((PATCHES, LANES), F32)
    step = 32
    for p in range(d // LANES):
        at = slice(p * LANES, (p + 1) * LANES)
        total = None
        for i, mask in enumerate(masks):
            scores = mm_nt(q_ref[:, at] * mask, k_ref[:, at])
            e, norm, top = [], [], []
            for r in range(PATCHES // step):
                part = scores[r * step : (r + 1) * step]
                most = jnp.max(part, axis=-1, keepdims=True)
                part = jnp.exp(part - most)
                e.append(part.astype(BF))
                norm.append(jnp.sum(part, axis=-1, keepdims=True))
                top.append(most)
            norm = jnp.concatenate(norm, axis=0)
            part = mm(jnp.concatenate(e, axis=0), v_ref[:, at] * mask) * (1.0 / norm)
            total = part if total is None else total + part
            sums = jnp.where(lane == 2 * p + i, jnp.concatenate(top, axis=0) + jnp.log(norm), sums)
        o_ref[:, at] = total.astype(BF)
    lse_ref[...] = sums
    done(4)
    done(5)
    return h + (mm(o_ref[...], get_m()[...]) + c[2:3])


def forward_body(at, get, put, out, *scratch):
    tok, sw, sg, ss, sb, sm, sx, sl, sr, mw, mg, ms, mb, m_m = range(14)
    (n0, q0, k0, v0, o0, l0, a0, n1, act, slope, first, n2, q2, k2, v2, o2, l2, second, n3, n3_cut) = out
    h = get(tok)[...].astype(F32)
    sg, ss, sb = get(sg), get(ss), get(sb)
    a = attend_kernel(
        h, sg[0:1], ss[0:1], lambda: get(sw), sb, lambda: get(sm), n0, q0, k0, v0, o0, l0, put
    )
    a0[...] = a
    put(6)
    unit, unused = norm_parts(a0[...])
    n1[...] = (unit * sg[1:2] + ss[1:2]).astype(BF)
    put(7)
    step = 512
    wx, lift = get(sx), get(sl)
    for f in range(wx.shape[1] // step):
        cols = slice(f * step, (f + 1) * step)
        active, bend = gelu_both(mm(n1[...], wx[:, cols]) + lift[cols][None, :])
        act[:, cols] = active.astype(BF)
        slope[:, cols] = bend.astype(BF)
    put(8)
    put(9)
    first[...] = (a0[...] + (mm(act[...], get(sr)[...]) + sb[3:4])).astype(BF)
    put(10)
    mg, ms, mb = get(mg), get(ms), get(mb)
    second[...] = attend_kernel(
        first[...].astype(F32), mg[0:1], ms[0:1], lambda: get(mw), mb, lambda: get(m_m), n2, q2, k2, v2,
        o2, l2, lambda i: put(11 + i),
    ).astype(BF)
    put(17)
    unit, unused = norm_parts(second[...].astype(F32))
    n3[...] = (unit * mg[1:2] + ms[1:2]).astype(BF)
    put(18)
    put(19, n3.at[pl.ds(pl.multiple_of(at[2] * HALF, 16), HALF), :])


def forward(section, tasks, tokens, weights):
    d = tokens.shape[1]
    ff = weights[5].shape[1]
    wide = ((PATCHES, d), BF)
    sums = ((PATCHES, LANES), F32)
    outs = [wide] * 5 + [sums, ((PATCHES, d), F32), wide, ((PATCHES, ff), BF), ((PATCHES, ff), BF)]
    outs += [wide] * 6 + [sums, wide, wide, ((HALF, d), BF, None)]
    inputs = [(tokens, rows_of(PATCHES), (PATCHES, d)), *weights]
    return call(forward_body, section, tasks, inputs, outs, flops=2e10)


def experts_body(own, at, get, put, out, gates, place, d3, n_all):
    n, routes, router, cot, dec, w_in0, w_in1, lift, w_out0, w_out1, drop = range(11)
    send, keep, xs, dys, acts, dus, full = out
    core = at[2]
    if own:
        n_ref = get(n)
    else:
        n_all[pl.ds(pl.multiple_of(core * HALF, 16), HALF), :] = get(n)[...]
        n_all[pl.ds(pl.multiple_of((1 - core) * HALF, 16), HALF), :] = get(11)[...]
        n_ref = n_all
    ids = lax.broadcasted_iota(jnp.int32, (EXPERTS, PATCHES), 0)
    member = jnp.zeros((EXPERTS, PATCHES), F32)
    named = get(routes)
    for k in range(TOP):
        member = member + jnp.where(ids == named[k : k + 1, :], 1.0, 0.0)
    logits = jnp.where(member > 0.0, mm_nt(get(router)[...], n_ref[...]), -1e30)
    e = jnp.where(member > 0.0, jnp.exp(logits - jnp.max(logits, axis=0, keepdims=True)), 0.0)
    gates[...] = e / jnp.sum(e, axis=0, keepdims=True)
    before = lax.broadcasted_iota(jnp.int32, (PATCHES, PATCHES), 0)
    after_ = lax.broadcasted_iota(jnp.int32, (PATCHES, PATCHES), 1)
    upper = jnp.where(before <= after_, 1.0, 0.0).astype(BF)
    place[...] = jnp.where(member > 0.0, mm(member.astype(BF), upper) - 1.0, -1.0)
    d3[...] = mm_nt(get(cot)[...], get(dec)[...]).astype(BF)
    total = None
    lifts, drops = get(lift), get(drop)
    for j in range(2):
        e = 2 * at[0] + j
        spot = place[pl.ds(e, 1), :].astype(jnp.int32)
        hit = lax.broadcasted_iota(jnp.int32, (CAP, PATCHES), 0) == spot
        pick = jnp.where(hit, 1.0, 0.0)
        weight = jnp.sum(pick * gates[pl.ds(e, 1), :], axis=1, keepdims=True)
        pick = pick.astype(BF)
        x = mm(pick, n_ref[...]).astype(BF)
        up = mm(pick, d3[...])
        dy = (weight * up).astype(BF)
        xs[j] = x
        dys[j] = dy
        w_in, w_out = get((w_in0, w_in1)[j]), get((w_out0, w_out1)[j])
        ff = w_in.shape[1]
        step = 512
        y = drops[pl.ds(e, 1), :]
        dx = None
        for f in range(ff // step):
            cols = slice(f * step, (f + 1) * step)
            active, bend = gelu_both(mm(x, w_in[:, cols]) + lifts[pl.ds(e, 1), cols])
            active = active.astype(BF)
            du = (bend * mm_nt(dy, w_out[cols, :])).astype(BF)
            y = y + mm(active, w_out[cols, :])
            part = mm_nt(du, w_in[:, cols])
            dx = part if dx is None else dx + part
            acts[j, :, cols] = active
            dus[j, :, cols] = du
        for i, kept in enumerate((xs, dys, acts, dus)):
            put(2 + i, kept.at[j], j)
        dots = jnp.sum(y * up, axis=1, keepdims=True)
        high = dots.astype(BF).astype(F32)
        lane = lane_ids()
        marks = jnp.where(lane == e, high, jnp.where(lane == e + EXPERTS, dots - high, 0.0))
        rhs = jnp.concatenate([(weight * y).astype(BF), dx.astype(BF), marks.astype(BF)], axis=1)
        home = mm_tn(pick, rhs)
        total = home if total is None else total + home
    full[...] = total.astype(BF)
    put(0, full.at[pl.ds(pl.multiple_of((1 - core) * HALF, 16), HALF), :])
    put(1, full.at[pl.ds(pl.multiple_of(core * HALF, 16), HALF), :])


def experts(own, section, tasks, n, routes_t, router_t, cot, dec, weights):
    expert_in, expert_lift, expert_out, expert_drop = weights
    d, ff = expert_in.shape[1:]
    width = 2 * d + LANES
    look = (lambda image: image) if own else (lambda image: 1 - image)
    which = lambda j: lambda s, image, core, tasks: 2 * s + j
    inputs = [
        n[0],
        (routes_t, lambda s, image, core, tasks: look(image), (TOP, PATCHES)),
        (router_t, lambda s, image, core, tasks: tasks[look(image)], (EXPERTS, d)),
        (cot, lambda s, image, core, tasks: pl.ds(pl.multiple_of(look(image) * PATCHES, PATCHES), PATCHES),
         (PATCHES, cot.shape[1])),
        (dec, lambda s, image, core, tasks: (
            slice(None), pl.ds(pl.multiple_of(tasks[look(image)] * cot.shape[1], LANES), cot.shape[1])),
         (d, cot.shape[1])),
        (expert_in, which(0), (d, ff)), (expert_in, which(1), (d, ff)), expert_lift,
        (expert_out, which(0), (ff, d)), (expert_out, which(1), (ff, d)), expert_drop, *n[1:],
    ]
    half = ((HALF, width), BF, None)
    outs = [half, half, ((2, CAP, d), BF), ((2, CAP, d), BF), ((2, CAP, ff), BF), ((2, CAP, ff), BF)]
    scratch = [
        VMEM((PATCHES, width), BF), VMEM((EXPERTS, PATCHES), F32), VMEM((EXPERTS, PATCHES), F32),
        VMEM((PATCHES, d), BF), VMEM((PATCHES, d), BF),
    ]

    def body(at, get, put, out, full, *rest):
        experts_body(own, at, get, put, [*out, full], *rest)

    return call(body, section, tasks, inputs, outs, scratch, flops=1e10)


def weight_grads(expert, section, tasks, own, far, blocks):
    d, ff = own[0].shape[2], own[2].shape[2]
    r = d // blocks // 4
    part = lambda x: (x, lambda s, image, core, tasks: expert, x.shape[1:])
    inputs = [part(x) for pair in zip(own, far) for x in pair]
    shape = (2, blocks // 2, 4, 2 * r, ff + LANES)

    def body(at, get, put, out, pay):
        both = lambda i: jnp.concatenate([get(2 * i)[...], get(2 * i + 1)[...]], axis=0)
        x, du = both(0), both(3)
        step = 512
        grad_in = [mm_tn(x, du[:, f * step : (f + 1) * step]) for f in range(ff // step)]
        lifts = jnp.sum(du.astype(F32), axis=0, keepdims=True)
        dy = both(1)
        drops = jnp.sum(dy.astype(F32), axis=0, keepdims=True)
        small = spread_blocks(lifts, 0, 4 * blocks) + columns_of([drops], [4])
        grad_out = mm_tn(both(2), dy)
        for b in range(blocks):
            i, j = (b % 2, b // 2) if expert == 0 else divmod(b, blocks // 2)
            for t in range(4):
                row = (4 * b + t) * r
                for f, value in enumerate(grad_in):
                    pay[i, j, t, :r, f * step : (f + 1) * step] = value[row : row + r].astype(BF)
                pay[i, j, t, :r, ff:] = small[row : row + r].astype(BF)
                for k in range(4):
                    at_row = (4 * (4 * b + t) + k) * r
                    pay[i, j, t, r:, k * d : (k + 1) * d] = grad_out[at_row : at_row + r].astype(BF)
                pay[i, j, t, r:, ff:] = jnp.zeros((r, LANES), BF)
        if expert == 0:
            put(0, pay.at[1 - at[4]])
            put(1, pay.at[at[4]])
        else:
            put(0, pay)

    half = (shape[1:], BF, None)
    outs = [half, half] if expert == 0 else [(shape, BF, None)]
    return call(body, section, tasks, inputs, outs, [VMEM(shape, BF)], flops=8e9)


def exact_rows(columns):
    sub = lax.broadcasted_iota(jnp.int32, (8, LANES), 0)
    eye = jnp.where(sub == lax.broadcasted_iota(jnp.int32, (8, LANES), 1), 1.0, 0.0).astype(BF)
    high, rest = split_low(columns)
    middle, low = split_low(columns - high.astype(F32))
    del rest
    return mm_nt(eye, high) + mm_nt(eye, middle) + mm_nt(eye, low)


def attend_back_kernel(h, gain, up, core, get_w, get_m, n, q, k, v, o, lse, dc_ref, do_ref, dqkv, pay):
    d = h.shape[1]
    dc_ref[...] = up.astype(BF)
    do_ref[...] = mm_nt(dc_ref[...], get_m()[...]).astype(BF)
    q, k, v, o = q(), k(), v(), o()
    masks = side_masks()
    sums = exact_rows(lse()[...])
    sub, lane = (lax.broadcasted_iota(jnp.int32, (8, d), i) for i in range(2))
    heads = jnp.where(lane // HDIM == sub, 1.0, 0.0).astype(BF)
    high, low = split_low(o[...].astype(F32) * do_ref[...].astype(F32))
    delta = mm_nt(heads, high) + mm_nt(heads, low)
    step = 64
    for p in range(d // LANES):
        at = slice(p * LANES, (p + 1) * LANES)
        dq = dk = dv = None
        for i, mask in enumerate(masks):
            head = 2 * p + i
            scores = mm_nt(k[:, at] * mask, q[:, at])
            dp = mm_nt(v[:, at] * mask, do_ref[:, at])
            probs, ds = [], []
            for r in range(PATCHES // step):
                rows = slice(r * step, (r + 1) * step)
                part = jnp.exp(scores[rows] - sums[head : head + 1])
                probs.append(part.astype(BF))
                ds.append((part * (dp[rows] - delta[head : head + 1])).astype(BF))
            ds = jnp.concatenate(ds, axis=0)
            part = mm(jnp.concatenate(probs, axis=0), do_ref[:, at] * mask)
            dv = part if dv is None else dv + part
            part = mm(ds, q[:, at] * mask)
            dk = part if dk is None else dk + part
            part = mm_tn(ds, k[:, at] * mask * SCALE)
            dq = part if dq is None else dq + part
        dqkv[:, at] = dq.astype(BF)
        dqkv[:, d + p * LANES : d + (p + 1) * LANES] = dk.astype(BF)
        dqkv[:, 2 * d + p * LANES : 2 * d + (p + 1) * LANES] = dv.astype(BF)
    rows = [
        jnp.sum(dqkv[:, :d].astype(F32), axis=0, keepdims=True),
        jnp.sum(dqkv[:, 2 * d :].astype(F32), axis=0, keepdims=True),
        jnp.sum(dc_ref[...].astype(F32), axis=0, keepdims=True),
    ]
    back, grad_gain, grad_shift = norm_back(h, gain, mm_nt(dqkv[...], get_w()[...]))
    n = n()

    @pl.when(core == 0)
    def queries():
        deal(pay, mm_tn(n[...], dqkv[:, :d]), 0)
        deal(pay, mm_tn(n[...], dqkv[:, 2 * d :]), d)

    @pl.when(core == 1)
    def keys_and_merge():
        deal(pay, mm_tn(n[...], dqkv[:, d : 2 * d]), 0)
        deal(pay, mm_tn(o[...], dc_ref[...]), d)

    return up + back, [grad_gain, grad_shift] + rows


def put_halves(put, first, pay, image):
    put(first, pay.at[1 - image])
    put(first + 1, pay.at[image])


def home_body(blocks, at, get, put, out, full, third, dc, do, dqkv, pay):
    (mine, near, second, n3, routes, router, cot, dec, bias, gains, h_in, mw, m_m, n, q, k, v, o, lse) = range(19)
    decoded, d1, small = out[0], out[1], out[2]
    s, image, core, tasks = at[:4]
    task = tasks[image]
    d = d1.shape[1]
    full[pl.ds(pl.multiple_of(core * HALF, 16), HALF), :] = get(mine)[...]
    full[pl.ds(pl.multiple_of((1 - core) * HALF, 16), HALF), :] = get(near)[...]
    stream = get(second)[...].astype(F32)
    third[...] = (stream + full[:, :d].astype(F32)).astype(BF)
    half = third[pl.ds(pl.multiple_of(core * HALF, 16), HALF), :]
    cot, dec, n3 = get(cot), get(dec), get(n3)
    decoded[...] = mm(half, dec[...]) + get(bias)[pl.ds(task, 1), :]
    put(0)
    hdec = cot.shape[1] // 2
    table = mm_tn(third[...], cot[:, pl.ds(pl.multiple_of(core * hdec, LANES), hdec)])
    deal(pay, jnp.where(task == 0, table, 0.0), 2 * d)
    deal(pay, jnp.where(task == 1, table, 0.0), 2 * d + hdec)

    lane = lane_ids()
    member = jnp.zeros((PATCHES, LANES), F32)
    named = get(routes)
    for i in range(TOP):
        member = member + jnp.where(lane == named[:, i : i + 1], 1.0, 0.0)
    table = get(router)
    logits = jnp.where(member > 0.0, mm(n3[...], table[...]), -1e30)
    e = jnp.where(member > 0.0, jnp.exp(logits - jnp.max(logits, axis=1, keepdims=True)), 0.0)
    gates = e / jnp.sum(e, axis=1, keepdims=True)
    dots = full[:, 2 * d :].astype(F32)
    dots = dots + pltpu.roll(dots, LANES - EXPERTS, 1)
    dz = gates * (dots - jnp.sum(gates * dots, axis=1, keepdims=True))
    high = dz.astype(BF).astype(F32)
    low = dz - high
    moved = lambda x: jnp.where(task == 0, x, pltpu.roll(x, EXPERTS, 1)).astype(BF)
    grad_router = mm_tn(n3[...], moved(high)) + mm_tn(n3[...], moved(low))
    dn = full[:, d : 2 * d].astype(F32) + mm_nt(high.astype(BF), table[...]) + mm_nt(low.astype(BF), table[...])
    gains = get(gains)
    back, gain1, shift1 = norm_back(stream, gains[1:2], dn)
    up = (mm_nt(cot[...], dec[...]).astype(BF).astype(F32) + back).astype(BF).astype(F32)
    later = lambda i: lambda: get(i)
    result, sums = attend_back_kernel(
        get(h_in)[...].astype(F32), gains[0:1], up, core, later(mw), later(m_m), later(n), later(q), later(k), later(v),
        later(o), later(lse), dc, do, dqkv, pay,
    )
    put_halves(put, 3, pay, image)
    d1[...] = result.astype(BF)
    put(1)
    gain0, shift0, b0, b1, b2 = sums
    small[...] = grad_router + columns_of(
        [gain0, gain1, shift0, shift1, b0, b1, b2], [16, 17, 18, 19, 20, 21, 22]
    )
    owners = jnp.sum(cot[...].astype(F32), axis=0, keepdims=True)
    count = cot.shape[1]
    column = columns_of([owners], [24])
    column = jnp.where(task == 0, column, pltpu.roll(column, 1, 1))
    r, some = d // blocks // 2, count // blocks // 2
    for b in range(2 * blocks):
        small[b * r : b * r + some, :] += column[b * some : (b + 1) * some]
    put(2)


def home(section, tasks, mine, near, second, n3, routes, router, cot, dec, bias, gains, first, mw, m_m, saved, blocks):
    d = second.shape[1]
    width = cot.shape[1]
    inputs = [
        mine, near, second, n3, (routes, rows_of(PATCHES), (PATCHES, TOP)), (router, of_task, (d, LANES)),
        (cot, rows_of(PATCHES), (PATCHES, width)),
        (dec, lambda s, image, core, tasks: (slice(None), pl.ds(pl.multiple_of(tasks[image] * width, LANES), width)),
         (d, width)),
        bias, gains, first, mw, m_m, *saved,
    ]
    shape = light_shape(d, blocks, 2 * d + width)
    half = (shape[1:], BF, None)
    outs = [((HALF, width), F32), ((PATCHES, d), BF), ((d, LANES), F32), half, half]
    scratch = [
        VMEM((PATCHES, 2 * d + LANES), BF), VMEM((PATCHES, d), BF), VMEM((PATCHES, d), BF), VMEM((PATCHES, d), BF),
        VMEM((PATCHES, 3 * d), BF), VMEM(shape, BF),
    ]
    return call(functools.partial(home_body, blocks), section, tasks, inputs, outs, scratch, flops=2e10)


def dense_back_body(blocks, at, get, put, out, du_all, pay):
    d1, sr, slope, sx, a0, gains, small_in, n1, act = range(9)
    da, small = out[0], out[1]
    image, core = at[1], at[2]
    d1, sr, slope, sx = get(d1), get(sr), get(slope), get(sx)
    d, ff = sx.shape
    step = 512
    dn = None
    for f in range(ff // step):
        cols = slice(f * step, (f + 1) * step)
        du = (slope[:, cols].astype(F32) * mm_nt(d1[...], sr[cols, :])).astype(BF)
        du_all[:, cols] = du
        part = mm_nt(du, sx[:, cols])
        dn = part if dn is None else dn + part
    up = d1[...].astype(F32)
    back, gain1, shift1 = norm_back(get(a0)[...], get(gains)[1:2], dn)
    da[...] = up + back
    put(0)
    lifts = jnp.sum(du_all[...].astype(F32), axis=0, keepdims=True)
    b3 = jnp.sum(up, axis=0, keepdims=True)
    small[...] = (
        get(small_in)[...] + spread_blocks(lifts, 40, 2 * blocks) + columns_of([gain1, shift1, b3], [33, 35, 39])
    )
    put(1)
    n1, act = get(n1), get(act)

    @pl.when(core == 0)
    def expand():
        for f in range(ff // step):
            deal(pay, mm_tn(n1[...], du_all[:, f * step : (f + 1) * step]), f * step)

    @pl.when(core == 1)
    def reduce():
        deal_long(pay, mm_tn(act[...], d1[...]))

    put_halves(put, 2, pay, image)


def dense_back(section, tasks, inputs, blocks):
    d, ff = inputs[3].shape
    shape = light_shape(d, blocks, ff)
    half = (shape[1:], BF, None)
    outs = [((PATCHES, d), F32), ((d, LANES), F32), half, half]
    return call(
        functools.partial(dense_back_body, blocks), section, tasks, inputs, outs,
        [VMEM((PATCHES, ff), BF), VMEM(shape, BF)], flops=8e9,
    )


def stem_back_body(at, get, put, out, full, dc, do, dqkv, pay):
    da, tok, gains, sw, sm, small_in, n, q, k, v, o, lse = range(12)
    image, core = at[1], at[2]
    up = get(da)[...]
    d = up.shape[1]
    later = lambda i: lambda: get(i)
    result, sums = attend_back_kernel(
        get(tok)[...].astype(F32), get(gains)[0:1], up, core, later(sw), later(sm), later(n), later(q), later(k), later(v),
        later(o), later(lse), dc, do, dqkv, pay,
    )
    gain0, shift0, b0, b1, b2 = sums
    small = get(small_in)[...] + columns_of([gain0, shift0, b0, b1, b2], [32, 34, 36, 37, 38])
    deal(pay, jnp.where(core == 0, small, 0.0), 2 * d)
    put_halves(put, 1, pay, image)
    full[...] = result
    put(0, full.at[pl.ds(pl.multiple_of(core * HALF, 8), HALF), :])


def stem_back(section, tasks, da, tokens, gains, sw, sm, small_in, saved, blocks):
    d = da.shape[1]
    inputs = [da, (tokens, rows_of(PATCHES), (PATCHES, d)), gains, sw, sm, small_in, *saved]
    shape = light_shape(d, blocks, 2 * d + LANES)
    half = (shape[1:], BF, None)
    outs = [((HALF, d), F32, None), half, half]
    scratch = [
        VMEM((PATCHES, d), F32), VMEM((PATCHES, d), BF), VMEM((PATCHES, d), BF), VMEM((PATCHES, 3 * d), BF),
        VMEM(shape, BF),
    ]
    return call(stem_back_body, section, tasks, inputs, outs, scratch, flops=1.5e10)


def one_hot(rows, columns, hits):
    sub, lane = (lax.broadcasted_iota(jnp.int32, (rows, columns), i) for i in range(2))
    total = jnp.zeros((rows, columns), F32)
    for i, j in hits:
        total = total + jnp.where((sub == i) & (lane == j), 1.0, 0.0)
    return total.astype(BF)


def heavy_out_body(at, get, put, out, gathered):
    grad_in, grad_out, lift, drop = out
    s = at[0]
    r, ff = grad_in.shape[0], grad_in.shape[2]
    d = grad_out.shape[2]
    for mask in range(4):
        for j in range(2):
            gathered[pl.ds(2 * jnp.bitwise_xor(s, mask) + j, 1)] = get(4 * j + mask)[...][None]
    small = []
    for e in range(EXPERTS):
        value = gathered[e].astype(F32)
        grad_in[:, e, :] = value[:r, :ff]
        small.append(value[:r, ff:])
        for k in range(4):
            grad_out[e, k * r : (k + 1) * r, :] = value[r:, k * d : (k + 1) * d]
    put(0)
    put(1)
    row = mm_nt(one_hot(8, LANES, [(k, k) for k in range(5)]), jnp.concatenate(small, axis=0).astype(BF))
    sub, lane = (lax.broadcasted_iota(jnp.int32, (EXPERTS, EXPERTS * r), i) for i in range(2))
    own = jnp.where(lane // r == sub, 1.0, 0.0)
    spread = lambda k, wide: jnp.where(
        lax.broadcasted_iota(jnp.int32, (EXPERTS * r, wide), 1)
        == k * r + lax.broadcasted_iota(jnp.int32, (EXPERTS * r, wide), 0) % r,
        1.0, 0.0,
    ).astype(BF)
    parts = [mm((own * row[k : k + 1]).astype(BF), spread(k, 4 * r)) for k in range(4)]
    lift[...] = parts[0] + parts[1] + parts[2] + parts[3]
    drop[...] = mm((own * row[4:5]).astype(BF), spread(0, r))
    put(2)
    put(3)


def heavy_out(section, tasks, pieces, d):
    r2, wide = pieces[0].shape
    r, ff = r2 // 2, wide - LANES
    outs = [
        ((r, EXPERTS, ff), F32), ((EXPERTS, 4 * r, d), F32), ((EXPERTS, 4 * r), F32), ((EXPERTS, r), F32)
    ]
    return call(heavy_out_body, section, tasks, pieces, outs, [VMEM((EXPERTS, r2, wide), BF)])


def light_out_body(d, dec, at, get, put, out, both):
    (mix_heads, mix_merge, dec_out, expand, reduce, stem_heads, stem_merge, router, lift, bias) = out[:10]
    rows = out[10:]
    core = at[2]
    both[pl.ds(core, 1)] = get(0)[...][None]
    both[pl.ds(1 - core, 1)] = get(1)[...][None]
    r = expand.shape[0]
    m, ff, hdec = 2 * d + dec, expand.shape[1], dec // 2
    a, b = both[0].astype(F32), both[1].astype(F32)
    tiny = a[:, m + ff + 2 * d :]
    order = (32, 33, 34, 35, 36, 37, 38, 39, 16, 17, 18, 19, 20, 21, 22, 24, 25, 40, 41, 42, 43)
    turned = mm_nt(one_hot(24, LANES, list(enumerate(order))), tiny.astype(BF))
    some = bias.shape[1]
    for c in range(2):

        @pl.when(core == c)
        def write():
            x, y = a[c * r : (c + 1) * r], b[c * r : (c + 1) * r]
            for heads, merge, base in ((mix_heads, mix_merge, 0), (stem_heads, stem_merge, m + ff)):
                heads[:, :d] = x[:, base : base + d]
                heads[:, d : 2 * d] = y[:, base : base + d]
                heads[:, 2 * d :] = x[:, base + d : base + 2 * d]
                merge[...] = y[:, base + d : base + 2 * d]
            for t in range(2):
                dec_out[:, t, :hdec] = x[:, 2 * d + t * hdec : 2 * d + (t + 1) * hdec]
                dec_out[:, t, hdec:] = y[:, 2 * d + t * hdec : 2 * d + (t + 1) * hdec]
                router[:, t, :] = tiny[c * r : (c + 1) * r, t * EXPERTS : (t + 1) * EXPERTS]
            expand[...] = x[:, m : m + ff]
            for k in range(2):
                at_lane = m + (2 * c + k) * d
                reduce[k * 2 * r : (k + 1) * 2 * r, :] = b[:, at_lane : at_lane + d]
            first = 0
            for part in rows:
                part[...] = turned[first : first + part.shape[0], c * r : (c + 1) * r]
                first += part.shape[0]
            bias[...] = turned[first : first + 2, c * some : (c + 1) * some]
            lift[...] = turned[first + 2 + 2 * c : first + 4 + 2 * c]

    for i in range(len(out)):
        put(i)


def light_out(section, tasks, mine, near, d, dec, ff, some):
    r2 = mine.shape[0]
    r = r2 // 2
    shapes = [
        (r, 3 * d), (r, d), (r, 2, dec), (r, ff), (4 * r, d), (r, 3 * d), (r, d), (r, 2, EXPERTS), (2, r2), (2, some),
        (2, r), (2, r), (4, r), (2, r), (2, r), (3, r),
    ]
    return call(
        functools.partial(light_out_body, d, dec), section, tasks, [mine, near], [(x, F32) for x in shapes],
        [VMEM((2,) + mine.shape, BF)],
    )


def after(x, *others):
    return lax.optimization_barrier((x, *others))[0]


def swap(x, axis, mask):
    size = lax.axis_size(axis)
    return lax.ppermute(x, axis, [(i, i ^ mask) for i in range(size)])


def add_low(*terms):
    return sum(t.astype(F32) for t in terms).astype(BF)


def take(x, i):
    return lax.dynamic_index_in_dim(x, i, 0, keepdims=False)


def halve(terms, axis, mask, bit, also_sent=False):
    send = add_low(*[take(t, 1 - bit) for t in terms])
    got = swap(send, axis, mask)
    keep = add_low(*[take(t, bit) for t in terms])
    return [keep, got, send] if also_sent else [keep, got]


def line_reduce(x):
    ndp = lax.axis_size("dp")
    groups = [list(range(p, ndp, 2)) for p in range(2)]
    return lax.psum_scatter(x, "dp", scatter_dimension=0, axis_index_groups=groups, tiled=True)


def body(
    tokens, routes, task_ids, cotangent, stem_gains, stem_shifts, stem_heads, stem_merge,
    stem_biases, stem_expand, stem_lift, stem_reduce, mix_gains, mix_shifts, mix_heads,
    mix_merge, mix_biases, router, expert_in, expert_lift, expert_out, expert_drop, decoder,
    decoder_bias,
):
    s = lax.axis_index("section")
    image = s // 2
    side = lax.axis_index("dp") % 2
    section = jnp.stack([s, side])
    ndp, ns = lax.axis_size("dp"), lax.axis_size("section")
    d, ff, dec = tokens.shape[1], stem_expand.shape[1], cotangent.shape[1]
    r, q = d // ndp, d // ndp // ns

    weights = [
        stem_heads, stem_gains, stem_shifts, stem_biases, stem_merge, stem_expand, stem_lift, stem_reduce, mix_heads,
        mix_gains, mix_shifts, mix_biases, mix_merge,
    ]
    (n0, q0, k0, v0, o0, l0, a0, n1, act, slope, first, n2, q2, k2, v2, o2, l2, second, n3, n3_cut) = forward(
        section, task_ids, tokens, weights
    )
    far = swap(n3_cut, "section", 2)

    routes_t = routes.reshape(-1, PATCHES, TOP).transpose(0, 2, 1)
    router_t = router.transpose(1, 2, 0)
    router_wide = jnp.pad(router.transpose(1, 0, 2), ((0, 0), (0, 0), (0, LANES - EXPERTS)))
    dec_flat = decoder.reshape(d, -1)
    common = (routes_t, router_t, cotangent, dec_flat, (expert_in, expert_lift, expert_out, expert_drop))
    own_send, own_keep, *own = experts(True, section, task_ids, [n3], *common)
    far = after(far, own_keep)
    near = swap(far, "section", 1)
    own_got = swap(own_send, "section", 1)
    far_send, far_keep, *away = experts(False, section, task_ids, [far, near], *common)
    far_got = swap(far_send, "section", 1)
    crossed = swap(add_low(far_keep, far_got), "section", 2)
    (later,) = weight_grads(1, section, task_ids, own, away, ndp)
    away[0] = after(away[0], later)
    sooner_send, sooner_keep = weight_grads(0, section, task_ids, own, away, ndp)
    sooner_got = swap(sooner_send, "dp", 1)
    later = line_reduce(later.reshape(-1, ff + LANES))
    crossed = after(crossed, sooner_keep)
    mine = add_low(own_keep, own_got, crossed)
    near = swap(mine, "section", 1)

    decoded, d1, small, mix_send, mix_keep = home(
        section, task_ids, mine, near, second, n3, routes, router_wide, cotangent, dec_flat, decoder_bias,
        mix_gains, first, mix_heads, mix_merge, (n2, q2, k2, v2, o2, l2), ndp,
    )
    mix_got = swap(mix_send, "section", 2)
    da, small, dense_send, dense_keep = dense_back(
        section, task_ids, [d1, stem_reduce, slope, stem_expand, a0, stem_gains, small, n1, act], ndp
    )
    dense_got = swap(dense_send, "section", 2)
    mix = halve([mix_keep, after(mix_got, da)], "dp", 1, side, True)
    sooner = add_low(sooner_keep, after(sooner_got, da)).reshape(-1, ff + LANES)
    da = after(da, mix[2], sooner)
    sooner = line_reduce(sooner)
    d0, stem_send, stem_keep = stem_back(
        section, task_ids, da, tokens, stem_gains, stem_heads, stem_merge, small, (n0, q0, k0, v0, o0, l0), ndp
    )
    stem_got = swap(stem_send, "section", 2)

    join = lambda xs, ys: [jnp.concatenate([x, y], axis=-1) for x, y in zip(xs, ys)]
    dense = halve([dense_keep, after(dense_got, d0)], "dp", 1, side)
    stem = halve([stem_keep, stem_got], "dp", 1, side)
    wide = join(mix[:2], dense)
    index = lax.axis_index("dp")
    mask = ndp // 2
    while mask > 1:
        bit = (index // mask) % 2
        cut = lambda xs: [x.reshape((2, x.shape[0] // 2) + x.shape[1:]) for x in xs]
        if mask == ndp // 2:
            wide, stem = halve(cut(wide), "dp", mask, bit), halve(cut(stem), "dp", mask, bit)
            light = join(wide, stem)
        else:
            light = halve(cut(light), "dp", mask, bit)
        mask //= 2
    light = add_low(*light)[0]
    light_near = swap(light, "section", 1)

    def pieces(x):
        return [take(x, s)] + [swap(take(x, s ^ mask), "section", mask) for mask in (1, 2, 3)]

    later = halve([later.reshape(2, ns, 2 * q, -1)], "dp", 1, side)
    later = pieces(add_low(*later))
    sooner = pieces(sooner.reshape(ns, 2 * q, -1))
    grad_in, grad_out, g_elift, g_edrop = heavy_out(section, task_ids, sooner + later, d)
    (
        g_mix_heads, g_mix_merge, g_dec, g_expand, g_reduce, g_stem_heads, g_stem_merge, g_router, g_lift, g_bias,
        g_stem_gains, g_stem_shifts, g_stem_biases, g_mix_gains, g_mix_shifts, g_mix_biases,
    ) = light_out(section, task_ids, light, light_near, d, dec, ff, dec // ndp // ns)
    return (
        decoded, d0, g_stem_gains, g_stem_shifts, g_stem_heads, g_stem_merge, g_stem_biases, g_expand,
        g_lift.reshape(-1), g_reduce, g_mix_gains, g_mix_shifts, g_mix_heads, g_mix_merge, g_mix_biases, g_router,
        grad_in.transpose(1, 0, 2), g_elift, grad_out, g_edrop, g_dec, g_bias,
    )


def solution(mesh):
    both = ("dp", "section")
    placed = (P("dp", None), P("dp", None), P("dp"), P("dp", None)) + (P(),) * 20
    rows, columns = P(both, None), P(None, both)
    return jax.shard_map(
        body,
        mesh=mesh,
        in_specs=placed,
        out_specs=(
            rows, rows, columns, columns, rows, rows, columns, rows, P(both), rows, columns,
            columns, rows, rows, columns, P(both, None, None), P(None, both, None), columns,
            P(None, both, None), columns, P(both, None, None), columns,
        ),
        check_vma=False,
    )
```

```python
import functools
import math

import jax
import jax.numpy as jnp
from jax import lax
from jax.experimental import pallas as pl
from jax.experimental.pallas import tpu as pltpu
from jax.sharding import PartitionSpec as P

HEADS = 6
HDIM = 64
EXPERTS = 8
TOP = 4
PATCHES = 576
HALF = PATCHES // 2
CAP = 288
LANES = 128
EPSILON = 1e-06
SCALE = 1.0 / math.sqrt(HDIM)
BF = jnp.bfloat16
F32 = jnp.float32
VMEM = pltpu.VMEM
MIB = 1 << 20


def mm(a, b):
    return jnp.dot(a, b, preferred_element_type=F32)


def mm_tn(a, b):
    return lax.dot_general(a, b, (((0,), (0,)), ((), ())), preferred_element_type=F32)


def mm_nt(a, b):
    return lax.dot_general(a, b, (((1,), (1,)), ((), ())), preferred_element_type=F32)


def split_low(v):
    high = v.astype(BF)
    return high, (v - high.astype(F32)).astype(BF)


def norm_parts(v):
    centred = v - jnp.mean(v, axis=-1, keepdims=True)
    inverse = lax.rsqrt(jnp.mean(centred * centred, axis=-1, keepdims=True) + EPSILON)
    return centred * inverse, inverse


def norm_back(v, gain, up):
    unit, inverse = norm_parts(v)
    scaled = up * gain
    back = inverse * (
        scaled
        - jnp.mean(scaled, axis=-1, keepdims=True)
        - unit * jnp.mean(scaled * unit, axis=-1, keepdims=True)
    )
    return back, jnp.sum(up * unit, axis=0, keepdims=True), jnp.sum(up, axis=0, keepdims=True)


def gelu_both(u):
    t = pl.reciprocal(1.0 + (0.3275911 / math.sqrt(2.0)) * jnp.abs(u), approx=True)
    bell = jnp.exp2((-0.5 / math.log(2.0)) * u * u)
    poly = 0.5 * 1.421413741 + t * (0.5 * -1.453152027 + t * (0.5 * 1.061405429))
    tail = bell * (t * (0.5 * 0.254829592 + t * (0.5 * -0.284496736 + t * poly)))
    cdf = jnp.where(u >= 0.0, 1.0 - tail, tail)
    return u * cdf, cdf + u * bell * (1.0 / math.sqrt(2.0 * math.pi))


def side_masks():
    lane = lax.broadcasted_iota(jnp.int32, (1, LANES), 1)
    left = (lane < HDIM).astype(F32)
    return left.astype(BF), (1.0 - left).astype(BF)


def lane_ids(rows=1):
    return lax.broadcasted_iota(jnp.int32, (rows, LANES), 1)


def near_first(blocks):
    return [1 << i for i in range(blocks.bit_length() - 1)]


def spot_of(block, masks):
    spot = 0
    for mask in masks:
        spot = 2 * spot + (block // mask) % 2
    return spot


def deal(pay, value, at):
    r, w = pay.shape[2], value.shape[1]
    for b in range(pay.shape[1]):
        spot = spot_of(b, near_first(pay.shape[1]))
        for y in range(2):
            piece = value[(2 * b + y) * r : (2 * b + y + 1) * r]
            pay[y, spot, :, at : at + w] = piece.astype(BF)


def deal_long(pay, value):
    r, w = pay.shape[2], value.shape[1]
    for b in range(pay.shape[1]):
        spot = spot_of(b, near_first(pay.shape[1]))
        for y in range(2):
            for k in range(4):
                piece = value[(8 * b + 4 * y + k) * r : (8 * b + 4 * y + k + 1) * r]
                pay[y, spot, :, k * w : (k + 1) * w] = piece.astype(BF)


def light_shape(d, blocks, width):
    return (2, blocks, d // blocks // 2, width)


def one_hot(rows, columns, hits):
    sub, lane = (lax.broadcasted_iota(jnp.int32, (rows, columns), i) for i in range(2))
    total = jnp.zeros((rows, columns), F32)
    for i, j in hits:
        total = total + jnp.where((sub == i) & (lane == j), 1.0, 0.0)
    return total.astype(BF)


def columns_of(rows, lanes):
    count = -(-len(lanes) // 8) * 8
    n = rows[0].shape[1]
    spare = [jnp.zeros((count - len(lanes), n), F32)] if count > len(lanes) else []
    stacked = jnp.concatenate(rows + spare, axis=0)
    place = lax.broadcasted_iota(jnp.int32, (count, LANES), 0)
    lane = lane_ids(count)
    spread = jnp.zeros((count, LANES), F32)
    for i, at in enumerate(lanes):
        spread = spread + jnp.where((place == i) & (lane == at), 1.0, 0.0)
    return mm_tn(stacked.astype(BF), spread.astype(BF))


def spread_blocks(row, first_lane, blocks):
    n = row.shape[1]
    r = n // 4 // blocks
    place = lax.broadcasted_iota(jnp.int32, (8, LANES), 0)
    stacked = jnp.concatenate([row, jnp.zeros((7, n), F32)], axis=0)
    column = mm_tn(stacked.astype(BF), jnp.where(place == 0, 1.0, 0.0).astype(BF))
    lane = lane_ids()
    parts = []
    for b in range(blocks):
        part = None
        for s in range(4):
            at = (4 * b + s) * r
            piece = jnp.where(lane == first_lane + s, column[at : at + r], 0.0)
            part = piece if part is None else part + piece
        parts.append(part)
    return jnp.concatenate(parts, axis=0)


class Near:
    def __init__(self, array):
        self.array = array


class Fetched:
    def __init__(self, moves):
        self.moves = moves
        for move in moves:
            move.start()

    def wait(self):
        for move in self.moves:
            move.wait()
        self.moves = []


def run_kernel(body, n_in, n_out, picks, near_out, *refs):
    section, tasks = refs[:2]
    inputs, outputs = refs[2 : 2 + n_in], refs[2 + n_in : 2 + n_in + n_out]
    rest = refs[2 + n_in + n_out :]
    kept_in, kept_out = rest[:n_in], rest[n_in : n_in + n_out]
    in_sems, out_sems = rest[n_in + n_out : n_in + n_out + 2]
    kept_out = [outputs[i] if i in near_out else kept_out[i] for i in range(n_out)]
    at = (section[0], section[0] // 2, section[0] % 2, tasks, section[1])
    fetched, moving = [], []
    for i in range(n_in):
        if picks[i] == "near":
            fetched.append(None)
            continue
        source = inputs[i] if picks[i] is None else inputs[i].at[picks[i](*at[:4])]
        fetched.append(Fetched([pltpu.make_async_copy(source, kept_in[i], in_sems.at[i])]))

    def get(i):
        if fetched[i] is None:
            return inputs[i]
        fetched[i].wait()
        return kept_in[i]

    def put(i, source=None, part=None):
        if i in near_out:
            return
        source = kept_out[i] if source is None else source
        target = outputs[i] if part is None else outputs[i].at[part]
        move = pltpu.make_async_copy(source, target, out_sems.at[i if part is None else i + part * n_out])
        move.start()
        moving.append(move)

    body(at, get, put, kept_out, *rest[n_in + n_out + 2 :])
    for i in range(n_in):
        get(i)
    for move in moving:
        move.wait()


def call(body, section, tasks, inputs, outs, scratch=(), us=3.0, limit=56):
    arrays, picks, kept = [], [], []
    for x in inputs:
        if isinstance(x, Near):
            arrays.append(x.array)
            picks.append("near")
            kept.append(VMEM((8, LANES), F32))
            continue
        array, pick, shape = x if isinstance(x, tuple) else (x, None, x.shape)
        arrays.append(array)
        picks.append(pick)
        kept.append(VMEM(shape, array.dtype))
    kept_out = [VMEM(o[0], o[1]) if len(o) == 2 else VMEM((8, LANES), F32) for o in outs]
    near_out = [i for i, o in enumerate(outs) if len(o) == 3 and o[2] == "near"]
    anywhere, scalar = pl.BlockSpec(memory_space=pl.ANY), pl.BlockSpec(memory_space=pltpu.SMEM)
    here = pl.BlockSpec(memory_space=pltpu.VMEM)
    return pl.pallas_call(
        functools.partial(run_kernel, body, len(arrays), len(outs), picks, near_out),
        out_shape=[jax.ShapeDtypeStruct(o[0], o[1]) for o in outs],
        in_specs=[scalar, scalar] + [here if p == "near" else anywhere for p in picks],
        out_specs=[here if i in near_out else anywhere for i in range(len(outs))],
        scratch_shapes=[
            *kept, *kept_out, pltpu.SemaphoreType.DMA((len(arrays),)), pltpu.SemaphoreType.DMA((2 * len(outs),)), *scratch
        ],
        compiler_params=pltpu.CompilerParams(vmem_limit_bytes=limit * MIB),
        cost_estimate=pl.CostEstimate(flops=int(us * 1.1e9), bytes_accessed=1, transcendentals=0),
    )(section, tasks, *arrays)


def rows_of(count):
    return lambda s, image, core, tasks: pl.ds(pl.multiple_of(image * count, count), count)


def of_task(s, image, core, tasks):
    return tasks[image]


def attend_kernel(h, gain, shift, get_w, c, get_m, n_ref, q_ref, k_ref, v_ref, o_ref, lse_ref, done):
    d = h.shape[1]
    unit, unused = norm_parts(h)
    n_ref[...] = (unit * gain + shift).astype(BF)
    done(0)
    n, w = n_ref[...], get_w()
    q_ref[...] = ((mm(n, w[:, :d]) + c[0:1]) * SCALE).astype(BF)
    done(1)
    k_ref[...] = mm(n, w[:, d : 2 * d]).astype(BF)
    done(2)
    v_ref[...] = (mm(n, w[:, 2 * d :]) + c[1:2]).astype(BF)
    done(3)
    masks = side_masks()
    lane = lane_ids()
    sums = jnp.zeros((PATCHES, LANES), F32)
    step = 32
    for p in range(d // LANES):
        at = slice(p * LANES, (p + 1) * LANES)
        total = None
        for i, mask in enumerate(masks):
            scores = mm_nt(q_ref[:, at] * mask, k_ref[:, at])
            e, norm, top = [], [], []
            for r in range(PATCHES // step):
                part = scores[r * step : (r + 1) * step]
                most = jnp.max(part, axis=-1, keepdims=True)
                part = jnp.exp(part - most)
                e.append(part.astype(BF))
                norm.append(jnp.sum(part, axis=-1, keepdims=True))
                top.append(most)
            norm = jnp.concatenate(norm, axis=0)
            part = mm(jnp.concatenate(e, axis=0), v_ref[:, at] * mask) * (1.0 / norm)
            total = part if total is None else total + part
            sums = jnp.where(lane == 2 * p + i, jnp.concatenate(top, axis=0) + jnp.log(norm), sums)
        o_ref[:, at] = total.astype(BF)
    lse_ref[...] = sums
    done(4)
    done(5)
    return h + (mm(o_ref[...], get_m()[...]) + c[2:3])


def forward_body(at, get, put, out, *scratch):
    tok, sw, sg, ss, sb, sm, sx, sl, sr, mw, mg, ms, mb, m_m = range(14)
    (n0, q0, k0, v0, o0, l0, a0, n1, act, slope, first, n2, q2, k2, v2, o2, l2, second, n3, n3_cut) = out
    h = get(tok)[...].astype(F32)
    sg, ss, sb = get(sg), get(ss), get(sb)
    a = attend_kernel(
        h, sg[0:1], ss[0:1], lambda: get(sw), sb, lambda: get(sm), n0, q0, k0, v0, o0, l0, put
    )
    a0[...] = a
    put(6)
    unit, unused = norm_parts(a0[...])
    n1[...] = (unit * sg[1:2] + ss[1:2]).astype(BF)
    put(7)
    step = 512
    wx, lift = get(sx), get(sl)
    for f in range(wx.shape[1] // step):
        cols = slice(f * step, (f + 1) * step)
        active, bend = gelu_both(mm(n1[...], wx[:, cols]) + lift[cols][None, :])
        act[:, cols] = active.astype(BF)
        slope[:, cols] = bend.astype(BF)
    put(8)
    put(9)
    first[...] = (a0[...] + (mm(act[...], get(sr)[...]) + sb[3:4])).astype(BF)
    put(10)
    mg, ms, mb = get(mg), get(ms), get(mb)
    second[...] = attend_kernel(
        first[...].astype(F32), mg[0:1], ms[0:1], lambda: get(mw), mb, lambda: get(m_m), n2, q2, k2, v2,
        o2, l2, lambda i: put(11 + i),
    ).astype(BF)
    put(17)
    unit, unused = norm_parts(second[...].astype(F32))
    n3[...] = (unit * mg[1:2] + ms[1:2]).astype(BF)
    put(18)
    n3_cut[...] = n3[pl.ds(pl.multiple_of(at[2] * HALF, 16), HALF), :]


def forward(section, tasks, tokens, weights):
    d = tokens.shape[1]
    ff = weights[5].shape[1]
    wide = ((PATCHES, d), BF)
    sums = ((PATCHES, LANES), F32)
    outs = [wide] * 5 + [sums, ((PATCHES, d), F32), wide, ((PATCHES, ff), BF), ((PATCHES, ff), BF)]
    outs += [wide] * 6 + [sums, wide, wide, ((HALF, d), BF, "near")]
    inputs = [(tokens, rows_of(PATCHES), (PATCHES, d)), *weights]
    return call(forward_body, section, tasks, inputs, outs, us=20.0)


def pick_routes(ref, image):
    every = ref[...]
    chosen = every[:, :PATCHES]
    for i in range(1, every.shape[1] // PATCHES):
        chosen = jnp.where(image == i, every[:, i * PATCHES : (i + 1) * PATCHES], chosen)
    return chosen


def experts_body(own, at, get, put, out, gates, place, d3, n_all):
    n, routes, router, cot, dec, w_in0, w_in1, lift, w_out0, w_out1, drop = range(11)
    core = at[2]
    if own:
        full, xs, dys, acts, dus = out
        first = 1
    else:
        send, keep, xs, dys, acts, dus, full = out
        first = 2
    if own:
        n_ref = get(n)
    else:
        n_all[pl.ds(pl.multiple_of(core * HALF, 16), HALF), :] = get(n)[...]
        n_all[pl.ds(pl.multiple_of((1 - core) * HALF, 16), HALF), :] = get(11)[...]
        n_ref = n_all
    ids = lax.broadcasted_iota(jnp.int32, (EXPERTS, PATCHES), 0)
    member = jnp.zeros((EXPERTS, PATCHES), F32)
    named = pick_routes(get(routes), at[1] if own else 1 - at[1])
    for k in range(TOP):
        member = member + jnp.where(ids == named[k : k + 1, :], 1.0, 0.0)
    logits = jnp.where(member > 0.0, mm_nt(get(router)[...], n_ref[...]), -1e30)
    e = jnp.where(member > 0.0, jnp.exp(logits - jnp.max(logits, axis=0, keepdims=True)), 0.0)
    gates[...] = e / jnp.sum(e, axis=0, keepdims=True)
    before = lax.broadcasted_iota(jnp.int32, (PATCHES, PATCHES), 0)
    after_ = lax.broadcasted_iota(jnp.int32, (PATCHES, PATCHES), 1)
    upper = jnp.where(before <= after_, 1.0, 0.0).astype(BF)
    place[...] = jnp.where(member > 0.0, mm(member.astype(BF), upper) - 1.0, -1.0)
    d3[...] = mm_nt(get(cot)[...], get(dec)[...]).astype(BF)
    total = None
    lifts, drops = get(lift), get(drop)
    for j in range(2):
        e = 2 * at[0] + j
        spot = place[pl.ds(e, 1), :].astype(jnp.int32)
        hit = lax.broadcasted_iota(jnp.int32, (CAP, PATCHES), 0) == spot
        pick = jnp.where(hit, 1.0, 0.0)
        weight = jnp.sum(pick * gates[pl.ds(e, 1), :], axis=1, keepdims=True)
        pick = pick.astype(BF)
        x = mm(pick, n_ref[...]).astype(BF)
        up = mm(pick, d3[...])
        dy = (weight * up).astype(BF)
        xs[j] = x
        dys[j] = dy
        w_in, w_out = get((w_in0, w_in1)[j]), get((w_out0, w_out1)[j])
        ff = w_in.shape[1]
        step = 512
        y = drops[pl.ds(e, 1), :]
        dx = None
        for f in range(ff // step):
            cols = slice(f * step, (f + 1) * step)
            active, bend = gelu_both(mm(x, w_in[:, cols]) + lifts[pl.ds(e, 1), cols])
            active = active.astype(BF)
            du = (bend * mm_nt(dy, w_out[cols, :])).astype(BF)
            y = y + mm(active, w_out[cols, :])
            part = mm_nt(du, w_in[:, cols])
            dx = part if dx is None else dx + part
            acts[j, :, cols] = active
            dus[j, :, cols] = du
        for i, kept in enumerate((xs, dys, acts, dus)):
            put(first + i, kept.at[j], j)
        dots = jnp.sum(y * up, axis=1, keepdims=True)
        high = dots.astype(BF).astype(F32)
        lane = lane_ids()
        marks = jnp.where(lane == e, high, jnp.where(lane == e + EXPERTS, dots - high, 0.0))
        rhs = jnp.concatenate([(weight * y).astype(BF), dx.astype(BF), marks.astype(BF)], axis=1)
        home = mm_tn(pick, rhs)
        total = home if total is None else total + home
    full[...] = total.astype(BF)
    if not own:
        send[...] = full[pl.ds(pl.multiple_of((1 - core) * HALF, 16), HALF), :]
        keep[...] = full[pl.ds(pl.multiple_of(core * HALF, 16), HALF), :]


def experts(own, section, tasks, n, routes_t, router_t, cot, dec, weights):
    expert_in, expert_lift, expert_out, expert_drop = weights
    d, ff = expert_in.shape[1:]
    width = 2 * d + LANES
    look = (lambda image: image) if own else (lambda image: 1 - image)
    which = lambda j: lambda s, image, core, tasks: 2 * s + j
    inputs = [
        n[0],
        routes_t,
        (router_t, lambda s, image, core, tasks: tasks[look(image)], (EXPERTS, d)),
        (cot, lambda s, image, core, tasks: pl.ds(pl.multiple_of(look(image) * PATCHES, PATCHES), PATCHES),
         (PATCHES, cot.shape[1])),
        (dec, lambda s, image, core, tasks: (
            slice(None), pl.ds(pl.multiple_of(tasks[look(image)] * cot.shape[1], LANES), cot.shape[1])),
         (d, cot.shape[1])),
        (expert_in, which(0), (d, ff)), (expert_in, which(1), (d, ff)), expert_lift,
        (expert_out, which(0), (ff, d)), (expert_out, which(1), (ff, d)), expert_drop, *n[1:],
    ]
    half = ((HALF, width), BF, "near")
    outs = [((PATCHES, width), BF, "near")] if own else [half, half]
    outs += [((2, CAP, d), BF), ((2, CAP, d), BF), ((2, CAP, ff), BF), ((2, CAP, ff), BF)]
    scratch = [] if own else [VMEM((PATCHES, width), BF)]
    scratch += [
        VMEM((EXPERTS, PATCHES), F32), VMEM((EXPERTS, PATCHES), F32),
        VMEM((PATCHES, d), BF), VMEM((PATCHES, d), BF),
    ]

    def body(at, get, put, out, *rest):
        if own:
            experts_body(own, at, get, put, out, *rest)
        else:
            experts_body(own, at, get, put, [*out, rest[0]], *rest[1:])

    return call(body, section, tasks, inputs, outs, scratch, us=13.0)


def expert_masks(expert, blocks):
    masks = near_first(blocks)
    return masks if expert == 1 else [masks[1], masks[0], *masks[2:]]


def weight_grads(expert, section, tasks, own, far, blocks):
    d, ff = own[0].shape[2], own[2].shape[2]
    r = d // blocks // 4
    part = lambda x: (x, lambda s, image, core, tasks: expert, x.shape[1:])
    inputs = [part(x) for pair in zip(own, far) for x in pair]
    shape = (2, blocks // 2, 4, 2 * r, ff + LANES)
    masks = expert_masks(expert, blocks)

    def body(at, get, put, out, pay):
        both = lambda i: jnp.concatenate([get(2 * i)[...], get(2 * i + 1)[...]], axis=0)
        x, du = both(0), both(3)
        step = 512
        grad_in = [mm_tn(x, du[:, f * step : (f + 1) * step]) for f in range(ff // step)]
        lifts = jnp.sum(du.astype(F32), axis=0, keepdims=True)
        dy = both(1)
        drops = jnp.sum(dy.astype(F32), axis=0, keepdims=True)
        small = spread_blocks(lifts, 0, 4 * blocks) + columns_of([drops], [4])
        grad_out = mm_tn(both(2), dy)
        for b in range(blocks):
            i, j = divmod(spot_of(b, masks), blocks // 2)
            for t in range(4):
                row = (4 * b + t) * r
                for f, value in enumerate(grad_in):
                    pay[i, j, t, :r, f * step : (f + 1) * step] = value[row : row + r].astype(BF)
                pay[i, j, t, :r, ff:] = small[row : row + r].astype(BF)
                for k in range(4):
                    at_row = (4 * (4 * b + t) + k) * r
                    pay[i, j, t, r:, k * d : (k + 1) * d] = grad_out[at_row : at_row + r].astype(BF)
                pay[i, j, t, r:, ff:] = jnp.zeros((r, LANES), BF)
        bit = (at[4] // masks[0]) % 2
        put(0, pay.at[1 - bit])
        put(1, pay.at[bit])

    half = (shape[1:], BF, None)
    return call(body, section, tasks, inputs, [half, half], [VMEM(shape, BF)], us=8.0)


def exact_rows(columns):
    sub = lax.broadcasted_iota(jnp.int32, (8, LANES), 0)
    eye = jnp.where(sub == lax.broadcasted_iota(jnp.int32, (8, LANES), 1), 1.0, 0.0).astype(BF)
    high, rest = split_low(columns)
    middle, low = split_low(columns - high.astype(F32))
    del rest
    return mm_nt(eye, high) + mm_nt(eye, middle) + mm_nt(eye, low)


def attend_back_kernel(h, gain, up, core, get_w, get_m, n, q, k, v, o, lse, dc_ref, do_ref, dqkv, pay):
    d = h.shape[1]
    dc_ref[...] = up.astype(BF)
    do_ref[...] = mm_nt(dc_ref[...], get_m()[...]).astype(BF)
    q, k, v, o = q(), k(), v(), o()
    masks = side_masks()
    sums = exact_rows(lse()[...])
    sub, lane = (lax.broadcasted_iota(jnp.int32, (8, d), i) for i in range(2))
    heads = jnp.where(lane // HDIM == sub, 1.0, 0.0).astype(BF)
    high, low = split_low(o[...].astype(F32) * do_ref[...].astype(F32))
    delta = mm_nt(heads, high) + mm_nt(heads, low)
    step = 64
    for p in range(d // LANES):
        at = slice(p * LANES, (p + 1) * LANES)
        dq = dk = dv = None
        for i, mask in enumerate(masks):
            head = 2 * p + i
            scores = mm_nt(k[:, at] * mask, q[:, at])
            dp = mm_nt(v[:, at] * mask, do_ref[:, at])
            probs, ds = [], []
            for r in range(PATCHES // step):
                rows = slice(r * step, (r + 1) * step)
                part = jnp.exp(scores[rows] - sums[head : head + 1])
                probs.append(part.astype(BF))
                ds.append((part * (dp[rows] - delta[head : head + 1])).astype(BF))
            ds = jnp.concatenate(ds, axis=0)
            part = mm(jnp.concatenate(probs, axis=0), do_ref[:, at] * mask)
            dv = part if dv is None else dv + part
            part = mm(ds, q[:, at] * mask)
            dk = part if dk is None else dk + part
            part = mm_tn(ds, k[:, at] * mask * SCALE)
            dq = part if dq is None else dq + part
        dqkv[:, at] = dq.astype(BF)
        dqkv[:, d + p * LANES : d + (p + 1) * LANES] = dk.astype(BF)
        dqkv[:, 2 * d + p * LANES : 2 * d + (p + 1) * LANES] = dv.astype(BF)
    rows = [
        jnp.sum(dqkv[:, :d].astype(F32), axis=0, keepdims=True),
        jnp.sum(dqkv[:, 2 * d :].astype(F32), axis=0, keepdims=True),
        jnp.sum(dc_ref[...].astype(F32), axis=0, keepdims=True),
    ]
    back, grad_gain, grad_shift = norm_back(h, gain, mm_nt(dqkv[...], get_w()[...]))
    n = n()

    @pl.when(core == 0)
    def queries():
        deal(pay, mm_tn(n[...], dqkv[:, :d]), 0)
        deal(pay, mm_tn(n[...], dqkv[:, 2 * d :]), d)

    @pl.when(core == 1)
    def keys_and_merge():
        deal(pay, mm_tn(n[...], dqkv[:, d : 2 * d]), 0)
        deal(pay, mm_tn(o[...], dc_ref[...]), d)

    return up + back, [grad_gain, grad_shift] + rows


def put_halves(put, first, pay, image):
    put(first, pay.at[1 - image])
    put(first + 1, pay.at[image])


def home_body(blocks, at, get, put, out, full, third, dc, do, dqkv, pay):
    (mine, near, whole_own, partner, second, n3, routes, router, cot, dec, bias, gains, h_in, mw, m_m, n, q, k, v, o, lse) = range(21)
    decoded, d1, small = out[0], out[1], out[2]
    s, image, core, tasks = at[:4]
    task = tasks[image]
    d = d1.shape[1]
    full[pl.ds(pl.multiple_of(core * HALF, 16), HALF), :] = get(mine)[...].astype(F32)
    full[pl.ds(pl.multiple_of((1 - core) * HALF, 16), HALF), :] = get(near)[...].astype(F32)
    full[...] += get(whole_own)[...].astype(F32) + get(partner)[...].astype(F32)
    stream = get(second)[...].astype(F32)
    third[...] = (stream + full[:, :d]).astype(BF)
    half = third[pl.ds(pl.multiple_of(core * HALF, 16), HALF), :]
    cot, dec, n3 = get(cot), get(dec), get(n3)
    decoded[...] = mm(half, dec[...]) + get(bias)[pl.ds(task, 1), :]
    put(0)
    hdec = cot.shape[1] // 2
    table = mm_tn(third[...], cot[:, pl.ds(pl.multiple_of(core * hdec, LANES), hdec)])
    deal(pay, jnp.where(task == 0, table, 0.0), 2 * d)
    deal(pay, jnp.where(task == 1, table, 0.0), 2 * d + hdec)

    ids = lax.broadcasted_iota(jnp.int32, (EXPERTS, PATCHES), 0)
    member = jnp.zeros((EXPERTS, PATCHES), F32)
    named = pick_routes(get(routes), image)
    for i in range(TOP):
        member = member + jnp.where(ids == named[i : i + 1, :], 1.0, 0.0)
    member = mm_tn(member.astype(BF), one_hot(EXPERTS, EXPERTS, [(i, i) for i in range(EXPERTS)]))
    table = get(router)
    logits = jnp.where(member > 0.0, mm_nt(n3[...], table[...]), -1e30)
    e = jnp.where(member > 0.0, jnp.exp(logits - jnp.max(logits, axis=1, keepdims=True)), 0.0)
    gates = e / jnp.sum(e, axis=1, keepdims=True)
    dots = full[:, 2 * d :]
    dots = dots[:, :EXPERTS] + dots[:, EXPERTS : 2 * EXPERTS]
    dz = gates * (dots - jnp.sum(gates * dots, axis=1, keepdims=True))
    high, low = split_low(dz)
    grad_router = mm_tn(high, n3[...]) + mm_tn(low, n3[...])
    dn = full[:, d : 2 * d] + mm(high, table[...]) + mm(low, table[...])
    gains = get(gains)
    back, gain1, shift1 = norm_back(stream, gains[1:2], dn)
    up = (mm_nt(cot[...], dec[...]).astype(BF).astype(F32) + back).astype(BF).astype(F32)
    later = lambda i: lambda: get(i)
    result, sums = attend_back_kernel(
        get(h_in)[...].astype(F32), gains[0:1], up, core, later(mw), later(m_m), later(n), later(q), later(k), later(v),
        later(o), later(lse), dc, do, dqkv, pay,
    )
    put_halves(put, 3, pay, image)
    d1[...] = result.astype(BF)
    put(1)
    gain0, shift0, b0, b1, b2 = sums
    routed = columns_of([grad_router], list(range(EXPERTS)))
    small[...] = jnp.where(task == 0, routed, pltpu.roll(routed, EXPERTS, 1)) + columns_of(
        [gain0, gain1, shift0, shift1, b0, b1, b2], [16, 17, 18, 19, 20, 21, 22]
    )
    owners = jnp.sum(cot[...].astype(F32), axis=0, keepdims=True)
    count = cot.shape[1]
    column = columns_of([owners], [24])
    column = jnp.where(task == 0, column, pltpu.roll(column, 1, 1))
    r, some = d // blocks // 2, count // blocks // 2
    for b in range(2 * blocks):
        small[b * r : b * r + some, :] += column[b * some : (b + 1) * some]
    put(2)


def home(section, tasks, payload, second, n3, routes, router, cot, dec, bias, gains, first, mw, m_m, saved, blocks):
    d = second.shape[1]
    width = cot.shape[1]
    inputs = [
        *payload, second, n3, routes, (router, of_task, (EXPERTS, d)),
        (cot, rows_of(PATCHES), (PATCHES, width)),
        (dec, lambda s, image, core, tasks: (slice(None), pl.ds(pl.multiple_of(tasks[image] * width, LANES), width)),
         (d, width)),
        bias, gains, first, mw, m_m, *saved,
    ]
    shape = light_shape(d, blocks, 2 * d + width)
    half = (shape[1:], BF, None)
    outs = [((HALF, width), F32), ((PATCHES, d), BF, "near"), ((d, LANES), F32, "near"), half, half]
    scratch = [
        VMEM((PATCHES, 2 * d + LANES), F32), VMEM((PATCHES, d), BF), VMEM((PATCHES, d), BF), VMEM((PATCHES, d), BF),
        VMEM((PATCHES, 3 * d), BF), VMEM(shape, BF),
    ]
    return call(functools.partial(home_body, blocks), section, tasks, inputs, outs, scratch, us=6.0)


def dense_back_body(blocks, at, get, put, out, du_all, pay):
    d1, sr, slope, sx, a0, gains, small_in, n1, act = range(9)
    da, small = out[0], out[1]
    image, core = at[1], at[2]
    d1, sr, slope, sx = get(d1), get(sr), get(slope), get(sx)
    d, ff = sx.shape
    step = 512
    dn = None
    for f in range(ff // step):
        cols = slice(f * step, (f + 1) * step)
        du = (slope[:, cols].astype(F32) * mm_nt(d1[...], sr[cols, :])).astype(BF)
        du_all[:, cols] = du
        part = mm_nt(du, sx[:, cols])
        dn = part if dn is None else dn + part
    up = d1[...].astype(F32)
    back, gain1, shift1 = norm_back(get(a0)[...], get(gains)[1:2], dn)
    da[...] = up + back
    put(0)
    lifts = jnp.sum(du_all[...].astype(F32), axis=0, keepdims=True)
    b3 = jnp.sum(up, axis=0, keepdims=True)
    small[...] = (
        get(small_in)[...] + spread_blocks(lifts, 40, 2 * blocks) + columns_of([gain1, shift1, b3], [33, 35, 39])
    )
    put(1)
    n1, act = get(n1), get(act)

    @pl.when(core == 0)
    def expand():
        for f in range(ff // step):
            deal(pay, mm_tn(n1[...], du_all[:, f * step : (f + 1) * step]), f * step)

    @pl.when(core == 1)
    def reduce():
        deal_long(pay, mm_tn(act[...], d1[...]))

    put_halves(put, 2, pay, image)


def dense_back(section, tasks, inputs, blocks):
    d, ff = inputs[3].shape
    shape = light_shape(d, blocks, ff)
    half = (shape[1:], BF, None)
    outs = [((PATCHES, d), F32, "near"), ((d, LANES), F32, "near"), half, half]
    return call(
        functools.partial(dense_back_body, blocks), section, tasks, inputs, outs,
        [VMEM((PATCHES, ff), BF), VMEM(shape, BF)], us=9.0,
    )


def stem_back_body(at, get, put, out, full, dc, do, dqkv, pay):
    da, tok, gains, sw, sm, small_in, n, q, k, v, o, lse = range(12)
    image, core = at[1], at[2]
    up = get(da)[...]
    d = up.shape[1]
    later = lambda i: lambda: get(i)
    result, sums = attend_back_kernel(
        get(tok)[...].astype(F32), get(gains)[0:1], up, core, later(sw), later(sm), later(n), later(q), later(k), later(v),
        later(o), later(lse), dc, do, dqkv, pay,
    )
    gain0, shift0, b0, b1, b2 = sums
    small = get(small_in)[...] + columns_of([gain0, shift0, b0, b1, b2], [32, 34, 36, 37, 38])
    deal(pay, jnp.where(core == 0, small, 0.0), 2 * d)
    put_halves(put, 1, pay, image)
    full[...] = result
    put(0, full.at[pl.ds(pl.multiple_of(core * HALF, 8), HALF), :])


def stem_back(section, tasks, da, tokens, gains, sw, sm, small_in, saved, blocks):
    d = da.shape[1]
    inputs = [Near(da), (tokens, rows_of(PATCHES), (PATCHES, d)), gains, sw, sm, Near(small_in), *saved]
    shape = light_shape(d, blocks, 2 * d + LANES)
    half = (shape[1:], BF, None)
    outs = [((HALF, d), F32, None), half, half]
    scratch = [
        VMEM((PATCHES, d), F32), VMEM((PATCHES, d), BF), VMEM((PATCHES, d), BF), VMEM((PATCHES, 3 * d), BF),
        VMEM(shape, BF),
    ]
    return call(stem_back_body, section, tasks, inputs, outs, scratch, us=14.0)


def heavy_out_body(at, get, put, out, gathered):
    grad_in, grad_out, lift, drop = out
    s = at[0]
    r, ff = grad_in.shape[0], grad_in.shape[2]
    d = grad_out.shape[2]
    for mask in range(4):
        for j in range(2):
            gathered[pl.ds(2 * jnp.bitwise_xor(s, mask) + j, 1)] = get(4 * j + mask)[...][None]
    small = []
    for e in range(EXPERTS):
        value = gathered[e].astype(F32)
        grad_in[:, e, :] = value[:r, :ff]
        small.append(value[:r, ff:])
        for k in range(4):
            grad_out[e, k * r : (k + 1) * r, :] = value[r:, k * d : (k + 1) * d]
    put(0)
    put(1)
    row = mm_nt(one_hot(8, LANES, [(k, k) for k in range(5)]), jnp.concatenate(small, axis=0).astype(BF))
    sub, lane = (lax.broadcasted_iota(jnp.int32, (EXPERTS, EXPERTS * r), i) for i in range(2))
    own = jnp.where(lane // r == sub, 1.0, 0.0)
    spread = lambda k, wide: jnp.where(
        lax.broadcasted_iota(jnp.int32, (EXPERTS * r, wide), 1)
        == k * r + lax.broadcasted_iota(jnp.int32, (EXPERTS * r, wide), 0) % r,
        1.0, 0.0,
    ).astype(BF)
    parts = [mm((own * row[k : k + 1]).astype(BF), spread(k, 4 * r)) for k in range(4)]
    lift[...] = parts[0] + parts[1] + parts[2] + parts[3]
    drop[...] = mm((own * row[4:5]).astype(BF), spread(0, r))
    put(2)
    put(3)


def heavy_out(section, tasks, pieces, d):
    r2, wide = pieces[0].shape
    r, ff = r2 // 2, wide - LANES
    outs = [
        ((r, EXPERTS, ff), F32), ((EXPERTS, 4 * r, d), F32), ((EXPERTS, 4 * r), F32), ((EXPERTS, r), F32)
    ]
    return call(heavy_out_body, section, tasks, [Near(x) for x in pieces], outs, [VMEM((EXPERTS, r2, wide), BF)])


def light_out_body(d, dec, at, get, put, out, both):
    (mix_heads, mix_merge, dec_out, expand, reduce, stem_heads, stem_merge, router, lift, bias) = out[:10]
    rows = out[10:]
    core = at[2]
    both[pl.ds(core, 1)] = get(0)[...][None]
    both[pl.ds(1 - core, 1)] = get(1)[...][None]
    r = expand.shape[0]
    m, ff, hdec = 2 * d + dec, expand.shape[1], dec // 2
    a, b = both[0].astype(F32), both[1].astype(F32)
    tiny = a[:, m + ff + 2 * d :]
    order = (32, 33, 34, 35, 36, 37, 38, 39, 16, 17, 18, 19, 20, 21, 22, 24, 25, 40, 41, 42, 43, 127, 127, 127)
    order = order + tuple(range(2 * EXPERTS))
    turned = mm_nt(one_hot(len(order), LANES, list(enumerate(order))), tiny.astype(BF))
    some = bias.shape[1]
    for c in range(2):

        @pl.when(core == c)
        def write():
            x, y = a[c * r : (c + 1) * r], b[c * r : (c + 1) * r]
            for heads, merge, base in ((mix_heads, mix_merge, 0), (stem_heads, stem_merge, m + ff)):
                heads[:, :d] = x[:, base : base + d]
                heads[:, d : 2 * d] = y[:, base : base + d]
                heads[:, 2 * d :] = x[:, base + d : base + 2 * d]
                merge[...] = y[:, base + d : base + 2 * d]
            for t in range(2):
                dec_out[:, t, :hdec] = x[:, 2 * d + t * hdec : 2 * d + (t + 1) * hdec]
                dec_out[:, t, hdec:] = y[:, 2 * d + t * hdec : 2 * d + (t + 1) * hdec]
                router[t] = turned[24 + t * EXPERTS : 24 + (t + 1) * EXPERTS, c * r : (c + 1) * r]
            expand[...] = x[:, m : m + ff]
            for k in range(2):
                at_lane = m + (2 * c + k) * d
                reduce[k * 2 * r : (k + 1) * 2 * r, :] = b[:, at_lane : at_lane + d]
            first = 0
            for part in rows:
                part[...] = turned[first : first + part.shape[0], c * r : (c + 1) * r]
                first += part.shape[0]
            bias[...] = turned[first : first + 2, c * some : (c + 1) * some]
            parts = [turned[first + 2 + 2 * c + k : first + 3 + 2 * c + k] for k in range(2)]
            lift[...] = jnp.concatenate(parts, axis=1)[0]

    for i in range(len(out)):
        put(i)


def light_out(section, tasks, mine, near, d, dec, ff, some):
    r2 = mine.shape[0]
    r = r2 // 2
    shapes = [
        (r, 3 * d), (r, d), (r, 2, dec), (r, ff), (4 * r, d), (r, 3 * d), (r, d), (2, EXPERTS, r), (2 * r2,), (2, some),
        (2, r), (2, r), (4, r), (2, r), (2, r), (3, r),
    ]
    return call(
        functools.partial(light_out_body, d, dec), section, tasks, [Near(mine), Near(near)], [(x, F32) for x in shapes],
        [VMEM((2,) + mine.shape, BF)],
    )


def after(x, *others):
    return lax.optimization_barrier((x, *others))[0]


def swap(x, axis, mask):
    size = lax.axis_size(axis)
    return lax.ppermute(x, axis, [(i, i ^ mask) for i in range(size)])


def add_low(*terms):
    return sum(t.astype(F32) for t in terms).astype(BF)


def take(x, i):
    return lax.dynamic_index_in_dim(x, i, 0, keepdims=False)


def halve(terms, axis, mask):
    bit = (lax.axis_index(axis) // mask) % 2
    terms = [x.reshape((2, x.shape[0] // 2) + x.shape[1:]) for x in terms]
    send = add_low(*[take(t, 1 - bit) for t in terms])
    return [add_low(*[take(t, bit) for t in terms]), swap(send, axis, mask)], send


def body(
    tokens, routes, task_ids, cotangent, stem_gains, stem_shifts, stem_heads, stem_merge,
    stem_biases, stem_expand, stem_lift, stem_reduce, mix_gains, mix_shifts, mix_heads,
    mix_merge, mix_biases, router, expert_in, expert_lift, expert_out, expert_drop, decoder,
    decoder_bias,
):
    s = lax.axis_index("section")
    image = s // 2
    section = jnp.stack([s, lax.axis_index("dp")])
    ndp, ns = lax.axis_size("dp"), lax.axis_size("section")
    d, ff, dec = tokens.shape[1], stem_expand.shape[1], cotangent.shape[1]
    r, q = d // ndp, d // ndp // ns

    weights = [
        stem_heads, stem_gains, stem_shifts, stem_biases, stem_merge, stem_expand, stem_lift, stem_reduce, mix_heads,
        mix_gains, mix_shifts, mix_biases, mix_merge,
    ]
    (n0, q0, k0, v0, o0, l0, a0, n1, act, slope, first, n2, q2, k2, v2, o2, l2, second, n3, n3_cut) = forward(
        section, task_ids, tokens, weights
    )
    far = swap(n3_cut, "section", 2)

    routes_t = routes.T
    router_t = router.transpose(1, 2, 0)
    dec_flat = decoder.reshape(d, -1)
    common = (routes_t, router_t, cotangent, dec_flat, (expert_in, expert_lift, expert_out, expert_drop))
    own_pay, *own = experts(True, section, task_ids, [n3], *common)
    far = after(far, own_pay)
    near = swap(far, "section", 1)
    own_got = swap(own_pay, "section", 1)
    far_send, far_keep, *away = experts(False, section, task_ids, [Near(far), Near(near)], *common)
    crossed = add_low(far_keep, swap(far_send, "section", 1))
    away[0] = after(away[0], crossed)
    crossed = swap(crossed, "section", 2)
    later_send, later_keep = weight_grads(1, section, task_ids, own, away, ndp)
    first_later, first_sooner = (expert_masks(e, ndp) for e in (1, 0))
    later_got = swap(later_send, "dp", first_later[0])
    crossed = after(crossed, later_keep)
    away[0] = after(away[0], crossed)
    sooner_send, sooner_keep = weight_grads(0, section, task_ids, own, away, ndp)
    sooner_got = swap(sooner_send, "dp", first_sooner[0])
    payload = [Near(crossed), Near(swap(crossed, "section", 1)), own_pay, own_got]

    decoded, d1, small, mix_send, mix_keep = home(
        section, task_ids, payload, second, n3, routes_t, router_t, cotangent, dec_flat, decoder_bias,
        mix_gains, first, mix_heads, mix_merge, (n2, q2, k2, v2, o2, l2), ndp,
    )
    mix_got = swap(mix_send, "section", 2)
    later, sent = halve([later_keep, after(later_got, mix_keep)], "dp", first_later[1])
    d1 = after(d1, sent)
    da, small, dense_send, dense_keep = dense_back(
        section, task_ids, [Near(d1), stem_reduce, slope, stem_expand, a0, stem_gains, Near(small), n1, act], ndp
    )
    dense_got = swap(dense_send, "section", 2)
    mix, mix_sent = halve([mix_keep, after(mix_got, da)], "dp", 1)
    sooner, sent = halve([sooner_keep, after(sooner_got, da)], "dp", first_sooner[1])
    da = after(da, mix_sent, sent)
    d0, stem_send, stem_keep = stem_back(
        section, task_ids, da, tokens, stem_gains, stem_heads, stem_merge, small, (n0, q0, k0, v0, o0, l0), ndp
    )
    stem_got = swap(stem_send, "section", 2)

    masks = near_first(ndp)
    join = lambda xs, ys: [jnp.concatenate([x, y], axis=-1) for x, y in zip(xs, ys)]
    later, later_sent = halve([later[0], after(later[1], d0)], "dp", masks[2])
    dense, dense_sent = halve([dense_keep, after(dense_got, d0, mix[1])], "dp", 1)
    sooner, sooner_sent = halve([sooner[0], after(sooner[1], d0, later_sent)], "dp", masks[2])
    stem, stem_sent = halve([stem_keep, after(stem_got, dense_sent, sooner_sent)], "dp", 1)
    wide, wide_sent = halve(join(mix, [dense[0], after(dense[1], stem_sent)]), "dp", 2)
    stem, stem_sent = halve([stem[0], after(stem[1], wide_sent)], "dp", 2)

    def pieces(terms):
        for mask in masks[3:]:
            terms, unused = halve(terms, "dp", mask)
        x = add_low(*terms)[0]
        return [take(x, s)] + [swap(take(x, s ^ mask), "section", mask) for mask in (1, 2, 3)]

    later = pieces([later[0], after(later[1], stem_sent)])
    light = join([wide[0], after(wide[1], stem_sent)], stem)
    for mask in masks[2:]:
        light, sent = halve(light, "dp", mask)
    sooner = pieces([sooner[0], after(sooner[1], sent)])
    grad_in, grad_out, g_elift, g_edrop = heavy_out(section, task_ids, sooner + later, d)
    light = add_low(*light)[0]
    light_near = swap(light, "section", 1)

    (
        g_mix_heads, g_mix_merge, g_dec, g_expand, g_reduce, g_stem_heads, g_stem_merge, g_router, g_lift, g_bias,
        g_stem_gains, g_stem_shifts, g_stem_biases, g_mix_gains, g_mix_shifts, g_mix_biases,
    ) = light_out(section, task_ids, light, light_near, d, dec, ff, dec // ndp // ns)
    return (
        decoded, d0, g_stem_gains, g_stem_shifts, g_stem_heads, g_stem_merge, g_stem_biases, g_expand,
        g_lift, g_reduce, g_mix_gains, g_mix_shifts, g_mix_heads, g_mix_merge, g_mix_biases, g_router.transpose(2, 0, 1),
        grad_in.transpose(1, 0, 2), g_elift, grad_out, g_edrop, g_dec, g_bias,
    )


def solution(mesh):
    both = ("dp", "section")
    placed = (P("dp", None), P("dp", None), P("dp"), P("dp", None)) + (P(),) * 20
    rows, columns = P(both, None), P(None, both)
    return jax.shard_map(
        body,
        mesh=mesh,
        in_specs=placed,
        out_specs=(
            rows, rows, columns, columns, rows, rows, columns, rows, P(both), rows, columns,
            columns, rows, rows, columns, P(both, None, None), P(None, both, None), columns,
            P(None, both, None), columns, P(both, None, None), columns,
        ),
        check_vma=False,
    )
```

```python
import functools
import math

import jax
import jax.numpy as jnp
from jax import lax
from jax.experimental import pallas as pl
from jax.experimental.pallas import tpu as pltpu
from jax.sharding import PartitionSpec as P

HEADS = 6
HDIM = 64
EXPERTS = 8
TOP = 4
PATCHES = 576
HALF = PATCHES // 2
CAP = 288
LANES = 128
EPSILON = 1e-06
SCALE = 1.0 / math.sqrt(HDIM)
BF = jnp.bfloat16
F32 = jnp.float32
VMEM = pltpu.VMEM
MIB = 1 << 20


def mm(a, b):
    return jnp.dot(a, b, preferred_element_type=F32)


def mm_tn(a, b):
    return lax.dot_general(a, b, (((0,), (0,)), ((), ())), preferred_element_type=F32)


def mm_nt(a, b):
    return lax.dot_general(a, b, (((1,), (1,)), ((), ())), preferred_element_type=F32)


def split_low(v):
    high = v.astype(BF)
    return high, (v - high.astype(F32)).astype(BF)


def norm_parts(v):
    centred = v - jnp.mean(v, axis=-1, keepdims=True)
    inverse = lax.rsqrt(jnp.mean(centred * centred, axis=-1, keepdims=True) + EPSILON)
    return centred * inverse, inverse


def norm_back(v, gain, up):
    unit, inverse = norm_parts(v)
    scaled = up * gain
    back = inverse * (
        scaled
        - jnp.mean(scaled, axis=-1, keepdims=True)
        - unit * jnp.mean(scaled * unit, axis=-1, keepdims=True)
    )
    return back, jnp.sum(up * unit, axis=0, keepdims=True), jnp.sum(up, axis=0, keepdims=True)


def gelu_both(u):
    t = pl.reciprocal(1.0 + (0.3275911 / math.sqrt(2.0)) * jnp.abs(u), approx=True)
    bell = jnp.exp2((-0.5 / math.log(2.0)) * u * u)
    poly = 0.5 * 1.421413741 + t * (0.5 * -1.453152027 + t * (0.5 * 1.061405429))
    tail = bell * (t * (0.5 * 0.254829592 + t * (0.5 * -0.284496736 + t * poly)))
    cdf = jnp.where(u >= 0.0, 1.0 - tail, tail)
    return u * cdf, cdf + u * bell * (1.0 / math.sqrt(2.0 * math.pi))


def side_masks():
    lane = lax.broadcasted_iota(jnp.int32, (1, LANES), 1)
    left = (lane < HDIM).astype(F32)
    return left.astype(BF), (1.0 - left).astype(BF)


def lane_ids(rows=1):
    return lax.broadcasted_iota(jnp.int32, (rows, LANES), 1)


def near_first(blocks):
    return [1 << i for i in range(blocks.bit_length() - 1)]


def spot_of(block, masks):
    spot = 0
    for mask in masks:
        spot = 2 * spot + (block // mask) % 2
    return spot


def deal(pay, value, at):
    r, w = pay.shape[2], value.shape[1]
    for b in range(pay.shape[1]):
        spot = spot_of(b, near_first(pay.shape[1]))
        for y in range(2):
            piece = value[(2 * b + y) * r : (2 * b + y + 1) * r]
            pay[y, spot, :, at : at + w] = piece.astype(BF)


def deal_long(pay, value, at):
    r, w = pay.shape[2], value.shape[1]
    for b in range(pay.shape[1]):
        spot = spot_of(b, near_first(pay.shape[1]))
        for y in range(2):
            for k in range(4):
                piece = value[(8 * b + 4 * y + k) * r : (8 * b + 4 * y + k + 1) * r]
                pay[y, spot, :, at + k * w : at + (k + 1) * w] = piece.astype(BF)


def light_shape(d, blocks, width):
    return (2, blocks, d // blocks // 2, width)


def one_hot(rows, columns, hits):
    sub, lane = (lax.broadcasted_iota(jnp.int32, (rows, columns), i) for i in range(2))
    total = jnp.zeros((rows, columns), F32)
    for i, j in hits:
        total = total + jnp.where((sub == i) & (lane == j), 1.0, 0.0)
    return total.astype(BF)


def columns_of(rows, lanes):
    count = -(-len(lanes) // 8) * 8
    n = rows[0].shape[1]
    spare = [jnp.zeros((count - len(lanes), n), F32)] if count > len(lanes) else []
    stacked = jnp.concatenate(rows + spare, axis=0)
    place = lax.broadcasted_iota(jnp.int32, (count, LANES), 0)
    lane = lane_ids(count)
    spread = jnp.zeros((count, LANES), F32)
    for i, at in enumerate(lanes):
        spread = spread + jnp.where((place == i) & (lane == at), 1.0, 0.0)
    return mm_tn(stacked.astype(BF), spread.astype(BF))


def spread_blocks(row, first_lane, blocks):
    n = row.shape[1]
    r = n // 4 // blocks
    place = lax.broadcasted_iota(jnp.int32, (8, LANES), 0)
    stacked = jnp.concatenate([row, jnp.zeros((7, n), F32)], axis=0)
    column = mm_tn(stacked.astype(BF), jnp.where(place == 0, 1.0, 0.0).astype(BF))
    lane = lane_ids()
    parts = []
    for b in range(blocks):
        part = None
        for s in range(4):
            at = (4 * b + s) * r
            piece = jnp.where(lane == first_lane + s, column[at : at + r], 0.0)
            part = piece if part is None else part + piece
        parts.append(part)
    return jnp.concatenate(parts, axis=0)


class Near:
    def __init__(self, array):
        self.array = array


class Fetched:
    def __init__(self, moves):
        self.moves = moves
        for move in moves:
            move.start()

    def wait(self):
        for move in self.moves:
            move.wait()
        self.moves = []


def run_kernel(body, n_in, n_out, picks, near_out, *refs):
    section, tasks = refs[:2]
    inputs, outputs = refs[2 : 2 + n_in], refs[2 + n_in : 2 + n_in + n_out]
    rest = refs[2 + n_in + n_out :]
    kept_in, kept_out = rest[:n_in], rest[n_in : n_in + n_out]
    in_sems, out_sems = rest[n_in + n_out : n_in + n_out + 2]
    kept_out = [outputs[i] if i in near_out else kept_out[i] for i in range(n_out)]
    at = (section[0], section[0] // 2, section[0] % 2, tasks, section[1])
    fetched, moving = [], []
    for i in range(n_in):
        if picks[i] == "near":
            fetched.append(None)
            continue
        source = inputs[i] if picks[i] is None else inputs[i].at[picks[i](*at[:4])]
        fetched.append(Fetched([pltpu.make_async_copy(source, kept_in[i], in_sems.at[i])]))

    def get(i):
        if fetched[i] is None:
            return inputs[i]
        fetched[i].wait()
        return kept_in[i]

    def put(i, source=None, part=None):
        if i in near_out:
            return
        source = kept_out[i] if source is None else source
        target = outputs[i] if part is None else outputs[i].at[part]
        move = pltpu.make_async_copy(source, target, out_sems.at[i if part is None else i + part * n_out])
        move.start()
        moving.append(move)

    body(at, get, put, kept_out, *rest[n_in + n_out + 2 :])
    for i in range(n_in):
        get(i)
    for move in moving:
        move.wait()


def call(body, section, tasks, inputs, outs, scratch=(), us=3.0, limit=56):
    arrays, picks, kept = [], [], []
    for x in inputs:
        if isinstance(x, Near):
            arrays.append(x.array)
            picks.append("near")
            kept.append(VMEM((8, LANES), F32))
            continue
        array, pick, shape = x if isinstance(x, tuple) else (x, None, x.shape)
        arrays.append(array)
        picks.append(pick)
        kept.append(VMEM(shape, array.dtype))
    kept_out = [VMEM(o[0], o[1]) if len(o) == 2 else VMEM((8, LANES), F32) for o in outs]
    near_out = [i for i, o in enumerate(outs) if len(o) == 3 and o[2] == "near"]
    anywhere, scalar = pl.BlockSpec(memory_space=pl.ANY), pl.BlockSpec(memory_space=pltpu.SMEM)
    here = pl.BlockSpec(memory_space=pltpu.VMEM)
    return pl.pallas_call(
        functools.partial(run_kernel, body, len(arrays), len(outs), picks, near_out),
        out_shape=[jax.ShapeDtypeStruct(o[0], o[1]) for o in outs],
        in_specs=[scalar, scalar] + [here if p == "near" else anywhere for p in picks],
        out_specs=[here if i in near_out else anywhere for i in range(len(outs))],
        scratch_shapes=[
            *kept, *kept_out, pltpu.SemaphoreType.DMA((len(arrays),)), pltpu.SemaphoreType.DMA((2 * len(outs),)), *scratch
        ],
        compiler_params=pltpu.CompilerParams(vmem_limit_bytes=limit * MIB),
        cost_estimate=pl.CostEstimate(flops=int(us * 1.1e9), bytes_accessed=1, transcendentals=0),
    )(section, tasks, *arrays)


def rows_of(count):
    return lambda s, image, core, tasks: pl.ds(pl.multiple_of(image * count, count), count)


def of_task(s, image, core, tasks):
    return tasks[image]


def attend_kernel(h, gain, shift, get_w, c, get_m, n_ref, q_ref, k_ref, v_ref, o_ref, lse_ref, done):
    d = h.shape[1]
    unit, unused = norm_parts(h)
    n_ref[...] = (unit * gain + shift).astype(BF)
    done(0)
    n, w = n_ref[...], get_w()
    q_ref[...] = ((mm(n, w[:, :d]) + c[0:1]) * SCALE).astype(BF)
    done(1)
    k_ref[...] = mm(n, w[:, d : 2 * d]).astype(BF)
    done(2)
    v_ref[...] = (mm(n, w[:, 2 * d :]) + c[1:2]).astype(BF)
    done(3)
    masks = side_masks()
    lane = lane_ids()
    sums = jnp.zeros((PATCHES, LANES), F32)
    step = 32
    for p in range(d // LANES):
        at = slice(p * LANES, (p + 1) * LANES)
        total = None
        for i, mask in enumerate(masks):
            scores = mm_nt(q_ref[:, at] * mask, k_ref[:, at])
            e, norm, top = [], [], []
            for r in range(PATCHES // step):
                part = scores[r * step : (r + 1) * step]
                most = jnp.max(part, axis=-1, keepdims=True)
                part = jnp.exp(part - most)
                e.append(part.astype(BF))
                norm.append(jnp.sum(part, axis=-1, keepdims=True))
                top.append(most)
            norm = jnp.concatenate(norm, axis=0)
            part = mm(jnp.concatenate(e, axis=0), v_ref[:, at] * mask) * (1.0 / norm)
            total = part if total is None else total + part
            sums = jnp.where(lane == 2 * p + i, jnp.concatenate(top, axis=0) + jnp.log(norm), sums)
        o_ref[:, at] = total.astype(BF)
    lse_ref[...] = sums
    done(4)
    done(5)
    return h + (mm(o_ref[...], get_m()[...]) + c[2:3])


def forward_body(at, get, put, out, *scratch):
    tok, sw, sg, ss, sb, sm, sx, sl, sr, mw, mg, ms, mb, m_m = range(14)
    (n0, q0, k0, v0, o0, l0, a0, n1, act, slope, first, n2, q2, k2, v2, o2, l2, second, n3) = out
    h = get(tok)[...].astype(F32)
    sg, ss, sb = get(sg), get(ss), get(sb)
    a = attend_kernel(
        h, sg[0:1], ss[0:1], lambda: get(sw), sb, lambda: get(sm), n0, q0, k0, v0, o0, l0, put
    )
    a0[...] = a
    put(6)
    unit, unused = norm_parts(a0[...])
    n1[...] = (unit * sg[1:2] + ss[1:2]).astype(BF)
    put(7)
    step = 512
    wx, lift = get(sx), get(sl)
    for f in range(wx.shape[1] // step):
        cols = slice(f * step, (f + 1) * step)
        active, bend = gelu_both(mm(n1[...], wx[:, cols]) + lift[cols][None, :])
        act[:, cols] = active.astype(BF)
        slope[:, cols] = bend.astype(BF)
    put(8)
    put(9)
    first[...] = (a0[...] + (mm(act[...], get(sr)[...]) + sb[3:4])).astype(BF)
    put(10)
    mg, ms, mb = get(mg), get(ms), get(mb)
    second[...] = attend_kernel(
        first[...].astype(F32), mg[0:1], ms[0:1], lambda: get(mw), mb, lambda: get(m_m), n2, q2, k2, v2,
        o2, l2, lambda i: put(11 + i),
    ).astype(BF)
    put(17)
    unit, unused = norm_parts(second[...].astype(F32))
    n3[...] = (unit * mg[1:2] + ms[1:2]).astype(BF)


def forward(section, tasks, tokens, weights):
    d = tokens.shape[1]
    ff = weights[5].shape[1]
    wide = ((PATCHES, d), BF)
    sums = ((PATCHES, LANES), F32)
    outs = [wide] * 5 + [sums, ((PATCHES, d), F32), wide, ((PATCHES, ff), BF), ((PATCHES, ff), BF)]
    outs += [wide] * 6 + [sums, wide, wide + ("near",)]
    inputs = [(tokens, rows_of(PATCHES), (PATCHES, d)), *weights]
    return call(forward_body, section, tasks, inputs, outs, us=20.0)


def pick_routes(ref, image):
    every = ref[...]
    chosen = every[:, :PATCHES]
    for i in range(1, every.shape[1] // PATCHES):
        chosen = jnp.where(image == i, every[:, i * PATCHES : (i + 1) * PATCHES], chosen)
    return chosen


def experts_body(own, at, get, put, out, gates, place, d3):
    n, routes, router, cot, dec, w_in0, w_in1, lift, w_out0, w_out1, drop = range(11)
    core = at[2]
    if own:
        full, xs, dys, acts, dus = out
        first = 1
    else:
        send, keep, xs, dys, acts, dus, full = out
        first = 2
    n_ref = get(n)
    ids = lax.broadcasted_iota(jnp.int32, (EXPERTS, PATCHES), 0)
    member = jnp.zeros((EXPERTS, PATCHES), F32)
    named = pick_routes(get(routes), at[1] if own else 1 - at[1])
    for k in range(TOP):
        member = member + jnp.where(ids == named[k : k + 1, :], 1.0, 0.0)
    logits = jnp.where(member > 0.0, mm_nt(get(router)[...], n_ref[...]), -1e30)
    e = jnp.where(member > 0.0, jnp.exp(logits - jnp.max(logits, axis=0, keepdims=True)), 0.0)
    gates[...] = e / jnp.sum(e, axis=0, keepdims=True)
    before = lax.broadcasted_iota(jnp.int32, (PATCHES, PATCHES), 0)
    after_ = lax.broadcasted_iota(jnp.int32, (PATCHES, PATCHES), 1)
    upper = jnp.where(before <= after_, 1.0, 0.0).astype(BF)
    place[...] = jnp.where(member > 0.0, mm(member.astype(BF), upper) - 1.0, -1.0)
    d3[...] = mm_nt(get(cot)[...], get(dec)[...]).astype(BF)
    total = None
    lifts, drops = get(lift), get(drop)
    for j in range(2):
        e = 2 * at[0] + j
        spot = place[pl.ds(e, 1), :].astype(jnp.int32)
        hit = lax.broadcasted_iota(jnp.int32, (CAP, PATCHES), 0) == spot
        pick = jnp.where(hit, 1.0, 0.0)
        weight = jnp.sum(pick * gates[pl.ds(e, 1), :], axis=1, keepdims=True)
        pick = pick.astype(BF)
        x = mm(pick, n_ref[...]).astype(BF)
        up = mm(pick, d3[...])
        dy = (weight * up).astype(BF)
        xs[j] = x
        dys[j] = dy
        w_in, w_out = get((w_in0, w_in1)[j]), get((w_out0, w_out1)[j])
        ff = w_in.shape[1]
        step = 1536
        y = drops[pl.ds(e, 1), :]
        dx = None
        for f in range(ff // step):
            cols = slice(f * step, (f + 1) * step)
            active, bend = gelu_both(mm(x, w_in[:, cols]) + lifts[pl.ds(e, 1), cols])
            active = active.astype(BF)
            du = (bend * mm_nt(dy, w_out[cols, :])).astype(BF)
            y = y + mm(active, w_out[cols, :])
            part = mm_nt(du, w_in[:, cols])
            dx = part if dx is None else dx + part
            acts[j, :, cols] = active
            dus[j, :, cols] = du
        for i, kept in enumerate((xs, dys, acts, dus)):
            put(first + i, kept.at[j], j)
        dots = jnp.sum(y * up, axis=1, keepdims=True)
        high = dots.astype(BF).astype(F32)
        lane = lane_ids()
        marks = jnp.where(lane == e, high, jnp.where(lane == e + EXPERTS, dots - high, 0.0))
        rhs = jnp.concatenate([(weight * y).astype(BF), dx.astype(BF), marks.astype(BF)], axis=1)
        home = mm_tn(pick, rhs)
        total = home if total is None else total + home
    full[...] = total.astype(BF)
    if not own:
        send[...] = full[pl.ds(pl.multiple_of((1 - core) * HALF, 16), HALF), :]
        keep[...] = full[pl.ds(pl.multiple_of(core * HALF, 16), HALF), :]


def experts(own, section, tasks, n, routes_t, router_t, cot, dec, weights):
    expert_in, expert_lift, expert_out, expert_drop = weights
    d, ff = expert_in.shape[1:]
    width = 2 * d + LANES
    look = (lambda image: image) if own else (lambda image: 1 - image)
    which = lambda j: lambda s, image, core, tasks: 2 * s + j
    inputs = [
        Near(n),
        routes_t,
        (router_t, lambda s, image, core, tasks: tasks[look(image)], (EXPERTS, d)),
        (cot, lambda s, image, core, tasks: pl.ds(pl.multiple_of(look(image) * PATCHES, PATCHES), PATCHES),
         (PATCHES, cot.shape[1])),
        (dec, lambda s, image, core, tasks: (
            slice(None), pl.ds(pl.multiple_of(tasks[look(image)] * cot.shape[1], LANES), cot.shape[1])),
         (d, cot.shape[1])),
        (expert_in, which(0), (d, ff)), (expert_in, which(1), (d, ff)), expert_lift,
        (expert_out, which(0), (ff, d)), (expert_out, which(1), (ff, d)), expert_drop,
    ]
    half = ((HALF, width), BF, "near")
    outs = [((PATCHES, width), BF, "near")] if own else [half, half]
    outs += [((2, CAP, d), BF), ((2, CAP, d), BF), ((2, CAP, ff), BF), ((2, CAP, ff), BF)]
    scratch = [] if own else [VMEM((PATCHES, width), BF)]
    scratch += [
        VMEM((EXPERTS, PATCHES), F32), VMEM((EXPERTS, PATCHES), F32),
        VMEM((PATCHES, d), BF),
    ]

    def body(at, get, put, out, *rest):
        if own:
            experts_body(own, at, get, put, out, *rest)
        else:
            experts_body(own, at, get, put, [*out, rest[0]], *rest[1:])

    return call(body, section, tasks, inputs, outs, scratch, us=13.0)


def expert_masks(expert, blocks):
    masks = near_first(blocks)
    return masks if expert == 1 else [masks[1], masks[0], *masks[2:]]


def weight_grads(section, tasks, own, far, blocks):
    d, ff = own[0].shape[2], own[2].shape[2]
    r = d // blocks // 4
    part = lambda x, e: (x, lambda s, image, core, tasks: e, x.shape[1:])
    inputs = [part(x, e) for e in (1, 0) for pair in zip(own, far) for x in pair]
    shape = (2, blocks // 2, 4, 2 * r, ff)

    def body(at, get, put, out, *pays):
        small = out[4]
        for place, e in enumerate((1, 0)):
            pay, masks = pays[place], expert_masks(e, blocks)
            both = lambda i: jnp.concatenate([get(8 * place + 2 * i)[...], get(8 * place + 2 * i + 1)[...]], axis=0)
            x, du = both(0), both(3)
            step = 512
            grad_in = [mm_tn(x, du[:, f * step : (f + 1) * step]) for f in range(ff // step)]
            lifts = jnp.sum(du.astype(F32), axis=0, keepdims=True)
            dy = both(1)
            drops = jnp.sum(dy.astype(F32), axis=0, keepdims=True)
            tiny = spread_blocks(lifts, 5 * e, 2 * blocks) + columns_of([drops], [5 * e + 4])
            small[...] = tiny if place == 0 else small[...] + tiny
            grad_out = mm_tn(both(2), dy)
            for b in range(blocks):
                i, j = divmod(spot_of(b, masks), blocks // 2)
                for t in range(4):
                    row = (4 * b + t) * r
                    for f, value in enumerate(grad_in):
                        pay[i, j, t, :r, f * step : (f + 1) * step] = value[row : row + r].astype(BF)
                    for k in range(4):
                        at_row = (4 * (4 * b + t) + k) * r
                        pay[i, j, t, r:, k * d : (k + 1) * d] = grad_out[at_row : at_row + r].astype(BF)
            bit = (at[4] // masks[0]) % 2
            put(2 * place, pay.at[1 - bit])
            put(2 * place + 1, pay.at[bit])
        moved = small[...]
        for s in range(4):
            moved = jnp.where(at[0] == s, pltpu.roll(small[...], 64 + 10 * s, 1), moved)
        small[...] = moved
        put(4)

    half = (shape[1:], BF, None)
    outs = [half] * 4 + [((d, LANES), F32)]
    return call(body, section, tasks, inputs, outs, [VMEM(shape, BF)] * 2, us=14.0)


def exact_rows(columns):
    sub = lax.broadcasted_iota(jnp.int32, (8, LANES), 0)
    eye = jnp.where(sub == lax.broadcasted_iota(jnp.int32, (8, LANES), 1), 1.0, 0.0).astype(BF)
    high, rest = split_low(columns)
    middle, low = split_low(columns - high.astype(F32))
    del rest
    return mm_nt(eye, high) + mm_nt(eye, middle) + mm_nt(eye, low)


def attend_back_kernel(h, gain, up, core, get_w, get_m, n, q, k, v, o, lse, dc_ref, do_ref, dqkv, pay):
    d = h.shape[1]
    dc_ref[...] = up.astype(BF)
    do_ref[...] = mm_nt(dc_ref[...], get_m()[...]).astype(BF)
    q, k, v, o = q(), k(), v(), o()
    masks = side_masks()
    sums = exact_rows(lse()[...])
    sub, lane = (lax.broadcasted_iota(jnp.int32, (8, d), i) for i in range(2))
    heads = jnp.where(lane // HDIM == sub, 1.0, 0.0).astype(BF)
    high, low = split_low(o[...].astype(F32) * do_ref[...].astype(F32))
    delta = mm_nt(heads, high) + mm_nt(heads, low)
    step = 64
    for p in range(d // LANES):
        at = slice(p * LANES, (p + 1) * LANES)
        dq = dk = dv = None
        for i, mask in enumerate(masks):
            head = 2 * p + i
            scores = mm_nt(k[:, at] * mask, q[:, at])
            dp = mm_nt(v[:, at] * mask, do_ref[:, at])
            probs, ds = [], []
            for r in range(PATCHES // step):
                rows = slice(r * step, (r + 1) * step)
                part = jnp.exp(scores[rows] - sums[head : head + 1])
                probs.append(part.astype(BF))
                ds.append((part * (dp[rows] - delta[head : head + 1])).astype(BF))
            ds = jnp.concatenate(ds, axis=0)
            part = mm(jnp.concatenate(probs, axis=0), do_ref[:, at] * mask)
            dv = part if dv is None else dv + part
            part = mm(ds, q[:, at] * mask)
            dk = part if dk is None else dk + part
            part = mm_tn(ds, k[:, at] * mask * SCALE)
            dq = part if dq is None else dq + part
        dqkv[:, at] = dq.astype(BF)
        dqkv[:, d + p * LANES : d + (p + 1) * LANES] = dk.astype(BF)
        dqkv[:, 2 * d + p * LANES : 2 * d + (p + 1) * LANES] = dv.astype(BF)
    rows = [
        jnp.sum(dqkv[:, :d].astype(F32), axis=0, keepdims=True),
        jnp.sum(dqkv[:, 2 * d :].astype(F32), axis=0, keepdims=True),
        jnp.sum(dc_ref[...].astype(F32), axis=0, keepdims=True),
    ]
    back, grad_gain, grad_shift = norm_back(h, gain, mm_nt(dqkv[...], get_w()[...]))
    n = n()

    @pl.when(core == 0)
    def queries():
        deal(pay, mm_tn(n[...], dqkv[:, :d]), 0)
        deal(pay, mm_tn(n[...], dqkv[:, 2 * d :]), d)

    @pl.when(core == 1)
    def keys_and_merge():
        deal(pay, mm_tn(n[...], dqkv[:, d : 2 * d]), 0)
        deal(pay, mm_tn(o[...], dc_ref[...]), d)

    return up + back, [grad_gain, grad_shift] + rows


def put_halves(put, first, pay, image):
    put(first, pay.at[1 - image])
    put(first + 1, pay.at[image])


def dense_part(blocks, at, get, d1, da, small, pay, du_all, lane):
    sr, slope, sx, a0, gains, n1, act = range(7)
    core = at[2]
    sr, slope, sx = get(sr), get(slope), get(sx)
    d, ff = sx.shape
    step = 512
    dn = None
    for f in range(ff // step):
        cols = slice(f * step, (f + 1) * step)
        du = (slope[:, cols].astype(F32) * mm_nt(d1[...], sr[cols, :])).astype(BF)
        du_all[:, cols] = du
        part = mm_nt(du, sx[:, cols])
        dn = part if dn is None else dn + part
    up = d1[...].astype(F32)
    back, gain1, shift1 = norm_back(get(a0)[...], get(gains)[1:2], dn)
    da[...] = up + back
    lifts = jnp.sum(du_all[...].astype(F32), axis=0, keepdims=True)
    b3 = jnp.sum(up, axis=0, keepdims=True)
    small[...] += spread_blocks(lifts, 40, 2 * blocks) + columns_of([gain1, shift1, b3], [33, 35, 39])
    n1, act = get(n1), get(act)

    @pl.when(core == 0)
    def expand():
        for f in range(ff // step):
            deal(pay, mm_tn(n1[...], du_all[:, f * step : (f + 1) * step]), lane + f * step)

    @pl.when(core == 1)
    def reduce():
        deal_long(pay, mm_tn(act[...], d1[...]), lane)


def home_body(blocks, at, get, put, out, full, third, dc, do, dqkv, pay, d1, du_all):
    (mine, near, whole_own, partner, second, n3, routes, router, cot, dec, bias, gains, h_in, mw, m_m, n, q, k, v, o, lse) = range(21)
    decoded, da, small = out[0], out[1], out[2]
    s, image, core, tasks = at[:4]
    task = tasks[image]
    d = d1.shape[1]
    full[pl.ds(pl.multiple_of(core * HALF, 16), HALF), :] = get(mine)[...].astype(F32)
    full[pl.ds(pl.multiple_of((1 - core) * HALF, 16), HALF), :] = get(near)[...].astype(F32)
    full[...] += get(whole_own)[...].astype(F32) + get(partner)[...].astype(F32)
    stream = get(second)[...].astype(F32)
    third[...] = (stream + full[:, :d]).astype(BF)
    half = third[pl.ds(pl.multiple_of(core * HALF, 16), HALF), :]
    cot, dec, n3 = get(cot), get(dec), get(n3)
    decoded[...] = mm(half, dec[...]) + get(bias)[pl.ds(task, 1), :]
    put(0)
    hdec = cot.shape[1] // 2
    table = mm_tn(third[...], cot[:, pl.ds(pl.multiple_of(core * hdec, LANES), hdec)])
    deal(pay, jnp.where(task == 0, table, 0.0), 2 * d)
    deal(pay, jnp.where(task == 1, table, 0.0), 2 * d + hdec)

    ids = lax.broadcasted_iota(jnp.int32, (EXPERTS, PATCHES), 0)
    member = jnp.zeros((EXPERTS, PATCHES), F32)
    named = pick_routes(get(routes), image)
    for i in range(TOP):
        member = member + jnp.where(ids == named[i : i + 1, :], 1.0, 0.0)
    member = mm_tn(member.astype(BF), one_hot(EXPERTS, EXPERTS, [(i, i) for i in range(EXPERTS)]))
    table = get(router)
    logits = jnp.where(member > 0.0, mm_nt(n3[...], table[...]), -1e30)
    e = jnp.where(member > 0.0, jnp.exp(logits - jnp.max(logits, axis=1, keepdims=True)), 0.0)
    gates = e / jnp.sum(e, axis=1, keepdims=True)
    dots = full[:, 2 * d :]
    dots = dots[:, :EXPERTS] + dots[:, EXPERTS : 2 * EXPERTS]
    dz = gates * (dots - jnp.sum(gates * dots, axis=1, keepdims=True))
    high, low = split_low(dz)
    grad_router = mm_tn(high, n3[...]) + mm_tn(low, n3[...])
    dn = full[:, d : 2 * d] + mm(high, table[...]) + mm(low, table[...])
    gains = get(gains)
    back, gain1, shift1 = norm_back(stream, gains[1:2], dn)
    up = (mm_nt(cot[...], dec[...]).astype(BF).astype(F32) + back).astype(BF).astype(F32)
    later = lambda i: lambda: get(i)
    result, sums = attend_back_kernel(
        get(h_in)[...].astype(F32), gains[0:1], up, core, later(mw), later(m_m), later(n), later(q), later(k), later(v),
        later(o), later(lse), dc, do, dqkv, pay,
    )
    d1[...] = result.astype(BF)
    gain0, shift0, b0, b1, b2 = sums
    routed = columns_of([grad_router], list(range(EXPERTS)))
    small[...] = jnp.where(task == 0, routed, pltpu.roll(routed, EXPERTS, 1)) + columns_of(
        [gain0, gain1, shift0, shift1, b0, b1, b2], [16, 17, 18, 19, 20, 21, 22]
    )
    owners = jnp.sum(cot[...].astype(F32), axis=0, keepdims=True)
    count = cot.shape[1]
    column = columns_of([owners], [24])
    column = jnp.where(task == 0, column, pltpu.roll(column, 1, 1))
    r, some = d // blocks // 2, count // blocks // 2
    for b in range(2 * blocks):
        small[b * r : b * r + some, :] += column[b * some : (b + 1) * some]
    dense_part(blocks, at, lambda i: get(21 + i), d1, da, small, pay, du_all, 2 * d + count)
    put_halves(put, 3, pay, image)


def home(section, tasks, payload, second, n3, routes, router, cot, dec, bias, gains, first, mw, m_m, saved, dense, blocks):
    d = second.shape[1]
    width = cot.shape[1]
    inputs = [
        *payload, second, Near(n3), routes, (router, of_task, (EXPERTS, d)),
        (cot, rows_of(PATCHES), (PATCHES, width)),
        (dec, lambda s, image, core, tasks: (slice(None), pl.ds(pl.multiple_of(tasks[image] * width, LANES), width)),
         (d, width)),
        bias, gains, first, mw, m_m, *saved, *dense,
    ]
    ff = dense[2].shape[1]
    shape = light_shape(d, blocks, 2 * d + width + ff)
    half = (shape[1:], BF, None)
    outs = [((HALF, width), F32), ((PATCHES, d), F32, "near"), ((d, LANES), F32, "near"), half, half]
    scratch = [
        VMEM((PATCHES, 2 * d + LANES), F32), VMEM((PATCHES, d), BF), VMEM((PATCHES, d), BF), VMEM((PATCHES, d), BF),
        VMEM((PATCHES, 3 * d), BF), VMEM(shape, BF), VMEM((PATCHES, d), BF), VMEM((PATCHES, ff), BF),
    ]
    return call(functools.partial(home_body, blocks), section, tasks, inputs, outs, scratch, us=15.0)


def stem_back_body(at, get, put, out, full, dc, do, dqkv, pay):
    da, tok, gains, sw, sm, small_in, expert_in, n, q, k, v, o, lse = range(13)
    image, core = at[1], at[2]
    up = get(da)[...]
    d = up.shape[1]
    later = lambda i: lambda: get(i)
    result, sums = attend_back_kernel(
        get(tok)[...].astype(F32), get(gains)[0:1], up, core, later(sw), later(sm), later(n), later(q), later(k), later(v),
        later(o), later(lse), dc, do, dqkv, pay,
    )
    gain0, shift0, b0, b1, b2 = sums
    small = get(small_in)[...] + columns_of([gain0, shift0, b0, b1, b2], [32, 34, 36, 37, 38])
    deal(pay, jnp.where(core == 0, small, 0.0) + get(expert_in)[...], 2 * d)
    put_halves(put, 1, pay, image)
    full[...] = result
    put(0, full.at[pl.ds(pl.multiple_of(core * HALF, 8), HALF), :])


def stem_back(section, tasks, da, tokens, gains, sw, sm, small_in, expert_small, saved, blocks):
    d = da.shape[1]
    inputs = [Near(da), (tokens, rows_of(PATCHES), (PATCHES, d)), gains, sw, sm, Near(small_in), expert_small, *saved]
    shape = light_shape(d, blocks, 2 * d + LANES)
    half = (shape[1:], BF, None)
    outs = [((HALF, d), F32, None), half, half]
    scratch = [
        VMEM((PATCHES, d), F32), VMEM((PATCHES, d), BF), VMEM((PATCHES, d), BF), VMEM((PATCHES, 3 * d), BF),
        VMEM(shape, BF),
    ]
    return call(stem_back_body, section, tasks, inputs, outs, scratch, us=14.0)


def heavy_out_body(at, get, put, out, gathered):
    grad_in, grad_out = out
    s = at[0]
    r = grad_in.shape[0]
    d = grad_out.shape[2]
    for mask in range(4):
        for j in range(2):
            gathered[pl.ds(2 * jnp.bitwise_xor(s, mask) + j, 1)] = get(4 * j + mask)[...][None]
    for e in range(EXPERTS):
        value = gathered[e].astype(F32)
        grad_in[:, e, :] = value[:r]
        for k in range(4):
            grad_out[e, k * r : (k + 1) * r, :] = value[r:, k * d : (k + 1) * d]
    put(0)
    put(1)


def heavy_out(section, tasks, pieces, d):
    r2, ff = pieces[0].shape
    r = r2 // 2
    outs = [((r, EXPERTS, ff), F32), ((EXPERTS, 4 * r, d), F32)]
    return call(heavy_out_body, section, tasks, [Near(x) for x in pieces], outs, [VMEM((EXPERTS, r2, ff), BF)])


def light_out_body(d, dec, at, get, put, out, both):
    (mix_heads, mix_merge, dec_out, expand, reduce, stem_heads, stem_merge, router, lift, bias) = out[:10]
    elift, edrop = out[10:12]
    rows = out[12:]
    core = at[2]
    both[pl.ds(core, 1)] = get(0)[...][None]
    both[pl.ds(1 - core, 1)] = get(1)[...][None]
    r = expand.shape[0]
    m, ff, hdec = 2 * d + dec, expand.shape[1], dec // 2
    a, b = both[0].astype(F32), both[1].astype(F32)
    tiny = a[:, m + ff + 2 * d :]
    order = (32, 33, 34, 35, 36, 37, 38, 39, 16, 17, 18, 19, 20, 21, 22, 24, 25, 40, 41, 42, 43, 127, 127, 127)
    order = order + tuple(range(2 * EXPERTS))
    turned = mm_nt(one_hot(len(order), LANES, list(enumerate(order))), tiny.astype(BF))
    some = bias.shape[1]
    own = one_hot(5 * EXPERTS, LANES, [(i, 64 + i) for i in range(5 * EXPERTS)])
    by_core = [mm_nt(own, v[:, m + ff + 2 * d :].astype(BF)) for v in (a, b)]
    for c in range(2):

        @pl.when(core == c)
        def write():
            x, y = a[c * r : (c + 1) * r], b[c * r : (c + 1) * r]
            for heads, merge, base in ((mix_heads, mix_merge, 0), (stem_heads, stem_merge, m + ff)):
                heads[:, :d] = x[:, base : base + d]
                heads[:, d : 2 * d] = y[:, base : base + d]
                heads[:, 2 * d :] = x[:, base + d : base + 2 * d]
                merge[...] = y[:, base + d : base + 2 * d]
            for t in range(2):
                dec_out[:, t, :hdec] = x[:, 2 * d + t * hdec : 2 * d + (t + 1) * hdec]
                dec_out[:, t, hdec:] = y[:, 2 * d + t * hdec : 2 * d + (t + 1) * hdec]
                router[t] = turned[24 + t * EXPERTS : 24 + (t + 1) * EXPERTS, c * r : (c + 1) * r]
            expand[...] = x[:, m : m + ff]
            for k in range(2):
                at_lane = m + (2 * c + k) * d
                reduce[k * 2 * r : (k + 1) * 2 * r, :] = b[:, at_lane : at_lane + d]
            first = 0
            for part in rows:
                part[...] = turned[first : first + part.shape[0], c * r : (c + 1) * r]
                first += part.shape[0]
            bias[...] = turned[first : first + 2, c * some : (c + 1) * some]
            for e in range(EXPERTS):
                every = by_core[e // 2 % 2][5 * e : 5 * e + 5]
                elift[e : e + 1, :] = jnp.concatenate([every[2 * c : 2 * c + 1], every[2 * c + 1 : 2 * c + 2]], axis=1)
                edrop[e : e + 1, :] = every[4:5, c * r : (c + 1) * r]
            parts = [turned[first + 2 + 2 * c + k : first + 3 + 2 * c + k] for k in range(2)]
            lift[...] = jnp.concatenate(parts, axis=1)[0]

    for i in range(len(out)):
        put(i)


def light_out(section, tasks, mine, near, d, dec, ff, some):
    r2 = mine.shape[0]
    r = r2 // 2
    shapes = [
        (r, 3 * d), (r, d), (r, 2, dec), (r, ff), (4 * r, d), (r, 3 * d), (r, d), (2, EXPERTS, r), (2 * r2,), (2, some), (EXPERTS, 2 * r2),
        (EXPERTS, r),
        (2, r), (2, r), (4, r), (2, r), (2, r), (3, r),
    ]
    return call(
        functools.partial(light_out_body, d, dec), section, tasks, [Near(mine), Near(near)], [(x, F32) for x in shapes],
        [VMEM((2,) + mine.shape, BF)],
    )


def after(x, *others):
    return lax.optimization_barrier((x, *others))[0]


def swap(x, axis, mask):
    size = lax.axis_size(axis)
    return lax.ppermute(x, axis, [(i, i ^ mask) for i in range(size)])


def add_low(*terms):
    return sum(t.astype(F32) for t in terms).astype(BF)


def take(x, i):
    return lax.dynamic_index_in_dim(x, i, 0, keepdims=False)


def halve(terms, axis, mask):
    bit = (lax.axis_index(axis) // mask) % 2
    terms = [x.reshape((2, x.shape[0] // 2) + x.shape[1:]) for x in terms]
    send = add_low(*[take(t, 1 - bit) for t in terms])
    return [add_low(*[take(t, bit) for t in terms]), swap(send, axis, mask)], send


def body(
    tokens, routes, task_ids, cotangent, stem_gains, stem_shifts, stem_heads, stem_merge,
    stem_biases, stem_expand, stem_lift, stem_reduce, mix_gains, mix_shifts, mix_heads,
    mix_merge, mix_biases, router, expert_in, expert_lift, expert_out, expert_drop, decoder,
    decoder_bias,
):
    s = lax.axis_index("section")
    image = s // 2
    section = jnp.stack([s, lax.axis_index("dp")])
    ndp, ns = lax.axis_size("dp"), lax.axis_size("section")
    d, ff, dec = tokens.shape[1], stem_expand.shape[1], cotangent.shape[1]
    r, q = d // ndp, d // ndp // ns

    weights = [
        stem_heads, stem_gains, stem_shifts, stem_biases, stem_merge, stem_expand, stem_lift, stem_reduce, mix_heads,
        mix_gains, mix_shifts, mix_biases, mix_merge,
    ]
    (n0, q0, k0, v0, o0, l0, a0, n1, act, slope, first, n2, q2, k2, v2, o2, l2, second, n3) = forward(
        section, task_ids, tokens, weights
    )
    far = swap(n3, "section", 2)

    routes_t = routes.T
    router_t = router.transpose(1, 2, 0)
    dec_flat = decoder.reshape(d, -1)
    common = (routes_t, router_t, cotangent, dec_flat, (expert_in, expert_lift, expert_out, expert_drop))
    own_pay, *own = experts(True, section, task_ids, n3, *common)
    far = after(far, own_pay)
    own_got = swap(own_pay, "section", 1)
    far_send, far_keep, *away = experts(False, section, task_ids, far, *common)
    crossed = add_low(far_keep, swap(far_send, "section", 1))
    away[0] = after(away[0], crossed)
    crossed = swap(crossed, "section", 2)
    later_send, later_keep, sooner_send, sooner_keep, expert_small = weight_grads(section, task_ids, own, away, ndp)
    first_later, first_sooner = (expert_masks(e, ndp) for e in (1, 0))
    crossed = after(crossed, later_keep)
    later_got = swap(later_send, "dp", first_later[0])
    sooner_got = swap(sooner_send, "dp", first_sooner[0])
    payload = [Near(crossed), Near(swap(crossed, "section", 1)), own_pay, own_got]

    dense_saved = (stem_reduce, slope, stem_expand, a0, stem_gains, n1, act)
    decoded, da, small, wide_send, wide_keep = home(
        section, task_ids, payload, second, n3, routes_t, router_t, cotangent, dec_flat, decoder_bias,
        mix_gains, first, mix_heads, mix_merge, (n2, q2, k2, v2, o2, l2), dense_saved, ndp,
    )
    wide_got = swap(wide_send, "section", 2)
    later, later_sent = halve([later_keep, after(later_got, da)], "dp", first_later[1])
    sooner, sent = halve([sooner_keep, after(sooner_got, da)], "dp", first_sooner[1])
    da = after(da, sent, later_sent)
    d0, stem_send, stem_keep = stem_back(
        section, task_ids, da, tokens, stem_gains, stem_heads, stem_merge, small, expert_small, (n0, q0, k0, v0, o0, l0), ndp
    )
    stem_got = swap(stem_send, "section", 2)

    masks = near_first(ndp)
    join = lambda xs, ys: [jnp.concatenate([x, y], axis=-1) for x, y in zip(xs, ys)]
    later, later_sent = halve([later[0], after(later[1], d0)], "dp", first_later[2])
    wide, wide_sent = halve([wide_keep, after(wide_got, d0, later_sent)], "dp", 1)
    stem, stem_sent = halve([stem_keep, after(stem_got, wide_sent)], "dp", 1)
    later[1] = after(later[1], stem_sent)
    sooner, sooner_sent = halve([sooner[0], after(sooner[1], later[1])], "dp", first_sooner[2])
    wide, wide_sent = halve([wide[0], after(wide[1], sooner_sent)], "dp", 2)
    stem, stem_sent = halve([stem[0], after(stem[1], wide_sent)], "dp", 2)

    def pieces(terms, masks):
        for mask in masks:
            terms, unused = halve(terms, "dp", mask)
        x = add_low(*terms)[0]
        return [take(x, s)] + [swap(take(x, s ^ mask), "section", mask) for mask in (1, 2, 3)]

    later = pieces([later[0], after(later[1], stem_sent)], first_later[3:])
    light = join([wide[0], after(wide[1], stem_sent)], stem)
    for mask in masks[2:]:
        light, sent = halve(light, "dp", mask)
    sooner = pieces([sooner[0], after(sooner[1], sent)], first_sooner[3:])
    grad_in, grad_out = heavy_out(section, task_ids, sooner + later, d)
    light = add_low(light[0], after(light[1], grad_in))[0]
    light_near = swap(light, "section", 1)

    (
        g_mix_heads, g_mix_merge, g_dec, g_expand, g_reduce, g_stem_heads, g_stem_merge, g_router, g_lift, g_bias, g_elift, g_edrop,
        g_stem_gains, g_stem_shifts, g_stem_biases, g_mix_gains, g_mix_shifts, g_mix_biases,
    ) = light_out(section, task_ids, light, light_near, d, dec, ff, dec // ndp // ns)
    return (
        decoded, d0, g_stem_gains, g_stem_shifts, g_stem_heads, g_stem_merge, g_stem_biases, g_expand,
        g_lift, g_reduce, g_mix_gains, g_mix_shifts, g_mix_heads, g_mix_merge, g_mix_biases, g_router.transpose(2, 0, 1),
        grad_in.transpose(1, 0, 2), g_elift, grad_out, g_edrop, g_dec, g_bias,
    )


def solution(mesh):
    both = ("dp", "section")
    placed = (P("dp", None), P("dp", None), P("dp"), P("dp", None)) + (P(),) * 20
    rows, columns = P(both, None), P(None, both)
    return jax.shard_map(
        body,
        mesh=mesh,
        in_specs=placed,
        out_specs=(
            rows, rows, columns, columns, rows, rows, columns, rows, P(both), rows, columns,
            columns, rows, rows, columns, P(both, None, None), P(None, both, None), columns,
            P(None, both, None), columns, P(both, None, None), columns,
        ),
        check_vma=False,
    )
```

```python
import functools
import math

import jax
import jax.numpy as jnp
from jax import lax
from jax.experimental import pallas as pl
from jax.experimental.pallas import tpu as pltpu
from jax.sharding import PartitionSpec as P

HEADS = 6
HDIM = 64
EXPERTS = 8
TOP = 4
PATCHES = 576
HALF = PATCHES // 2
CAP = 288
LANES = 128
EPSILON = 1e-06
SCALE = 1.0 / math.sqrt(HDIM)
BF = jnp.bfloat16
F32 = jnp.float32
VMEM = pltpu.VMEM
MIB = 1 << 20


def mm(a, b):
    return jnp.dot(a, b, preferred_element_type=F32)


def mm_tn(a, b):
    return lax.dot_general(a, b, (((0,), (0,)), ((), ())), preferred_element_type=F32)


def mm_nt(a, b):
    return lax.dot_general(a, b, (((1,), (1,)), ((), ())), preferred_element_type=F32)


def split_low(v):
    high = v.astype(BF)
    return high, (v - high.astype(F32)).astype(BF)


def norm_parts(v):
    centred = v - jnp.mean(v, axis=-1, keepdims=True)
    inverse = lax.rsqrt(jnp.mean(centred * centred, axis=-1, keepdims=True) + EPSILON)
    return centred * inverse, inverse


def norm_back(v, gain, up):
    unit, inverse = norm_parts(v)
    scaled = up * gain
    back = inverse * (
        scaled
        - jnp.mean(scaled, axis=-1, keepdims=True)
        - unit * jnp.mean(scaled * unit, axis=-1, keepdims=True)
    )
    return back, jnp.sum(up * unit, axis=0, keepdims=True), jnp.sum(up, axis=0, keepdims=True)


def gelu_both(u):
    t = pl.reciprocal(1.0 + (0.3275911 / math.sqrt(2.0)) * jnp.abs(u), approx=True)
    bell = jnp.exp2((-0.5 / math.log(2.0)) * u * u)
    poly = 0.5 * 1.421413741 + t * (0.5 * -1.453152027 + t * (0.5 * 1.061405429))
    tail = bell * (t * (0.5 * 0.254829592 + t * (0.5 * -0.284496736 + t * poly)))
    cdf = jnp.where(u >= 0.0, 1.0 - tail, tail)
    return u * cdf, cdf + u * bell * (1.0 / math.sqrt(2.0 * math.pi))


def side_masks():
    lane = lax.broadcasted_iota(jnp.int32, (1, LANES), 1)
    left = (lane < HDIM).astype(F32)
    return left.astype(BF), (1.0 - left).astype(BF)


def lane_ids(rows=1):
    return lax.broadcasted_iota(jnp.int32, (rows, LANES), 1)


def near_first(blocks):
    return [1 << i for i in range(blocks.bit_length() - 1)]


def spot_of(block, masks):
    spot = 0
    for mask in masks:
        spot = 2 * spot + (block // mask) % 2
    return spot


def deal(pay, value, at):
    r, w = pay.shape[2], value.shape[1]
    for b in range(pay.shape[1]):
        spot = spot_of(b, near_first(pay.shape[1]))
        for y in range(2):
            piece = value[(2 * b + y) * r : (2 * b + y + 1) * r]
            pay[y, spot, :, at : at + w] = piece.astype(BF)


def deal_long(pay, value, at):
    r, w = pay.shape[2], value.shape[1]
    for b in range(pay.shape[1]):
        spot = spot_of(b, near_first(pay.shape[1]))
        for y in range(2):
            for k in range(4):
                piece = value[(8 * b + 4 * y + k) * r : (8 * b + 4 * y + k + 1) * r]
                pay[y, spot, :, at + k * w : at + (k + 1) * w] = piece.astype(BF)


def light_shape(d, blocks, width):
    return (2, blocks, d // blocks // 2, width)


def one_hot(rows, columns, hits):
    sub, lane = (lax.broadcasted_iota(jnp.int32, (rows, columns), i) for i in range(2))
    total = jnp.zeros((rows, columns), F32)
    for i, j in hits:
        total = total + jnp.where((sub == i) & (lane == j), 1.0, 0.0)
    return total.astype(BF)


def columns_of(rows, lanes):
    count = -(-len(lanes) // 8) * 8
    n = rows[0].shape[1]
    spare = [jnp.zeros((count - len(lanes), n), F32)] if count > len(lanes) else []
    stacked = jnp.concatenate(rows + spare, axis=0)
    place = lax.broadcasted_iota(jnp.int32, (count, LANES), 0)
    lane = lane_ids(count)
    spread = jnp.zeros((count, LANES), F32)
    for i, at in enumerate(lanes):
        spread = spread + jnp.where((place == i) & (lane == at), 1.0, 0.0)
    return mm_tn(stacked.astype(BF), spread.astype(BF))


def spread_blocks(row, first_lane, blocks):
    n = row.shape[1]
    r = n // 4 // blocks
    place = lax.broadcasted_iota(jnp.int32, (8, LANES), 0)
    stacked = jnp.concatenate([row, jnp.zeros((7, n), F32)], axis=0)
    column = mm_tn(stacked.astype(BF), jnp.where(place == 0, 1.0, 0.0).astype(BF))
    lane = lane_ids()
    parts = []
    for b in range(blocks):
        part = None
        for s in range(4):
            at = (4 * b + s) * r
            piece = jnp.where(lane == first_lane + s, column[at : at + r], 0.0)
            part = piece if part is None else part + piece
        parts.append(part)
    return jnp.concatenate(parts, axis=0)


class Near:
    def __init__(self, array):
        self.array = array


class Fetched:
    def __init__(self, moves):
        self.moves = moves
        for move in moves:
            move.start()

    def wait(self):
        for move in self.moves:
            move.wait()
        self.moves = []


def run_kernel(body, n_in, n_out, picks, near_out, *refs):
    section, tasks = refs[:2]
    inputs, outputs = refs[2 : 2 + n_in], refs[2 + n_in : 2 + n_in + n_out]
    rest = refs[2 + n_in + n_out :]
    kept_in, kept_out = rest[:n_in], rest[n_in : n_in + n_out]
    in_sems, out_sems = rest[n_in + n_out : n_in + n_out + 2]
    kept_out = [outputs[i] if i in near_out else kept_out[i] for i in range(n_out)]
    at = (section[0], section[0] // 2, section[0] % 2, tasks, section[1])
    fetched, moving = [], []
    for i in range(n_in):
        if picks[i] == "near":
            fetched.append(None)
            continue
        source = inputs[i] if picks[i] is None else inputs[i].at[picks[i](*at[:4])]
        fetched.append(Fetched([pltpu.make_async_copy(source, kept_in[i], in_sems.at[i])]))

    def get(i):
        if fetched[i] is None:
            return inputs[i]
        fetched[i].wait()
        return kept_in[i]

    def put(i, source=None, part=None):
        if i in near_out:
            return
        source = kept_out[i] if source is None else source
        target = outputs[i] if part is None else outputs[i].at[part]
        move = pltpu.make_async_copy(source, target, out_sems.at[i if part is None else i + part * n_out])
        move.start()
        moving.append(move)

    body(at, get, put, kept_out, *rest[n_in + n_out + 2 :])
    for i in range(n_in):
        get(i)
    for move in moving:
        move.wait()


def call(body, section, tasks, inputs, outs, scratch=(), us=3.0, limit=56):
    arrays, picks, kept = [], [], []
    for x in inputs:
        if isinstance(x, Near):
            arrays.append(x.array)
            picks.append("near")
            kept.append(VMEM((8, LANES), F32))
            continue
        array, pick, shape = x if isinstance(x, tuple) else (x, None, x.shape)
        arrays.append(array)
        picks.append(pick)
        kept.append(VMEM(shape, array.dtype))
    kept_out = [VMEM(o[0], o[1]) if len(o) == 2 else VMEM((8, LANES), F32) for o in outs]
    near_out = [i for i, o in enumerate(outs) if len(o) == 3 and o[2] == "near"]
    anywhere, scalar = pl.BlockSpec(memory_space=pl.ANY), pl.BlockSpec(memory_space=pltpu.SMEM)
    here = pl.BlockSpec(memory_space=pltpu.VMEM)
    return pl.pallas_call(
        functools.partial(run_kernel, body, len(arrays), len(outs), picks, near_out),
        out_shape=[jax.ShapeDtypeStruct(o[0], o[1]) for o in outs],
        in_specs=[scalar, scalar] + [here if p == "near" else anywhere for p in picks],
        out_specs=[here if i in near_out else anywhere for i in range(len(outs))],
        scratch_shapes=[
            *kept, *kept_out, pltpu.SemaphoreType.DMA((len(arrays),)), pltpu.SemaphoreType.DMA((2 * len(outs),)), *scratch
        ],
        compiler_params=pltpu.CompilerParams(vmem_limit_bytes=limit * MIB),
        cost_estimate=pl.CostEstimate(flops=int(us * 1.1e9), bytes_accessed=1, transcendentals=0),
    )(section, tasks, *arrays)


def rows_of(count):
    return lambda s, image, core, tasks: pl.ds(pl.multiple_of(image * count, count), count)


def of_task(s, image, core, tasks):
    return tasks[image]


def attend_kernel(h, gain, shift, get_w, c, get_m, n_ref, q_ref, k_ref, v_ref, o_ref, lse_ref, done):
    d = h.shape[1]
    unit, unused = norm_parts(h)
    n_ref[...] = (unit * gain + shift).astype(BF)
    done(0)
    n, w = n_ref[...], get_w()
    q_ref[...] = ((mm(n, w[:, :d]) + c[0:1]) * SCALE).astype(BF)
    done(1)
    k_ref[...] = mm(n, w[:, d : 2 * d]).astype(BF)
    done(2)
    v_ref[...] = (mm(n, w[:, 2 * d :]) + c[1:2]).astype(BF)
    done(3)
    masks = side_masks()
    lane = lane_ids()
    sums = jnp.zeros((PATCHES, LANES), F32)
    step = 32
    for p in range(d // LANES):
        at = slice(p * LANES, (p + 1) * LANES)
        total = None
        for i, mask in enumerate(masks):
            scores = mm_nt(q_ref[:, at] * mask, k_ref[:, at])
            e, norm, top = [], [], []
            for r in range(PATCHES // step):
                part = scores[r * step : (r + 1) * step]
                most = jnp.max(part, axis=-1, keepdims=True)
                part = jnp.exp(part - most)
                e.append(part.astype(BF))
                norm.append(jnp.sum(part, axis=-1, keepdims=True))
                top.append(most)
            norm = jnp.concatenate(norm, axis=0)
            part = mm(jnp.concatenate(e, axis=0), v_ref[:, at] * mask) * (1.0 / norm)
            total = part if total is None else total + part
            sums = jnp.where(lane == 2 * p + i, jnp.concatenate(top, axis=0) + jnp.log(norm), sums)
        o_ref[:, at] = total.astype(BF)
    lse_ref[...] = sums
    done(4)
    done(5)
    return h + (mm(o_ref[...], get_m()[...]) + c[2:3])


def forward_body(at, get, put, out, *scratch):
    tok, sw, sg, ss, sb, sm, sx, sl, sr, mw, mg, ms, mb, m_m = range(14)
    (n0, q0, k0, v0, o0, l0, a0, n1, act, slope, first, n2, q2, k2, v2, o2, l2, second, n3) = out
    h = get(tok)[...].astype(F32)
    sg, ss, sb = get(sg), get(ss), get(sb)
    a = attend_kernel(
        h, sg[0:1], ss[0:1], lambda: get(sw), sb, lambda: get(sm), n0, q0, k0, v0, o0, l0, put
    )
    a0[...] = a
    put(6)
    unit, unused = norm_parts(a0[...])
    n1[...] = (unit * sg[1:2] + ss[1:2]).astype(BF)
    put(7)
    step = 1536
    wx, lift = get(sx), get(sl)
    for f in range(wx.shape[1] // step):
        cols = slice(f * step, (f + 1) * step)
        active, bend = gelu_both(mm(n1[...], wx[:, cols]) + lift[cols][None, :])
        act[:, cols] = active.astype(BF)
        slope[:, cols] = bend.astype(BF)
    put(8)
    put(9)
    first[...] = (a0[...] + (mm(act[...], get(sr)[...]) + sb[3:4])).astype(BF)
    put(10)
    mg, ms, mb = get(mg), get(ms), get(mb)
    second[...] = attend_kernel(
        first[...].astype(F32), mg[0:1], ms[0:1], lambda: get(mw), mb, lambda: get(m_m), n2, q2, k2, v2,
        o2, l2, lambda i: put(11 + i),
    ).astype(BF)
    put(17)
    unit, unused = norm_parts(second[...].astype(F32))
    n3[...] = (unit * mg[1:2] + ms[1:2]).astype(BF)


def forward(section, tasks, tokens, weights):
    d = tokens.shape[1]
    ff = weights[5].shape[1]
    wide = ((PATCHES, d), BF)
    sums = ((PATCHES, LANES), F32)
    outs = [wide] * 5 + [sums, ((PATCHES, d), F32), wide, ((PATCHES, ff), BF), ((PATCHES, ff), BF)]
    outs += [wide] * 6 + [sums, wide, wide + ("near",)]
    inputs = [(tokens, rows_of(PATCHES), (PATCHES, d)), *weights]
    return call(forward_body, section, tasks, inputs, outs, us=20.0)


def pick_routes(ref, image):
    every = ref[...]
    chosen = every[:, :PATCHES]
    for i in range(1, every.shape[1] // PATCHES):
        chosen = jnp.where(image == i, every[:, i * PATCHES : (i + 1) * PATCHES], chosen)
    return chosen


def experts_body(own, at, get, put, out, gates, place, d3):
    n, routes, router, cot, dec, w_in0, w_in1, lift, w_out0, w_out1, drop = range(11)
    core = at[2]
    if own:
        full, xs, dys, acts, dus = out
        first = 1
    else:
        send, keep, xs, dys, acts, dus, full = out
        first = 2
    n_ref = get(n)
    ids = lax.broadcasted_iota(jnp.int32, (EXPERTS, PATCHES), 0)
    member = jnp.zeros((EXPERTS, PATCHES), F32)
    named = pick_routes(get(routes), at[1] if own else 1 - at[1])
    for k in range(TOP):
        member = member + jnp.where(ids == named[k : k + 1, :], 1.0, 0.0)
    logits = jnp.where(member > 0.0, mm_nt(get(router)[...], n_ref[...]), -1e30)
    e = jnp.where(member > 0.0, jnp.exp(logits - jnp.max(logits, axis=0, keepdims=True)), 0.0)
    gates[...] = e / jnp.sum(e, axis=0, keepdims=True)
    before = lax.broadcasted_iota(jnp.int32, (PATCHES, PATCHES), 0)
    after_ = lax.broadcasted_iota(jnp.int32, (PATCHES, PATCHES), 1)
    upper = jnp.where(before <= after_, 1.0, 0.0).astype(BF)
    place[...] = jnp.where(member > 0.0, mm(member.astype(BF), upper) - 1.0, -1.0)
    d3[...] = mm_nt(get(cot)[...], get(dec)[...]).astype(BF)
    total = None
    lifts, drops = get(lift), get(drop)
    for j in range(2):
        e = 2 * at[0] + j
        spot = place[pl.ds(e, 1), :].astype(jnp.int32)
        hit = lax.broadcasted_iota(jnp.int32, (CAP, PATCHES), 0) == spot
        pick = jnp.where(hit, 1.0, 0.0)
        weight = jnp.sum(pick * gates[pl.ds(e, 1), :], axis=1, keepdims=True)
        pick = pick.astype(BF)
        x = mm(pick, n_ref[...]).astype(BF)
        up = mm(pick, d3[...])
        dy = (weight * up).astype(BF)
        xs[j] = x
        dys[j] = dy
        w_in, w_out = get((w_in0, w_in1)[j]), get((w_out0, w_out1)[j])
        ff = w_in.shape[1]
        step = 1536
        y = drops[pl.ds(e, 1), :]
        dx = None
        for f in range(ff // step):
            cols = slice(f * step, (f + 1) * step)
            active, bend = gelu_both(mm(x, w_in[:, cols]) + lifts[pl.ds(e, 1), cols])
            active = active.astype(BF)
            du = (bend * mm_nt(dy, w_out[cols, :])).astype(BF)
            y = y + mm(active, w_out[cols, :])
            part = mm_nt(du, w_in[:, cols])
            dx = part if dx is None else dx + part
            acts[j, :, cols] = active
            dus[j, :, cols] = du
        for i, kept in enumerate((xs, dys, acts, dus)):
            put(first + i, kept.at[j], j)
        dots = jnp.sum(y * up, axis=1, keepdims=True)
        high = dots.astype(BF).astype(F32)
        lane = lane_ids()
        marks = jnp.where(lane == e, high, jnp.where(lane == e + EXPERTS, dots - high, 0.0))
        rhs = jnp.concatenate([(weight * y).astype(BF), dx.astype(BF), marks.astype(BF)], axis=1)
        home = mm_tn(pick, rhs)
        total = home if total is None else total + home
    full[...] = total.astype(BF)
    if not own:
        send[...] = full[pl.ds(pl.multiple_of((1 - core) * HALF, 16), HALF), :]
        keep[...] = full[pl.ds(pl.multiple_of(core * HALF, 16), HALF), :]


def experts(own, section, tasks, n, routes_t, router_t, cot, dec, weights):
    expert_in, expert_lift, expert_out, expert_drop = weights
    d, ff = expert_in.shape[1:]
    width = 2 * d + LANES
    look = (lambda image: image) if own else (lambda image: 1 - image)
    which = lambda j: lambda s, image, core, tasks: 2 * s + j
    inputs = [
        Near(n),
        routes_t,
        (router_t, lambda s, image, core, tasks: tasks[look(image)], (EXPERTS, d)),
        (cot, lambda s, image, core, tasks: pl.ds(pl.multiple_of(look(image) * PATCHES, PATCHES), PATCHES),
         (PATCHES, cot.shape[1])),
        (dec, lambda s, image, core, tasks: (
            slice(None), pl.ds(pl.multiple_of(tasks[look(image)] * cot.shape[1], LANES), cot.shape[1])),
         (d, cot.shape[1])),
        (expert_in, which(0), (d, ff)), (expert_in, which(1), (d, ff)), expert_lift,
        (expert_out, which(0), (ff, d)), (expert_out, which(1), (ff, d)), expert_drop,
    ]
    half = ((HALF, width), BF, "near")
    outs = [((PATCHES, width), BF, "near")] if own else [half, half]
    outs += [((2, CAP, d), BF), ((2, CAP, d), BF), ((2, CAP, ff), BF), ((2, CAP, ff), BF)]
    scratch = [] if own else [VMEM((PATCHES, width), BF)]
    scratch += [
        VMEM((EXPERTS, PATCHES), F32), VMEM((EXPERTS, PATCHES), F32),
        VMEM((PATCHES, d), BF),
    ]

    def body(at, get, put, out, *rest):
        if own:
            experts_body(own, at, get, put, out, *rest)
        else:
            experts_body(own, at, get, put, [*out, rest[0]], *rest[1:])

    return call(body, section, tasks, inputs, outs, scratch, us=13.0)


def expert_masks(expert, blocks):
    masks = near_first(blocks)
    return masks if expert == 1 else [masks[1], masks[0], *masks[2:]]


def weight_grads(section, tasks, own, far, blocks):
    d, ff = own[0].shape[2], own[2].shape[2]
    r = d // blocks // 4
    part = lambda x, e: (x, lambda s, image, core, tasks: e, x.shape[1:])
    inputs = [part(x, e) for e in (1, 0) for pair in zip(own, far) for x in pair]
    shape = (2, blocks // 2, 4, 2 * r, ff)

    def body(at, get, put, out, *pays):
        small = out[4]
        for place, e in enumerate((1, 0)):
            pay, masks = pays[place], expert_masks(e, blocks)
            both = lambda i: jnp.concatenate([get(8 * place + 2 * i)[...], get(8 * place + 2 * i + 1)[...]], axis=0)
            x, du = both(0), both(3)
            step = 1536
            grad_in = [mm_tn(x, du[:, f * step : (f + 1) * step]) for f in range(ff // step)]
            lifts = jnp.sum(du.astype(F32), axis=0, keepdims=True)
            dy = both(1)
            drops = jnp.sum(dy.astype(F32), axis=0, keepdims=True)
            tiny = spread_blocks(lifts, 5 * e, 2 * blocks) + columns_of([drops], [5 * e + 4])
            small[...] = tiny if place == 0 else small[...] + tiny
            grad_out = mm_tn(both(2), dy)
            for b in range(blocks):
                i, j = divmod(spot_of(b, masks), blocks // 2)
                for t in range(4):
                    row = (4 * b + t) * r
                    for f, value in enumerate(grad_in):
                        pay[i, j, t, :r, f * step : (f + 1) * step] = value[row : row + r].astype(BF)
                    for k in range(4):
                        at_row = (4 * (4 * b + t) + k) * r
                        pay[i, j, t, r:, k * d : (k + 1) * d] = grad_out[at_row : at_row + r].astype(BF)
            bit = (at[4] // masks[0]) % 2
            put(2 * place, pay.at[1 - bit])
            put(2 * place + 1, pay.at[bit])
        moved = small[...]
        for s in range(4):
            moved = jnp.where(at[0] == s, pltpu.roll(small[...], 64 + 10 * s, 1), moved)
        small[...] = moved
        put(4)

    half = (shape[1:], BF, None)
    outs = [half] * 4 + [((d, LANES), F32)]
    return call(body, section, tasks, inputs, outs, [VMEM(shape, BF)] * 2, us=14.0)


def exact_rows(columns):
    sub = lax.broadcasted_iota(jnp.int32, (8, LANES), 0)
    eye = jnp.where(sub == lax.broadcasted_iota(jnp.int32, (8, LANES), 1), 1.0, 0.0).astype(BF)
    high, rest = split_low(columns)
    middle, low = split_low(columns - high.astype(F32))
    del rest
    return mm_nt(eye, high) + mm_nt(eye, middle) + mm_nt(eye, low)


def attend_back_kernel(h, gain, up, core, get_w, get_m, n, q, k, v, o, lse, dc_ref, do_ref, dqkv, pay):
    d = h.shape[1]
    dc_ref[...] = up.astype(BF)
    do_ref[...] = mm_nt(dc_ref[...], get_m()[...]).astype(BF)
    q, k, v, o = q(), k(), v(), o()
    masks = side_masks()
    sums = exact_rows(lse()[...])
    sub, lane = (lax.broadcasted_iota(jnp.int32, (8, d), i) for i in range(2))
    heads = jnp.where(lane // HDIM == sub, 1.0, 0.0).astype(BF)
    high, low = split_low(o[...].astype(F32) * do_ref[...].astype(F32))
    delta = mm_nt(heads, high) + mm_nt(heads, low)
    step = 64
    for p in range(d // LANES):
        at = slice(p * LANES, (p + 1) * LANES)
        dq = dk = dv = None
        for i, mask in enumerate(masks):
            head = 2 * p + i
            scores = mm_nt(k[:, at] * mask, q[:, at])
            dp = mm_nt(v[:, at] * mask, do_ref[:, at])
            probs, ds = [], []
            for r in range(PATCHES // step):
                rows = slice(r * step, (r + 1) * step)
                part = jnp.exp(scores[rows] - sums[head : head + 1])
                probs.append(part.astype(BF))
                ds.append((part * (dp[rows] - delta[head : head + 1])).astype(BF))
            ds = jnp.concatenate(ds, axis=0)
            part = mm(jnp.concatenate(probs, axis=0), do_ref[:, at] * mask)
            dv = part if dv is None else dv + part
            part = mm(ds, q[:, at] * mask)
            dk = part if dk is None else dk + part
            part = mm_tn(ds, k[:, at] * mask * SCALE)
            dq = part if dq is None else dq + part
        dqkv[:, at] = dq.astype(BF)
        dqkv[:, d + p * LANES : d + (p + 1) * LANES] = dk.astype(BF)
        dqkv[:, 2 * d + p * LANES : 2 * d + (p + 1) * LANES] = dv.astype(BF)
    rows = [
        jnp.sum(dqkv[:, :d].astype(F32), axis=0, keepdims=True),
        jnp.sum(dqkv[:, 2 * d :].astype(F32), axis=0, keepdims=True),
        jnp.sum(dc_ref[...].astype(F32), axis=0, keepdims=True),
    ]
    back, grad_gain, grad_shift = norm_back(h, gain, mm_nt(dqkv[...], get_w()[...]))
    n = n()

    @pl.when(core == 0)
    def queries():
        deal(pay, mm_tn(n[...], dqkv[:, :d]), 0)
        deal(pay, mm_tn(n[...], dqkv[:, 2 * d :]), d)

    @pl.when(core == 1)
    def keys_and_merge():
        deal(pay, mm_tn(n[...], dqkv[:, d : 2 * d]), 0)
        deal(pay, mm_tn(o[...], dc_ref[...]), d)

    return up + back, [grad_gain, grad_shift] + rows


def put_halves(put, first, pay, image):
    put(first, pay.at[1 - image])
    put(first + 1, pay.at[image])


def dense_part(blocks, at, get, d1, da, small, pay, du_all, lane):
    sr, slope, sx, a0, gains, n1, act = range(7)
    core = at[2]
    sr, slope, sx = get(sr), get(slope), get(sx)
    d, ff = sx.shape
    step = 1536
    dn = None
    for f in range(ff // step):
        cols = slice(f * step, (f + 1) * step)
        du = (slope[:, cols].astype(F32) * mm_nt(d1[...], sr[cols, :])).astype(BF)
        du_all[:, cols] = du
        part = mm_nt(du, sx[:, cols])
        dn = part if dn is None else dn + part
    up = d1[...].astype(F32)
    back, gain1, shift1 = norm_back(get(a0)[...], get(gains)[1:2], dn)
    da[...] = up + back
    lifts = jnp.sum(du_all[...].astype(F32), axis=0, keepdims=True)
    b3 = jnp.sum(up, axis=0, keepdims=True)
    small[...] += spread_blocks(lifts, 40, 2 * blocks) + columns_of([gain1, shift1, b3], [33, 35, 39])
    n1, act = get(n1), get(act)

    @pl.when(core == 0)
    def expand():
        for f in range(ff // step):
            deal(pay, mm_tn(n1[...], du_all[:, f * step : (f + 1) * step]), lane + f * step)

    @pl.when(core == 1)
    def reduce():
        deal_long(pay, mm_tn(act[...], d1[...]), lane)


def home_body(blocks, at, get, put, out, full, third, dc, do, dqkv, pay, d1, du_all):
    (mine, near, whole_own, partner, second, n3, routes, router, cot, dec, bias, gains, h_in, mw, m_m, n, q, k, v, o, lse) = range(21)
    decoded, da, small = out[0], out[1], out[2]
    s, image, core, tasks = at[:4]
    task = tasks[image]
    d = d1.shape[1]
    full[pl.ds(pl.multiple_of(core * HALF, 16), HALF), :] = get(mine)[...].astype(F32)
    full[pl.ds(pl.multiple_of((1 - core) * HALF, 16), HALF), :] = get(near)[...].astype(F32)
    full[...] += get(whole_own)[...].astype(F32) + get(partner)[...].astype(F32)
    stream = get(second)[...].astype(F32)
    third[...] = (stream + full[:, :d]).astype(BF)
    half = third[pl.ds(pl.multiple_of(core * HALF, 16), HALF), :]
    cot, dec, n3 = get(cot), get(dec), get(n3)
    decoded[...] = mm(half, dec[...]) + get(bias)[pl.ds(task, 1), :]
    put(0)
    hdec = cot.shape[1] // 2
    table = mm_tn(third[...], cot[:, pl.ds(pl.multiple_of(core * hdec, LANES), hdec)])
    deal(pay, jnp.where(task == 0, table, 0.0), 2 * d)
    deal(pay, jnp.where(task == 1, table, 0.0), 2 * d + hdec)

    ids = lax.broadcasted_iota(jnp.int32, (EXPERTS, PATCHES), 0)
    member = jnp.zeros((EXPERTS, PATCHES), F32)
    named = pick_routes(get(routes), image)
    for i in range(TOP):
        member = member + jnp.where(ids == named[i : i + 1, :], 1.0, 0.0)
    member = mm_tn(member.astype(BF), one_hot(EXPERTS, EXPERTS, [(i, i) for i in range(EXPERTS)]))
    table = get(router)
    logits = jnp.where(member > 0.0, mm_nt(n3[...], table[...]), -1e30)
    e = jnp.where(member > 0.0, jnp.exp(logits - jnp.max(logits, axis=1, keepdims=True)), 0.0)
    gates = e / jnp.sum(e, axis=1, keepdims=True)
    dots = full[:, 2 * d :]
    dots = dots[:, :EXPERTS] + dots[:, EXPERTS : 2 * EXPERTS]
    dz = gates * (dots - jnp.sum(gates * dots, axis=1, keepdims=True))
    high, low = split_low(dz)
    grad_router = mm_tn(high, n3[...]) + mm_tn(low, n3[...])
    dn = full[:, d : 2 * d] + mm(high, table[...]) + mm(low, table[...])
    gains = get(gains)
    back, gain1, shift1 = norm_back(stream, gains[1:2], dn)
    up = (mm_nt(cot[...], dec[...]).astype(BF).astype(F32) + back).astype(BF).astype(F32)
    later = lambda i: lambda: get(i)
    result, sums = attend_back_kernel(
        get(h_in)[...].astype(F32), gains[0:1], up, core, later(mw), later(m_m), later(n), later(q), later(k), later(v),
        later(o), later(lse), dc, do, dqkv, pay,
    )
    d1[...] = result.astype(BF)
    gain0, shift0, b0, b1, b2 = sums
    routed = columns_of([grad_router], list(range(EXPERTS)))
    small[...] = jnp.where(task == 0, routed, pltpu.roll(routed, EXPERTS, 1)) + columns_of(
        [gain0, gain1, shift0, shift1, b0, b1, b2], [16, 17, 18, 19, 20, 21, 22]
    )
    owners = jnp.sum(cot[...].astype(F32), axis=0, keepdims=True)
    count = cot.shape[1]
    column = columns_of([owners], [24])
    column = jnp.where(task == 0, column, pltpu.roll(column, 1, 1))
    r, some = d // blocks // 2, count // blocks // 2
    for b in range(2 * blocks):
        small[b * r : b * r + some, :] += column[b * some : (b + 1) * some]
    dense_part(blocks, at, lambda i: get(21 + i), d1, da, small, pay, du_all, 2 * d + count)
    put_halves(put, 3, pay, image)


def home(section, tasks, payload, second, n3, routes, router, cot, dec, bias, gains, first, mw, m_m, saved, dense, blocks):
    d = second.shape[1]
    width = cot.shape[1]
    inputs = [
        *payload, second, Near(n3), routes, (router, of_task, (EXPERTS, d)),
        (cot, rows_of(PATCHES), (PATCHES, width)),
        (dec, lambda s, image, core, tasks: (slice(None), pl.ds(pl.multiple_of(tasks[image] * width, LANES), width)),
         (d, width)),
        bias, gains, first, mw, m_m, *saved, *dense,
    ]
    ff = dense[2].shape[1]
    shape = light_shape(d, blocks, 2 * d + width + ff)
    half = (shape[1:], BF, None)
    outs = [((HALF, width), F32), ((PATCHES, d), F32, "near"), ((d, LANES), F32, "near"), half, half]
    scratch = [
        VMEM((PATCHES, 2 * d + LANES), F32), VMEM((PATCHES, d), BF), VMEM((PATCHES, d), BF), VMEM((PATCHES, d), BF),
        VMEM((PATCHES, 3 * d), BF), VMEM(shape, BF), VMEM((PATCHES, d), BF), VMEM((PATCHES, ff), BF),
    ]
    return call(functools.partial(home_body, blocks), section, tasks, inputs, outs, scratch, us=15.0)


def stem_back_body(at, get, put, out, full, dc, do, dqkv, pay):
    da, tok, gains, sw, sm, small_in, expert_in, n, q, k, v, o, lse = range(13)
    image, core = at[1], at[2]
    up = get(da)[...]
    d = up.shape[1]
    later = lambda i: lambda: get(i)
    result, sums = attend_back_kernel(
        get(tok)[...].astype(F32), get(gains)[0:1], up, core, later(sw), later(sm), later(n), later(q), later(k), later(v),
        later(o), later(lse), dc, do, dqkv, pay,
    )
    gain0, shift0, b0, b1, b2 = sums
    small = get(small_in)[...] + columns_of([gain0, shift0, b0, b1, b2], [32, 34, 36, 37, 38])
    deal(pay, jnp.where(core == 0, small, 0.0) + get(expert_in)[...], 2 * d)
    put_halves(put, 1, pay, image)
    full[...] = result
    put(0, full.at[pl.ds(pl.multiple_of(core * HALF, 8), HALF), :])


def stem_back(section, tasks, da, tokens, gains, sw, sm, small_in, expert_small, saved, blocks):
    d = da.shape[1]
    inputs = [Near(da), (tokens, rows_of(PATCHES), (PATCHES, d)), gains, sw, sm, Near(small_in), expert_small, *saved]
    shape = light_shape(d, blocks, 2 * d + LANES)
    half = (shape[1:], BF, None)
    outs = [((HALF, d), F32, None), half, half]
    scratch = [
        VMEM((PATCHES, d), F32), VMEM((PATCHES, d), BF), VMEM((PATCHES, d), BF), VMEM((PATCHES, 3 * d), BF),
        VMEM(shape, BF),
    ]
    return call(stem_back_body, section, tasks, inputs, outs, scratch, us=14.0)


def heavy_out_body(at, get, put, out, gathered):
    grad_in, grad_out = out
    s = at[0]
    r = grad_in.shape[0]
    d = grad_out.shape[2]
    for mask in range(4):
        for j in range(2):
            gathered[pl.ds(2 * jnp.bitwise_xor(s, mask) + j, 1)] = get(4 * j + mask)[...][None]
    for e in range(EXPERTS):
        value = gathered[e].astype(F32)
        grad_in[:, e, :] = value[:r]
        for k in range(4):
            grad_out[e, k * r : (k + 1) * r, :] = value[r:, k * d : (k + 1) * d]
    put(0)
    put(1)


def heavy_out(section, tasks, pieces, d):
    r2, ff = pieces[0].shape
    r = r2 // 2
    outs = [((r, EXPERTS, ff), F32), ((EXPERTS, 4 * r, d), F32)]
    return call(heavy_out_body, section, tasks, [Near(x) for x in pieces], outs, [VMEM((EXPERTS, r2, ff), BF)], us=0.2)


def light_out_body(d, dec, at, get, put, out, both):
    (mix_heads, mix_merge, dec_out, expand, reduce, stem_heads, stem_merge, router, lift, bias) = out[:10]
    elift, edrop = out[10:12]
    rows = out[12:]
    core = at[2]
    both[pl.ds(core, 1)] = get(0)[...][None]
    both[pl.ds(1 - core, 1)] = get(1)[...][None]
    r = expand.shape[0]
    m, ff, hdec = 2 * d + dec, expand.shape[1], dec // 2
    a, b = both[0].astype(F32), both[1].astype(F32)
    tiny = a[:, m + ff + 2 * d :]
    order = (32, 33, 34, 35, 36, 37, 38, 39, 16, 17, 18, 19, 20, 21, 22, 24, 25, 40, 41, 42, 43, 127, 127, 127)
    order = order + tuple(range(2 * EXPERTS))
    turned = mm_nt(one_hot(len(order), LANES, list(enumerate(order))), tiny.astype(BF))
    some = bias.shape[1]
    own = one_hot(5 * EXPERTS, LANES, [(i, 64 + i) for i in range(5 * EXPERTS)])
    by_core = [mm_nt(own, v[:, m + ff + 2 * d :].astype(BF)) for v in (a, b)]
    for c in range(2):

        @pl.when(core == c)
        def write():
            x, y = a[c * r : (c + 1) * r], b[c * r : (c + 1) * r]
            for heads, merge, base in ((mix_heads, mix_merge, 0), (stem_heads, stem_merge, m + ff)):
                heads[:, :d] = x[:, base : base + d]
                heads[:, d : 2 * d] = y[:, base : base + d]
                heads[:, 2 * d :] = x[:, base + d : base + 2 * d]
                merge[...] = y[:, base + d : base + 2 * d]
            for t in range(2):
                dec_out[:, t, :hdec] = x[:, 2 * d + t * hdec : 2 * d + (t + 1) * hdec]
                dec_out[:, t, hdec:] = y[:, 2 * d + t * hdec : 2 * d + (t + 1) * hdec]
                router[t] = turned[24 + t * EXPERTS : 24 + (t + 1) * EXPERTS, c * r : (c + 1) * r]
            expand[...] = x[:, m : m + ff]
            for k in range(2):
                at_lane = m + (2 * c + k) * d
                reduce[k * 2 * r : (k + 1) * 2 * r, :] = b[:, at_lane : at_lane + d]
            first = 0
            for part in rows:
                part[...] = turned[first : first + part.shape[0], c * r : (c + 1) * r]
                first += part.shape[0]
            bias[...] = turned[first : first + 2, c * some : (c + 1) * some]
            for e in range(EXPERTS):
                every = by_core[e // 2 % 2][5 * e : 5 * e + 5]
                elift[e : e + 1, :] = jnp.concatenate([every[2 * c : 2 * c + 1], every[2 * c + 1 : 2 * c + 2]], axis=1)
                edrop[e : e + 1, :] = every[4:5, c * r : (c + 1) * r]
            parts = [turned[first + 2 + 2 * c + k : first + 3 + 2 * c + k] for k in range(2)]
            lift[...] = jnp.concatenate(parts, axis=1)[0]

    for i in range(len(out)):
        put(i)


def light_out(section, tasks, mine, near, d, dec, ff, some):
    r2 = mine.shape[0]
    r = r2 // 2
    shapes = [
        (r, 3 * d), (r, d), (r, 2, dec), (r, ff), (4 * r, d), (r, 3 * d), (r, d), (2, EXPERTS, r), (2 * r2,), (2, some), (EXPERTS, 2 * r2),
        (EXPERTS, r),
        (2, r), (2, r), (4, r), (2, r), (2, r), (3, r),
    ]
    return call(
        functools.partial(light_out_body, d, dec), section, tasks, [Near(mine), Near(near)], [(x, F32) for x in shapes],
        [VMEM((2,) + mine.shape, BF)],
    )


def after(x, *others):
    return lax.optimization_barrier((x, *others))[0]


def swap(x, axis, mask):
    size = lax.axis_size(axis)
    return lax.ppermute(x, axis, [(i, i ^ mask) for i in range(size)])


def add_low(*terms):
    return sum(t.astype(F32) for t in terms).astype(BF)


def take(x, i):
    return lax.dynamic_index_in_dim(x, i, 0, keepdims=False)


def halve(terms, axis, mask):
    bit = (lax.axis_index(axis) // mask) % 2
    terms = [x.reshape((2, x.shape[0] // 2) + x.shape[1:]) for x in terms]
    send = add_low(*[take(t, 1 - bit) for t in terms])
    return [add_low(*[take(t, bit) for t in terms]), swap(send, axis, mask)], send


def body(
    tokens, routes, task_ids, cotangent, stem_gains, stem_shifts, stem_heads, stem_merge,
    stem_biases, stem_expand, stem_lift, stem_reduce, mix_gains, mix_shifts, mix_heads,
    mix_merge, mix_biases, router, expert_in, expert_lift, expert_out, expert_drop, decoder,
    decoder_bias,
):
    s = lax.axis_index("section")
    image = s // 2
    section = jnp.stack([s, lax.axis_index("dp")])
    ndp, ns = lax.axis_size("dp"), lax.axis_size("section")
    d, ff, dec = tokens.shape[1], stem_expand.shape[1], cotangent.shape[1]
    r, q = d // ndp, d // ndp // ns

    weights = [
        stem_heads, stem_gains, stem_shifts, stem_biases, stem_merge, stem_expand, stem_lift, stem_reduce, mix_heads,
        mix_gains, mix_shifts, mix_biases, mix_merge,
    ]
    (n0, q0, k0, v0, o0, l0, a0, n1, act, slope, first, n2, q2, k2, v2, o2, l2, second, n3) = forward(
        section, task_ids, tokens, weights
    )
    far = swap(n3, "section", 2)

    routes_t = routes.T
    router_t = router.transpose(1, 2, 0)
    dec_flat = decoder.reshape(d, -1)
    common = (routes_t, router_t, cotangent, dec_flat, (expert_in, expert_lift, expert_out, expert_drop))
    own_pay, *own = experts(True, section, task_ids, n3, *common)
    far = after(far, own_pay)
    own_got = swap(own_pay, "section", 1)
    far_send, far_keep, *away = experts(False, section, task_ids, far, *common)
    crossed = add_low(far_keep, swap(far_send, "section", 1))
    away[0] = after(away[0], crossed)
    crossed = swap(crossed, "section", 2)
    later_send, later_keep, sooner_send, sooner_keep, expert_small = weight_grads(section, task_ids, own, away, ndp)
    first_later, first_sooner = (expert_masks(e, ndp) for e in (1, 0))
    crossed = after(crossed, later_keep)
    later_got = swap(later_send, "dp", first_later[0])
    sooner_got = swap(sooner_send, "dp", first_sooner[0])
    payload = [Near(crossed), Near(swap(crossed, "section", 1)), own_pay, own_got]

    dense_saved = (stem_reduce, slope, stem_expand, a0, stem_gains, n1, act)
    decoded, da, small, wide_send, wide_keep = home(
        section, task_ids, payload, second, n3, routes_t, router_t, cotangent, dec_flat, decoder_bias,
        mix_gains, first, mix_heads, mix_merge, (n2, q2, k2, v2, o2, l2), dense_saved, ndp,
    )
    wide_got = swap(wide_send, "section", 2)
    later, later_sent = halve([later_keep, after(later_got, da)], "dp", first_later[1])
    sooner, sent = halve([sooner_keep, after(sooner_got, da)], "dp", first_sooner[1])
    da = after(da, sent, later_sent)
    d0, stem_send, stem_keep = stem_back(
        section, task_ids, da, tokens, stem_gains, stem_heads, stem_merge, small, expert_small, (n0, q0, k0, v0, o0, l0), ndp
    )
    stem_got = swap(stem_send, "section", 2)

    masks = near_first(ndp)
    join = lambda xs, ys: [jnp.concatenate([x, y], axis=-1) for x, y in zip(xs, ys)]
    later, later_sent = halve([later[0], after(later[1], d0)], "dp", first_later[2])
    wide, wide_sent = halve([wide_keep, after(wide_got, d0, later_sent)], "dp", 1)
    stem, stem_sent = halve([stem_keep, after(stem_got, wide_sent)], "dp", 1)
    later[1] = after(later[1], stem_sent)
    sooner, sooner_sent = halve([sooner[0], after(sooner[1], later[1])], "dp", first_sooner[2])
    wide, wide_sent = halve([wide[0], after(wide[1], sooner_sent)], "dp", 2)
    stem, stem_sent = halve([stem[0], after(stem[1], wide_sent)], "dp", 2)

    def pieces(terms, masks):
        for mask in masks:
            terms, unused = halve(terms, "dp", mask)
        x = add_low(*terms)[0]
        return [take(x, s)] + [swap(take(x, s ^ mask), "section", mask) for mask in (1, 2, 3)]

    later = pieces([later[0], after(later[1], stem_sent)], first_later[3:])
    light = join([wide[0], after(wide[1], stem_sent)], stem)
    for mask in masks[2:]:
        light, sent = halve(light, "dp", mask)
    sooner = pieces([sooner[0], after(sooner[1], sent)], first_sooner[3:])
    grad_in, grad_out = heavy_out(section, task_ids, sooner + later, d)
    light = add_low(light[0], after(light[1], grad_in))[0]
    light_near = swap(light, "section", 1)

    (
        g_mix_heads, g_mix_merge, g_dec, g_expand, g_reduce, g_stem_heads, g_stem_merge, g_router, g_lift, g_bias, g_elift, g_edrop,
        g_stem_gains, g_stem_shifts, g_stem_biases, g_mix_gains, g_mix_shifts, g_mix_biases,
    ) = light_out(section, task_ids, light, light_near, d, dec, ff, dec // ndp // ns)
    return (
        decoded, d0, g_stem_gains, g_stem_shifts, g_stem_heads, g_stem_merge, g_stem_biases, g_expand,
        g_lift, g_reduce, g_mix_gains, g_mix_shifts, g_mix_heads, g_mix_merge, g_mix_biases, g_router.transpose(2, 0, 1),
        grad_in.transpose(1, 0, 2), g_elift, grad_out, g_edrop, g_dec, g_bias,
    )


def solution(mesh):
    both = ("dp", "section")
    placed = (P("dp", None), P("dp", None), P("dp"), P("dp", None)) + (P(),) * 20
    rows, columns = P(both, None), P(None, both)
    return jax.shard_map(
        body,
        mesh=mesh,
        in_specs=placed,
        out_specs=(
            rows, rows, columns, columns, rows, rows, columns, rows, P(both), rows, columns,
            columns, rows, rows, columns, P(both, None, None), P(None, both, None), columns,
            P(None, both, None), columns, P(both, None, None), columns,
        ),
        check_vma=False,
    )
```

```python
import functools
import math

import jax
import jax.numpy as jnp
from jax import lax
from jax.experimental import pallas as pl
from jax.experimental.pallas import tpu as pltpu
from jax.sharding import PartitionSpec as P

HEADS = 6
HDIM = 64
EXPERTS = 8
TOP = 4
PATCHES = 576
HALF = PATCHES // 2
CAP = 288
LANES = 128
EPSILON = 1e-06
SCALE = 1.0 / math.sqrt(HDIM)
BF = jnp.bfloat16
F32 = jnp.float32
VMEM = pltpu.VMEM
MIB = 1 << 20


def mm(a, b):
    return jnp.dot(a, b, preferred_element_type=F32)


def mm_tn(a, b):
    return lax.dot_general(a, b, (((0,), (0,)), ((), ())), preferred_element_type=F32)


def mm_nt(a, b):
    return lax.dot_general(a, b, (((1,), (1,)), ((), ())), preferred_element_type=F32)


def split_low(v):
    high = v.astype(BF)
    return high, (v - high.astype(F32)).astype(BF)


def norm_parts(v):
    centred = v - jnp.mean(v, axis=-1, keepdims=True)
    inverse = lax.rsqrt(jnp.mean(centred * centred, axis=-1, keepdims=True) + EPSILON)
    return centred * inverse, inverse


def norm_back(v, gain, up):
    unit, inverse = norm_parts(v)
    scaled = up * gain
    back = inverse * (
        scaled
        - jnp.mean(scaled, axis=-1, keepdims=True)
        - unit * jnp.mean(scaled * unit, axis=-1, keepdims=True)
    )
    return back, jnp.sum(up * unit, axis=0, keepdims=True), jnp.sum(up, axis=0, keepdims=True)


def gelu_both(u):
    t = pl.reciprocal(1.0 + (0.3275911 / math.sqrt(2.0)) * jnp.abs(u), approx=True)
    bell = jnp.exp2((-0.5 / math.log(2.0)) * u * u)
    poly = 0.5 * 1.421413741 + t * (0.5 * -1.453152027 + t * (0.5 * 1.061405429))
    tail = bell * (t * (0.5 * 0.254829592 + t * (0.5 * -0.284496736 + t * poly)))
    cdf = jnp.where(u >= 0.0, 1.0 - tail, tail)
    return u * cdf, cdf + u * bell * (1.0 / math.sqrt(2.0 * math.pi))


def side_masks():
    lane = lax.broadcasted_iota(jnp.int32, (1, LANES), 1)
    left = (lane < HDIM).astype(F32)
    return left.astype(BF), (1.0 - left).astype(BF)


def lane_ids(rows=1):
    return lax.broadcasted_iota(jnp.int32, (rows, LANES), 1)


def near_first(blocks):
    return [1 << i for i in range(blocks.bit_length() - 1)]


def spot_of(block, masks):
    spot = 0
    for mask in masks:
        spot = 2 * spot + (block // mask) % 2
    return spot


def deal(pay, value, at):
    r, w = pay.shape[2], value.shape[1]
    for b in range(pay.shape[1]):
        spot = spot_of(b, near_first(pay.shape[1]))
        for y in range(2):
            piece = value[(2 * b + y) * r : (2 * b + y + 1) * r]
            pay[y, spot, :, at : at + w] = piece.astype(BF)


def deal_long(pay, value, at):
    r, w = pay.shape[2], value.shape[1]
    for b in range(pay.shape[1]):
        spot = spot_of(b, near_first(pay.shape[1]))
        for y in range(2):
            for k in range(4):
                piece = value[(8 * b + 4 * y + k) * r : (8 * b + 4 * y + k + 1) * r]
                pay[y, spot, :, at + k * w : at + (k + 1) * w] = piece.astype(BF)


def light_shape(d, blocks, width):
    return (2, blocks, d // blocks // 2, width)


def one_hot(rows, columns, hits):
    sub, lane = (lax.broadcasted_iota(jnp.int32, (rows, columns), i) for i in range(2))
    total = jnp.zeros((rows, columns), F32)
    for i, j in hits:
        total = total + jnp.where((sub == i) & (lane == j), 1.0, 0.0)
    return total.astype(BF)


def columns_of(rows, lanes):
    count = -(-len(lanes) // 8) * 8
    n = rows[0].shape[1]
    spare = [jnp.zeros((count - len(lanes), n), F32)] if count > len(lanes) else []
    stacked = jnp.concatenate(rows + spare, axis=0)
    place = lax.broadcasted_iota(jnp.int32, (count, LANES), 0)
    lane = lane_ids(count)
    spread = jnp.zeros((count, LANES), F32)
    for i, at in enumerate(lanes):
        spread = spread + jnp.where((place == i) & (lane == at), 1.0, 0.0)
    return mm_tn(stacked.astype(BF), spread.astype(BF))


def spread_blocks(row, first_lane, blocks):
    n = row.shape[1]
    r = n // 4 // blocks
    place = lax.broadcasted_iota(jnp.int32, (8, LANES), 0)
    stacked = jnp.concatenate([row, jnp.zeros((7, n), F32)], axis=0)
    column = mm_tn(stacked.astype(BF), jnp.where(place == 0, 1.0, 0.0).astype(BF))
    lane = lane_ids()
    parts = []
    for b in range(blocks):
        part = None
        for s in range(4):
            at = (4 * b + s) * r
            piece = jnp.where(lane == first_lane + s, column[at : at + r], 0.0)
            part = piece if part is None else part + piece
        parts.append(part)
    return jnp.concatenate(parts, axis=0)


class Near:
    def __init__(self, array):
        self.array = array


class Fetched:
    def __init__(self, moves):
        self.moves = moves
        for move in moves:
            move.start()

    def wait(self):
        for move in self.moves:
            move.wait()
        self.moves = []


def run_kernel(body, n_in, n_out, picks, near_out, *refs):
    section, tasks = refs[:2]
    inputs, outputs = refs[2 : 2 + n_in], refs[2 + n_in : 2 + n_in + n_out]
    rest = refs[2 + n_in + n_out :]
    kept_in, kept_out = rest[:n_in], rest[n_in : n_in + n_out]
    in_sems, out_sems = rest[n_in + n_out : n_in + n_out + 2]
    kept_out = [outputs[i] if i in near_out else kept_out[i] for i in range(n_out)]
    at = (section[0], section[0] // 2, section[0] % 2, tasks, section[1])
    fetched, moving = [], []
    for i in range(n_in):
        if picks[i] == "near":
            fetched.append(None)
            continue
        source = inputs[i] if picks[i] is None else inputs[i].at[picks[i](*at[:4])]
        fetched.append(Fetched([pltpu.make_async_copy(source, kept_in[i], in_sems.at[i])]))

    def get(i):
        if fetched[i] is None:
            return inputs[i]
        fetched[i].wait()
        return kept_in[i]

    def put(i, source=None, part=None):
        if i in near_out:
            return
        source = kept_out[i] if source is None else source
        target = outputs[i] if part is None else outputs[i].at[part]
        move = pltpu.make_async_copy(source, target, out_sems.at[i if part is None else i + part * n_out])
        move.start()
        moving.append(move)

    body(at, get, put, kept_out, *rest[n_in + n_out + 2 :])
    for i in range(n_in):
        get(i)
    for move in moving:
        move.wait()


def call(body, section, tasks, inputs, outs, scratch=(), us=3.0, limit=56):
    arrays, picks, kept = [], [], []
    for x in inputs:
        if isinstance(x, Near):
            arrays.append(x.array)
            picks.append("near")
            kept.append(VMEM((8, LANES), F32))
            continue
        array, pick, shape = x if isinstance(x, tuple) else (x, None, x.shape)
        arrays.append(array)
        picks.append(pick)
        kept.append(VMEM(shape, array.dtype))
    kept_out = [VMEM(o[0], o[1]) if len(o) == 2 else VMEM((8, LANES), F32) for o in outs]
    near_out = [i for i, o in enumerate(outs) if len(o) == 3 and o[2] == "near"]
    anywhere, scalar = pl.BlockSpec(memory_space=pl.ANY), pl.BlockSpec(memory_space=pltpu.SMEM)
    here = pl.BlockSpec(memory_space=pltpu.VMEM)
    return pl.pallas_call(
        functools.partial(run_kernel, body, len(arrays), len(outs), picks, near_out),
        out_shape=[jax.ShapeDtypeStruct(o[0], o[1]) for o in outs],
        in_specs=[scalar, scalar] + [here if p == "near" else anywhere for p in picks],
        out_specs=[here if i in near_out else anywhere for i in range(len(outs))],
        scratch_shapes=[
            *kept, *kept_out, pltpu.SemaphoreType.DMA((len(arrays),)), pltpu.SemaphoreType.DMA((2 * len(outs),)), *scratch
        ],
        compiler_params=pltpu.CompilerParams(vmem_limit_bytes=limit * MIB),
        cost_estimate=pl.CostEstimate(flops=int(us * 1.1e9), bytes_accessed=1, transcendentals=0),
    )(section, tasks, *arrays)


def rows_of(count):
    return lambda s, image, core, tasks: pl.ds(pl.multiple_of(image * count, count), count)


def of_task(s, image, core, tasks):
    return tasks[image]


def attend_kernel(h, gain, shift, get_w, c, get_m, n_ref, q_ref, k_ref, v_ref, o_ref, lse_ref, done):
    d = h.shape[1]
    unit, unused = norm_parts(h)
    n_ref[...] = (unit * gain + shift).astype(BF)
    done(0)
    n, w = n_ref[...], get_w()
    q_ref[...] = ((mm(n, w[:, :d]) + c[0:1]) * SCALE).astype(BF)
    done(1)
    k_ref[...] = mm(n, w[:, d : 2 * d]).astype(BF)
    done(2)
    v_ref[...] = (mm(n, w[:, 2 * d :]) + c[1:2]).astype(BF)
    done(3)
    masks = side_masks()
    lane = lane_ids()
    sums = jnp.zeros((PATCHES, LANES), F32)
    step = 32
    for p in range(d // LANES):
        at = slice(p * LANES, (p + 1) * LANES)
        total = None
        for i, mask in enumerate(masks):
            scores = mm_nt(q_ref[:, at] * mask, k_ref[:, at])
            e, norm, top = [], [], []
            for r in range(PATCHES // step):
                part = scores[r * step : (r + 1) * step]
                most = jnp.max(part, axis=-1, keepdims=True)
                part = jnp.exp(part - most)
                e.append(part.astype(BF))
                norm.append(jnp.sum(part, axis=-1, keepdims=True))
                top.append(most)
            norm = jnp.concatenate(norm, axis=0)
            part = mm(jnp.concatenate(e, axis=0), v_ref[:, at] * mask) * (1.0 / norm)
            total = part if total is None else total + part
            sums = jnp.where(lane == 2 * p + i, jnp.concatenate(top, axis=0) + jnp.log(norm), sums)
        o_ref[:, at] = total.astype(BF)
    lse_ref[...] = sums
    done(4)
    done(5)
    return h + (mm(o_ref[...], get_m()[...]) + c[2:3])


def forward_body(at, get, put, out, *scratch):
    tok, sw, sg, ss, sb, sm, sx, sl, sr, mw, mg, ms, mb, m_m = range(14)
    (n0, q0, k0, v0, o0, l0, a0, n1, act, slope, first, n2, q2, k2, v2, o2, l2, second, n3) = out
    h = get(tok)[...].astype(F32)
    sg, ss, sb = get(sg), get(ss), get(sb)
    a = attend_kernel(
        h, sg[0:1], ss[0:1], lambda: get(sw), sb, lambda: get(sm), n0, q0, k0, v0, o0, l0, put
    )
    a0[...] = a
    put(6)
    unit, unused = norm_parts(a0[...])
    n1[...] = (unit * sg[1:2] + ss[1:2]).astype(BF)
    put(7)
    step = 1536
    wx, lift = get(sx), get(sl)
    for f in range(wx.shape[1] // step):
        cols = slice(f * step, (f + 1) * step)
        active, bend = gelu_both(mm(n1[...], wx[:, cols]) + lift[cols][None, :])
        act[:, cols] = active.astype(BF)
        slope[:, cols] = bend.astype(BF)
    put(8)
    put(9)
    first[...] = (a0[...] + (mm(act[...], get(sr)[...]) + sb[3:4])).astype(BF)
    put(10)
    mg, ms, mb = get(mg), get(ms), get(mb)
    second[...] = attend_kernel(
        first[...].astype(F32), mg[0:1], ms[0:1], lambda: get(mw), mb, lambda: get(m_m), n2, q2, k2, v2,
        o2, l2, lambda i: put(11 + i),
    ).astype(BF)
    put(17)
    unit, unused = norm_parts(second[...].astype(F32))
    n3[...] = (unit * mg[1:2] + ms[1:2]).astype(BF)


def forward(section, tasks, tokens, weights):
    d = tokens.shape[1]
    ff = weights[5].shape[1]
    wide = ((PATCHES, d), BF)
    sums = ((PATCHES, LANES), F32)
    outs = [wide] * 5 + [sums, ((PATCHES, d), F32), wide, ((PATCHES, ff), BF), ((PATCHES, ff), BF)]
    outs += [wide] * 6 + [sums, wide, wide + ("near",)]
    inputs = [(tokens, rows_of(PATCHES), (PATCHES, d)), *weights]
    return call(forward_body, section, tasks, inputs, outs, us=20.0)


def pick_routes(ref, image):
    every = ref[...]
    chosen = every[:, :PATCHES]
    for i in range(1, every.shape[1] // PATCHES):
        chosen = jnp.where(image == i, every[:, i * PATCHES : (i + 1) * PATCHES], chosen)
    return chosen


def experts_body(own, at, get, put, out, gates, place, d3):
    n, routes, router, cot, dec, w_in0, w_in1, lift, w_out0, w_out1, drop = range(11)
    core = at[2]
    if own:
        full, xs, dys, acts, dus = out
        first = 1
    else:
        send, keep, xs, dys, acts, dus, full = out
        first = 2
    n_ref = get(n)
    ids = lax.broadcasted_iota(jnp.int32, (EXPERTS, PATCHES), 0)
    member = jnp.zeros((EXPERTS, PATCHES), F32)
    named = pick_routes(get(routes), at[1] if own else 1 - at[1])
    for k in range(TOP):
        member = member + jnp.where(ids == named[k : k + 1, :], 1.0, 0.0)
    logits = jnp.where(member > 0.0, mm_nt(get(router)[...], n_ref[...]), -1e30)
    e = jnp.where(member > 0.0, jnp.exp(logits - jnp.max(logits, axis=0, keepdims=True)), 0.0)
    gates[...] = e / jnp.sum(e, axis=0, keepdims=True)
    before = lax.broadcasted_iota(jnp.int32, (PATCHES, PATCHES), 0)
    after_ = lax.broadcasted_iota(jnp.int32, (PATCHES, PATCHES), 1)
    upper = jnp.where(before <= after_, 1.0, 0.0).astype(BF)
    place[...] = jnp.where(member > 0.0, mm(member.astype(BF), upper) - 1.0, -1.0)
    d3[...] = mm_nt(get(cot)[...], get(dec)[...]).astype(BF)
    total = None
    lifts, drops = get(lift), get(drop)
    for j in range(2):
        e = 2 * at[0] + j
        spot = place[pl.ds(e, 1), :].astype(jnp.int32)
        hit = lax.broadcasted_iota(jnp.int32, (CAP, PATCHES), 0) == spot
        pick = jnp.where(hit, 1.0, 0.0)
        weight = jnp.sum(pick * gates[pl.ds(e, 1), :], axis=1, keepdims=True)
        pick = pick.astype(BF)
        x = mm(pick, n_ref[...]).astype(BF)
        up = mm(pick, d3[...])
        dy = (weight * up).astype(BF)
        xs[j] = x
        dys[j] = dy
        w_in, w_out = get((w_in0, w_in1)[j]), get((w_out0, w_out1)[j])
        ff = w_in.shape[1]
        step = 1536
        y = drops[pl.ds(e, 1), :]
        dx = None
        for f in range(ff // step):
            cols = slice(f * step, (f + 1) * step)
            active, bend = gelu_both(mm(x, w_in[:, cols]) + lifts[pl.ds(e, 1), cols])
            active = active.astype(BF)
            du = (bend * mm_nt(dy, w_out[cols, :])).astype(BF)
            y = y + mm(active, w_out[cols, :])
            part = mm_nt(du, w_in[:, cols])
            dx = part if dx is None else dx + part
            acts[j, :, cols] = active
            dus[j, :, cols] = du
        for i, kept in enumerate((xs, dys, acts, dus)):
            put(first + i, kept.at[j], j)
        dots = jnp.sum(y * up, axis=1, keepdims=True)
        high = dots.astype(BF).astype(F32)
        lane = lane_ids()
        marks = jnp.where(lane == e, high, jnp.where(lane == e + EXPERTS, dots - high, 0.0))
        rhs = jnp.concatenate([(weight * y).astype(BF), dx.astype(BF), marks.astype(BF)], axis=1)
        home = mm_tn(pick, rhs)
        total = home if total is None else total + home
    full[...] = total.astype(BF)
    if not own:
        send[...] = full[pl.ds(pl.multiple_of((1 - core) * HALF, 16), HALF), :]
        keep[...] = full[pl.ds(pl.multiple_of(core * HALF, 16), HALF), :]


def experts(own, section, tasks, n, routes_t, router_t, cot, dec, weights):
    expert_in, expert_lift, expert_out, expert_drop = weights
    d, ff = expert_in.shape[1:]
    width = 2 * d + LANES
    look = (lambda image: image) if own else (lambda image: 1 - image)
    which = lambda j: lambda s, image, core, tasks: 2 * s + j
    inputs = [
        Near(n),
        routes_t,
        (router_t, lambda s, image, core, tasks: tasks[look(image)], (EXPERTS, d)),
        (cot, lambda s, image, core, tasks: pl.ds(pl.multiple_of(look(image) * PATCHES, PATCHES), PATCHES),
         (PATCHES, cot.shape[1])),
        (dec, lambda s, image, core, tasks: (
            slice(None), pl.ds(pl.multiple_of(tasks[look(image)] * cot.shape[1], LANES), cot.shape[1])),
         (d, cot.shape[1])),
        (expert_in, which(0), (d, ff)), (expert_in, which(1), (d, ff)), expert_lift,
        (expert_out, which(0), (ff, d)), (expert_out, which(1), (ff, d)), expert_drop,
    ]
    half = ((HALF, width), BF, "near")
    outs = [((PATCHES, width), BF, "near")] if own else [half, half]
    outs += [((2, CAP, d), BF), ((2, CAP, d), BF), ((2, CAP, ff), BF), ((2, CAP, ff), BF)]
    scratch = [] if own else [VMEM((PATCHES, width), BF)]
    scratch += [
        VMEM((EXPERTS, PATCHES), F32), VMEM((EXPERTS, PATCHES), F32),
        VMEM((PATCHES, d), BF),
    ]

    def body(at, get, put, out, *rest):
        if own:
            experts_body(own, at, get, put, out, *rest)
        else:
            experts_body(own, at, get, put, [*out, rest[0]], *rest[1:])

    return call(body, section, tasks, inputs, outs, scratch, us=13.0)


def expert_masks(expert, blocks):
    masks = near_first(blocks)
    return masks if expert == 1 else [masks[1], masks[0], *masks[2:]]


def weight_grads(section, tasks, own, far, blocks):
    d, ff = own[0].shape[2], own[2].shape[2]
    r = d // blocks // 4
    part = lambda x, e: (x, lambda s, image, core, tasks: e, x.shape[1:])
    inputs = [part(x, e) for e in (1, 0) for pair in zip(own, far) for x in pair]
    shape = (2, blocks // 2, 4, 2 * r, ff)

    def body(at, get, put, out, *pays):
        small = out[4]
        for place, e in enumerate((1, 0)):
            pay, masks = pays[place], expert_masks(e, blocks)
            both = lambda i: jnp.concatenate([get(8 * place + 2 * i)[...], get(8 * place + 2 * i + 1)[...]], axis=0)
            x, du = both(0), both(3)
            step = 1536
            grad_in = [mm_tn(x, du[:, f * step : (f + 1) * step]) for f in range(ff // step)]
            lifts = jnp.sum(du.astype(F32), axis=0, keepdims=True)
            dy = both(1)
            drops = jnp.sum(dy.astype(F32), axis=0, keepdims=True)
            tiny = spread_blocks(lifts, 5 * e, 2 * blocks) + columns_of([drops], [5 * e + 4])
            small[...] = tiny if place == 0 else small[...] + tiny
            grad_out = mm_tn(both(2), dy)
            for b in range(blocks):
                i, j = divmod(spot_of(b, masks), blocks // 2)
                for t in range(4):
                    row = (4 * b + t) * r
                    for f, value in enumerate(grad_in):
                        pay[i, j, t, :r, f * step : (f + 1) * step] = value[row : row + r].astype(BF)
                    for k in range(4):
                        at_row = (4 * (4 * b + t) + k) * r
                        pay[i, j, t, r:, k * d : (k + 1) * d] = grad_out[at_row : at_row + r].astype(BF)
            bit = (at[4] // masks[0]) % 2
            put(2 * place, pay.at[1 - bit])
            put(2 * place + 1, pay.at[bit])
        moved = small[...]
        for s in range(4):
            moved = jnp.where(at[0] == s, pltpu.roll(small[...], 64 + 10 * s, 1), moved)
        small[...] = moved
        put(4)

    half = (shape[1:], BF, None)
    outs = [half] * 4 + [((d, LANES), F32)]
    return call(body, section, tasks, inputs, outs, [VMEM(shape, BF)] * 2, us=14.0)


def exact_rows(columns):
    sub = lax.broadcasted_iota(jnp.int32, (8, LANES), 0)
    eye = jnp.where(sub == lax.broadcasted_iota(jnp.int32, (8, LANES), 1), 1.0, 0.0).astype(BF)
    high, rest = split_low(columns)
    middle, low = split_low(columns - high.astype(F32))
    del rest
    return mm_nt(eye, high) + mm_nt(eye, middle) + mm_nt(eye, low)


def attend_back_kernel(h, gain, up, core, get_w, get_m, n, q, k, v, o, lse, dc_ref, do_ref, dqkv, pay):
    d = h.shape[1]
    dc_ref[...] = up.astype(BF)
    do_ref[...] = mm_nt(dc_ref[...], get_m()[...]).astype(BF)
    q, k, v, o = q(), k(), v(), o()
    masks = side_masks()
    sums = exact_rows(lse()[...])
    sub, lane = (lax.broadcasted_iota(jnp.int32, (8, d), i) for i in range(2))
    heads = jnp.where(lane // HDIM == sub, 1.0, 0.0).astype(BF)
    high, low = split_low(o[...].astype(F32) * do_ref[...].astype(F32))
    delta = mm_nt(heads, high) + mm_nt(heads, low)
    step = 64
    for p in range(d // LANES):
        at = slice(p * LANES, (p + 1) * LANES)
        dq = dk = dv = None
        for i, mask in enumerate(masks):
            head = 2 * p + i
            scores = mm_nt(k[:, at] * mask, q[:, at])
            dp = mm_nt(v[:, at] * mask, do_ref[:, at])
            probs, ds = [], []
            for r in range(PATCHES // step):
                rows = slice(r * step, (r + 1) * step)
                part = jnp.exp(scores[rows] - sums[head : head + 1])
                probs.append(part.astype(BF))
                ds.append((part * (dp[rows] - delta[head : head + 1])).astype(BF))
            ds = jnp.concatenate(ds, axis=0)
            part = mm(jnp.concatenate(probs, axis=0), do_ref[:, at] * mask)
            dv = part if dv is None else dv + part
            part = mm(ds, q[:, at] * mask)
            dk = part if dk is None else dk + part
            part = mm_tn(ds, k[:, at] * mask * SCALE)
            dq = part if dq is None else dq + part
        dqkv[:, at] = dq.astype(BF)
        dqkv[:, d + p * LANES : d + (p + 1) * LANES] = dk.astype(BF)
        dqkv[:, 2 * d + p * LANES : 2 * d + (p + 1) * LANES] = dv.astype(BF)
    rows = [
        jnp.sum(dqkv[:, :d].astype(F32), axis=0, keepdims=True),
        jnp.sum(dqkv[:, 2 * d :].astype(F32), axis=0, keepdims=True),
        jnp.sum(dc_ref[...].astype(F32), axis=0, keepdims=True),
    ]
    back, grad_gain, grad_shift = norm_back(h, gain, mm_nt(dqkv[...], get_w()[...]))
    n = n()

    @pl.when(core == 0)
    def queries():
        deal(pay, mm_tn(n[...], dqkv[:, :d]), 0)
        deal(pay, mm_tn(n[...], dqkv[:, 2 * d :]), d)

    @pl.when(core == 1)
    def keys_and_merge():
        deal(pay, mm_tn(n[...], dqkv[:, d : 2 * d]), 0)
        deal(pay, mm_tn(o[...], dc_ref[...]), d)

    return up + back, [grad_gain, grad_shift] + rows


def put_halves(put, first, pay, image):
    put(first, pay.at[1 - image])
    put(first + 1, pay.at[image])


def dense_part(blocks, at, get, d1, da, small, pay, du_all, lane):
    sr, slope, sx, a0, gains, n1, act = range(7)
    core = at[2]
    sr, slope, sx = get(sr), get(slope), get(sx)
    d, ff = sx.shape
    step = 1536
    dn = None
    for f in range(ff // step):
        cols = slice(f * step, (f + 1) * step)
        du = (slope[:, cols].astype(F32) * mm_nt(d1[...], sr[cols, :])).astype(BF)
        du_all[:, cols] = du
        part = mm_nt(du, sx[:, cols])
        dn = part if dn is None else dn + part
    up = d1[...].astype(F32)
    back, gain1, shift1 = norm_back(get(a0)[...], get(gains)[1:2], dn)
    da[...] = up + back
    lifts = jnp.sum(du_all[...].astype(F32), axis=0, keepdims=True)
    b3 = jnp.sum(up, axis=0, keepdims=True)
    small[...] += spread_blocks(lifts, 40, 2 * blocks) + columns_of([gain1, shift1, b3], [33, 35, 39])
    n1, act = get(n1), get(act)

    @pl.when(core == 0)
    def expand():
        for f in range(ff // step):
            deal(pay, mm_tn(n1[...], du_all[:, f * step : (f + 1) * step]), lane + f * step)

    @pl.when(core == 1)
    def reduce():
        deal_long(pay, mm_tn(act[...], d1[...]), lane)


def home_body(blocks, at, get, put, out, full, third, dc, do, dqkv, pay, d1, du_all):
    (mine, near, whole_own, partner, second, n3, routes, router, cot, dec, bias, gains, h_in, mw, m_m, n, q, k, v, o, lse) = range(21)
    decoded, da, small = out[0], out[1], out[2]
    s, image, core, tasks = at[:4]
    task = tasks[image]
    d = d1.shape[1]
    full[pl.ds(pl.multiple_of(core * HALF, 16), HALF), :] = get(mine)[...].astype(F32)
    full[pl.ds(pl.multiple_of((1 - core) * HALF, 16), HALF), :] = get(near)[...].astype(F32)
    full[...] += get(whole_own)[...].astype(F32) + get(partner)[...].astype(F32)
    stream = get(second)[...].astype(F32)
    third[...] = (stream + full[:, :d]).astype(BF)
    half = third[pl.ds(pl.multiple_of(core * HALF, 16), HALF), :]
    cot, dec, n3 = get(cot), get(dec), get(n3)
    decoded[...] = mm(half, dec[...]) + get(bias)[pl.ds(task, 1), :]
    put(0)
    hdec = cot.shape[1] // 2
    table = mm_tn(third[...], cot[:, pl.ds(pl.multiple_of(core * hdec, LANES), hdec)])
    deal(pay, jnp.where(task == 0, table, 0.0), 2 * d)
    deal(pay, jnp.where(task == 1, table, 0.0), 2 * d + hdec)

    ids = lax.broadcasted_iota(jnp.int32, (EXPERTS, PATCHES), 0)
    member = jnp.zeros((EXPERTS, PATCHES), F32)
    named = pick_routes(get(routes), image)
    for i in range(TOP):
        member = member + jnp.where(ids == named[i : i + 1, :], 1.0, 0.0)
    member = mm_tn(member.astype(BF), one_hot(EXPERTS, EXPERTS, [(i, i) for i in range(EXPERTS)]))
    table = get(router)
    logits = jnp.where(member > 0.0, mm_nt(n3[...], table[...]), -1e30)
    e = jnp.where(member > 0.0, jnp.exp(logits - jnp.max(logits, axis=1, keepdims=True)), 0.0)
    gates = e / jnp.sum(e, axis=1, keepdims=True)
    dots = full[:, 2 * d :]
    dots = dots[:, :EXPERTS] + dots[:, EXPERTS : 2 * EXPERTS]
    dz = gates * (dots - jnp.sum(gates * dots, axis=1, keepdims=True))
    high, low = split_low(dz)
    grad_router = mm_tn(high, n3[...]) + mm_tn(low, n3[...])
    dn = full[:, d : 2 * d] + mm(high, table[...]) + mm(low, table[...])
    gains = get(gains)
    back, gain1, shift1 = norm_back(stream, gains[1:2], dn)
    up = (mm_nt(cot[...], dec[...]).astype(BF).astype(F32) + back).astype(BF).astype(F32)
    later = lambda i: lambda: get(i)
    result, sums = attend_back_kernel(
        get(h_in)[...].astype(F32), gains[0:1], up, core, later(mw), later(m_m), later(n), later(q), later(k), later(v),
        later(o), later(lse), dc, do, dqkv, pay,
    )
    d1[...] = result.astype(BF)
    gain0, shift0, b0, b1, b2 = sums
    routed = columns_of([grad_router], list(range(EXPERTS)))
    small[...] = jnp.where(task == 0, routed, pltpu.roll(routed, EXPERTS, 1)) + columns_of(
        [gain0, gain1, shift0, shift1, b0, b1, b2], [16, 17, 18, 19, 20, 21, 22]
    )
    owners = jnp.sum(cot[...].astype(F32), axis=0, keepdims=True)
    count = cot.shape[1]
    column = columns_of([owners], [24])
    column = jnp.where(task == 0, column, pltpu.roll(column, 1, 1))
    r, some = d // blocks // 2, count // blocks // 2
    for b in range(2 * blocks):
        small[b * r : b * r + some, :] += column[b * some : (b + 1) * some]
    dense_part(blocks, at, lambda i: get(21 + i), d1, da, small, pay, du_all, 2 * d + count)
    n, lanes = pay.shape[1] // 2, pay.shape[3] // 2
    side = at[4] % 2
    for i, (y, x) in enumerate(((1 - image, 1 - side), (image, side))):
        put(3 + i, pay.at[y, :, :, pl.ds(0, lanes)])
        put(5 + i, pay.at[:, pl.ds(x * n, n), :, pl.ds(lanes, lanes)])


def home(section, tasks, payload, second, n3, routes, router, cot, dec, bias, gains, first, mw, m_m, saved, dense, blocks):
    d = second.shape[1]
    width = cot.shape[1]
    inputs = [
        *payload, second, Near(n3), routes, (router, of_task, (EXPERTS, d)),
        (cot, rows_of(PATCHES), (PATCHES, width)),
        (dec, lambda s, image, core, tasks: (slice(None), pl.ds(pl.multiple_of(tasks[image] * width, LANES), width)),
         (d, width)),
        bias, gains, first, mw, m_m, *saved, *dense,
    ]
    ff = dense[2].shape[1]
    shape = light_shape(d, blocks, 2 * d + width + ff)
    half = (shape[1:3] + (shape[3] // 2,), BF, None)
    other = ((2, shape[1] // 2, shape[2], shape[3] // 2), BF, None)
    outs = [((HALF, width), F32), ((PATCHES, d), F32, "near"), ((d, LANES), F32, "near"), half, half, other, other]
    scratch = [
        VMEM((PATCHES, 2 * d + LANES), F32), VMEM((PATCHES, d), BF), VMEM((PATCHES, d), BF), VMEM((PATCHES, d), BF),
        VMEM((PATCHES, 3 * d), BF), VMEM(shape, BF), VMEM((PATCHES, d), BF), VMEM((PATCHES, ff), BF),
    ]
    return call(functools.partial(home_body, blocks), section, tasks, inputs, outs, scratch, us=15.0)


def stem_back_body(at, get, put, out, full, dc, do, dqkv, pay):
    da, tok, gains, sw, sm, small_in, expert_in, n, q, k, v, o, lse = range(13)
    image, core = at[1], at[2]
    up = get(da)[...]
    d = up.shape[1]
    later = lambda i: lambda: get(i)
    result, sums = attend_back_kernel(
        get(tok)[...].astype(F32), get(gains)[0:1], up, core, later(sw), later(sm), later(n), later(q), later(k), later(v),
        later(o), later(lse), dc, do, dqkv, pay,
    )
    gain0, shift0, b0, b1, b2 = sums
    small = get(small_in)[...] + columns_of([gain0, shift0, b0, b1, b2], [32, 34, 36, 37, 38])
    deal(pay, jnp.where(core == 0, small, 0.0) + get(expert_in)[...], 2 * d)
    put_halves(put, 1, pay, image)
    full[...] = result
    put(0, full.at[pl.ds(pl.multiple_of(core * HALF, 8), HALF), :])


def stem_back(section, tasks, da, tokens, gains, sw, sm, small_in, expert_small, saved, blocks):
    d = da.shape[1]
    inputs = [Near(da), (tokens, rows_of(PATCHES), (PATCHES, d)), gains, sw, sm, Near(small_in), expert_small, *saved]
    shape = light_shape(d, blocks, 2 * d + LANES)
    half = (shape[1:], BF, None)
    outs = [((HALF, d), F32, None), half, half]
    scratch = [
        VMEM((PATCHES, d), F32), VMEM((PATCHES, d), BF), VMEM((PATCHES, d), BF), VMEM((PATCHES, 3 * d), BF),
        VMEM(shape, BF),
    ]
    return call(stem_back_body, section, tasks, inputs, outs, scratch, us=14.0)


def heavy_out_body(at, get, put, out, gathered):
    grad_in, grad_out = out
    s = at[0]
    r = grad_in.shape[0]
    d = grad_out.shape[2]
    for mask in range(4):
        for j in range(2):
            gathered[pl.ds(2 * jnp.bitwise_xor(s, mask) + j, 1)] = get(4 * j + mask)[...][None]
    for e in range(EXPERTS):
        value = gathered[e].astype(F32)
        grad_in[:, e, :] = value[:r]
        for k in range(4):
            grad_out[e, k * r : (k + 1) * r, :] = value[r:, k * d : (k + 1) * d]
    put(0)
    put(1)


def heavy_out(section, tasks, pieces, d):
    r2, ff = pieces[0].shape
    r = r2 // 2
    outs = [((r, EXPERTS, ff), F32), ((EXPERTS, 4 * r, d), F32)]
    return call(heavy_out_body, section, tasks, [Near(x) for x in pieces], outs, [VMEM((EXPERTS, r2, ff), BF)], us=0.2)


def light_out_body(d, dec, at, get, put, out, both):
    (mix_heads, mix_merge, dec_out, expand, reduce, stem_heads, stem_merge, router, lift, bias) = out[:10]
    elift, edrop = out[10:12]
    rows = out[12:]
    core = at[2]
    both[pl.ds(core, 1)] = get(0)[...][None]
    both[pl.ds(1 - core, 1)] = get(1)[...][None]
    r = expand.shape[0]
    m, ff, hdec = 2 * d + dec, expand.shape[1], dec // 2
    a, b = both[0].astype(F32), both[1].astype(F32)
    tiny = a[:, m + ff + 2 * d :]
    order = (32, 33, 34, 35, 36, 37, 38, 39, 16, 17, 18, 19, 20, 21, 22, 24, 25, 40, 41, 42, 43, 127, 127, 127)
    order = order + tuple(range(2 * EXPERTS))
    turned = mm_nt(one_hot(len(order), LANES, list(enumerate(order))), tiny.astype(BF))
    some = bias.shape[1]
    own = one_hot(5 * EXPERTS, LANES, [(i, 64 + i) for i in range(5 * EXPERTS)])
    by_core = [mm_nt(own, v[:, m + ff + 2 * d :].astype(BF)) for v in (a, b)]
    for c in range(2):

        @pl.when(core == c)
        def write():
            x, y = a[c * r : (c + 1) * r], b[c * r : (c + 1) * r]
            for heads, merge, base in ((mix_heads, mix_merge, 0), (stem_heads, stem_merge, m + ff)):
                heads[:, :d] = x[:, base : base + d]
                heads[:, d : 2 * d] = y[:, base : base + d]
                heads[:, 2 * d :] = x[:, base + d : base + 2 * d]
                merge[...] = y[:, base + d : base + 2 * d]
            for t in range(2):
                dec_out[:, t, :hdec] = x[:, 2 * d + t * hdec : 2 * d + (t + 1) * hdec]
                dec_out[:, t, hdec:] = y[:, 2 * d + t * hdec : 2 * d + (t + 1) * hdec]
                router[t] = turned[24 + t * EXPERTS : 24 + (t + 1) * EXPERTS, c * r : (c + 1) * r]
            expand[...] = x[:, m : m + ff]
            for k in range(2):
                at_lane = m + (2 * c + k) * d
                reduce[k * 2 * r : (k + 1) * 2 * r, :] = b[:, at_lane : at_lane + d]
            first = 0
            for part in rows:
                part[...] = turned[first : first + part.shape[0], c * r : (c + 1) * r]
                first += part.shape[0]
            bias[...] = turned[first : first + 2, c * some : (c + 1) * some]
            for e in range(EXPERTS):
                every = by_core[e // 2 % 2][5 * e : 5 * e + 5]
                elift[e : e + 1, :] = jnp.concatenate([every[2 * c : 2 * c + 1], every[2 * c + 1 : 2 * c + 2]], axis=1)
                edrop[e : e + 1, :] = every[4:5, c * r : (c + 1) * r]
            parts = [turned[first + 2 + 2 * c + k : first + 3 + 2 * c + k] for k in range(2)]
            lift[...] = jnp.concatenate(parts, axis=1)[0]

    for i in range(len(out)):
        put(i)


def light_out(section, tasks, mine, near, d, dec, ff, some):
    r2 = mine.shape[0]
    r = r2 // 2
    shapes = [
        (r, 3 * d), (r, d), (r, 2, dec), (r, ff), (4 * r, d), (r, 3 * d), (r, d), (2, EXPERTS, r), (2 * r2,), (2, some), (EXPERTS, 2 * r2),
        (EXPERTS, r),
        (2, r), (2, r), (4, r), (2, r), (2, r), (3, r),
    ]
    return call(
        functools.partial(light_out_body, d, dec), section, tasks, [Near(mine), Near(near)], [(x, F32) for x in shapes],
        [VMEM((2,) + mine.shape, BF)],
    )


def after(x, *others):
    return lax.optimization_barrier((x, *others))[0]


def swap(x, axis, mask):
    size = lax.axis_size(axis)
    return lax.ppermute(x, axis, [(i, i ^ mask) for i in range(size)])


def add_low(*terms):
    return sum(t.astype(F32) for t in terms).astype(BF)


def take(x, i):
    return lax.dynamic_index_in_dim(x, i, 0, keepdims=False)


def halve(terms, axis, mask):
    bit = (lax.axis_index(axis) // mask) % 2
    terms = [x.reshape((2, x.shape[0] // 2) + x.shape[1:]) for x in terms]
    send = add_low(*[take(t, 1 - bit) for t in terms])
    return [add_low(*[take(t, bit) for t in terms]), swap(send, axis, mask)], send


def body(
    tokens, routes, task_ids, cotangent, stem_gains, stem_shifts, stem_heads, stem_merge,
    stem_biases, stem_expand, stem_lift, stem_reduce, mix_gains, mix_shifts, mix_heads,
    mix_merge, mix_biases, router, expert_in, expert_lift, expert_out, expert_drop, decoder,
    decoder_bias,
):
    s = lax.axis_index("section")
    image = s // 2
    section = jnp.stack([s, lax.axis_index("dp")])
    ndp, ns = lax.axis_size("dp"), lax.axis_size("section")
    d, ff, dec = tokens.shape[1], stem_expand.shape[1], cotangent.shape[1]
    r, q = d // ndp, d // ndp // ns

    weights = [
        stem_heads, stem_gains, stem_shifts, stem_biases, stem_merge, stem_expand, stem_lift, stem_reduce, mix_heads,
        mix_gains, mix_shifts, mix_biases, mix_merge,
    ]
    (n0, q0, k0, v0, o0, l0, a0, n1, act, slope, first, n2, q2, k2, v2, o2, l2, second, n3) = forward(
        section, task_ids, tokens, weights
    )
    far = swap(n3, "section", 2)

    routes_t = routes.T
    router_t = router.transpose(1, 2, 0)
    dec_flat = decoder.reshape(d, -1)
    common = (routes_t, router_t, cotangent, dec_flat, (expert_in, expert_lift, expert_out, expert_drop))
    own_pay, *own = experts(True, section, task_ids, n3, *common)
    far = after(far, own_pay)
    own_got = swap(own_pay, "section", 1)
    far_send, far_keep, *away = experts(False, section, task_ids, far, *common)
    crossed = add_low(far_keep, swap(far_send, "section", 1))
    away[0] = after(away[0], crossed)
    crossed = swap(crossed, "section", 2)
    later_send, later_keep, sooner_send, sooner_keep, expert_small = weight_grads(section, task_ids, own, away, ndp)
    first_later, first_sooner = (expert_masks(e, ndp) for e in (1, 0))
    crossed = after(crossed, later_keep)
    later_got = swap(later_send, "dp", first_later[0])
    sooner_got = swap(sooner_send, "dp", first_sooner[0])
    payload = [Near(crossed), Near(swap(crossed, "section", 1)), own_pay, own_got]

    dense_saved = (stem_reduce, slope, stem_expand, a0, stem_gains, n1, act)
    decoded, da, small, wide_send, wide_keep, broad_send, broad_keep = home(
        section, task_ids, payload, second, n3, routes_t, router_t, cotangent, dec_flat, decoder_bias,
        mix_gains, first, mix_heads, mix_merge, (n2, q2, k2, v2, o2, l2), dense_saved, ndp,
    )
    wide_got = swap(wide_send, "section", 2)
    broad_got = swap(broad_send, "dp", 1)
    later, later_sent = halve([later_keep, after(later_got, da)], "dp", first_later[1])
    sooner, sent = halve([sooner_keep, after(sooner_got, da)], "dp", first_sooner[1])
    da = after(da, sent, later_sent)
    d0, stem_send, stem_keep = stem_back(
        section, task_ids, da, tokens, stem_gains, stem_heads, stem_merge, small, expert_small, (n0, q0, k0, v0, o0, l0), ndp
    )
    stem_got = swap(stem_send, "section", 2)

    masks = near_first(ndp)
    join = lambda xs, ys: [jnp.concatenate([x, y], axis=-1) for x, y in zip(xs, ys)]
    later, later_sent = halve([later[0], after(later[1], d0)], "dp", first_later[2])
    wide, wide_sent = halve([wide_keep, after(wide_got, d0, later_sent)], "dp", 1)
    broad, broad_sent = halve([broad_keep, after(broad_got, d0, wide_sent)], "section", 2)
    stem, stem_sent = halve([stem_keep, after(stem_got, broad_sent)], "dp", 1)
    later[1] = after(later[1], stem_sent)
    sooner, sooner_sent = halve([sooner[0], after(sooner[1], later[1])], "dp", first_sooner[2])
    every = zip(wide, [broad[0][0], after(broad[1], sooner_sent)[0]], [stem[0], after(stem[1], sooner_sent)])
    light, stem_sent = halve([jnp.concatenate(x, axis=-1) for x in every], "dp", 2)

    def pieces(terms, masks):
        for mask in masks:
            terms, unused = halve(terms, "dp", mask)
        x = add_low(*terms)[0]
        return [take(x, s)] + [swap(take(x, s ^ mask), "section", mask) for mask in (1, 2, 3)]

    later = pieces([later[0], after(later[1], stem_sent)], first_later[3:])
    for mask in masks[2:]:
        light, sent = halve(light, "dp", mask)
    sooner = pieces([sooner[0], after(sooner[1], sent)], first_sooner[3:])
    grad_in, grad_out = heavy_out(section, task_ids, sooner + later, d)
    light = add_low(light[0], after(light[1], grad_in))[0]
    light_near = swap(light, "section", 1)

    (
        g_mix_heads, g_mix_merge, g_dec, g_expand, g_reduce, g_stem_heads, g_stem_merge, g_router, g_lift, g_bias, g_elift, g_edrop,
        g_stem_gains, g_stem_shifts, g_stem_biases, g_mix_gains, g_mix_shifts, g_mix_biases,
    ) = light_out(section, task_ids, light, light_near, d, dec, ff, dec // ndp // ns)
    return (
        decoded, d0, g_stem_gains, g_stem_shifts, g_stem_heads, g_stem_merge, g_stem_biases, g_expand,
        g_lift, g_reduce, g_mix_gains, g_mix_shifts, g_mix_heads, g_mix_merge, g_mix_biases, g_router.transpose(2, 0, 1),
        grad_in.transpose(1, 0, 2), g_elift, grad_out, g_edrop, g_dec, g_bias,
    )


def solution(mesh):
    both = ("dp", "section")
    placed = (P("dp", None), P("dp", None), P("dp"), P("dp", None)) + (P(),) * 20
    rows, columns = P(both, None), P(None, both)
    return jax.shard_map(
        body,
        mesh=mesh,
        in_specs=placed,
        out_specs=(
            rows, rows, columns, columns, rows, rows, columns, rows, P(both), rows, columns,
            columns, rows, rows, columns, P(both, None, None), P(None, both, None), columns,
            P(None, both, None), columns, P(both, None, None), columns,
        ),
        check_vma=False,
    )
```
